32 devices in a mesh: gx: 4 (over z), gy: 8 (over y, x, core).
Axes of the slice: x: 2, y: 2, z: 4, core: 2. Of those that a mesh axis runs over, the one named last changes fastest.
Arguments:
- hidden: float32 [16384, 1024], P(('gx', 'gy')), may hold values from -6 to 6
- memory: bfloat16 [18816, 1024], P(('gx', 'gy')), may hold values from -6 to 6
- lengths: int32 [32], P(('gx', 'gy')), may hold values from 192 to 512, as said below
- page_class: int32 [32], P(('gx', 'gy')), may hold values from 0 to 1
- cotangent: float32 [16384, 1024], P(('gx', 'gy')), may hold values from -6 to 6
- w_self_qkv: bfloat16 [1024, 3072], P(('gx', 'gy')), may hold values from -0.1875 to 0.1875
- w_self_out: bfloat16 [1024, 1024], P(('gx', 'gy')), may hold values from -3 to 3
- w_cross_q: bfloat16 [1024, 1024], P(('gx', 'gy')), may hold values from -0.1875 to 0.1875
- w_cross_kv: bfloat16 [1024, 2048], P(('gx', 'gy')), may hold values from -0.1875 to 0.1875
- w_cross_out: bfloat16 [1024, 1024], P(('gx', 'gy')), may hold values from -3 to 3
- w_fc1: bfloat16 [1024, 4096], P(('gx', 'gy')), may hold values from -0.1875 to 0.1875
- w_fc2: bfloat16 [4096, 1024], P(('gx', 'gy')), may hold values from -0.09375 to 0.09375
- norm_gains: bfloat16 [3, 1024], P(None, ('gx', 'gy')), may hold values from 0.5 to 1.5
- norm_biases: bfloat16 [3, 1024], P(None, ('gx', 'gy')), may hold values from -1.75 to 1.75
Outputs:
- result: float32 [16384, 1024], P(('gx', 'gy'))
- grad_hidden: float32 [16384, 1024], P(('gx', 'gy'))
- grad_memory: float32 [18816, 1024], P(('gx', 'gy'))
- grad_self_qkv: float32 [1024, 3072], P(('gx', 'gy'))
- grad_self_out: float32 [1024, 1024], P(('gx', 'gy'))
- grad_cross_q: float32 [1024, 1024], P(('gx', 'gy'))
- grad_cross_kv: float32 [1024, 2048], P(('gx', 'gy'))
- grad_cross_out: float32 [1024, 1024], P(('gx', 'gy'))
- grad_fc1: float32 [1024, 4096], P(('gx', 'gy'))
- grad_fc2: float32 [4096, 1024], P(('gx', 'gy'))
- grad_gains: float32 [3, 1024], P(None, ('gx', 'gy'))
- grad_biases: float32 [3, 1024], P(None, ('gx', 'gy'))
The draws below stay inside these ranges and needn't reach their ends.
Inputs may be any that keep to these rules, and one draw needn't show every extreme that they name: `lengths`: some page has exactly 512 decoder tokens; every page has at least 192.
All inputs are finite; a program needn't handle non-finite values.
Results may differ from the reference program's by a relative error of at most 0.017.
Values may be sent and summed in bfloat16 or wider, within the bound.
No kernel may reach another device: no remote copies, remote signals or barrier semaphores. Data moves between devices by JAX's collectives and lax.ppermute only.
A program may use at most 320 MiB of HBM per device.

```python
import jax
import jax.numpy as jnp
from jax import lax

D = 1024
HEADS = 16
FF = 4096
LSLOT = 512
MEM_BIG = 588
PAGES_DEV = 1
PAGES = 32
TOKENS = 16384
MEMORY_ROWS = 18816


def draw_lengths(key, part):
    key = jax.random.fold_in(key, 11)
    first_key, second_key = jax.random.split(key)
    drawn = jax.random.randint(first_key, (PAGES,), LSLOT * 3 // 8, LSLOT + 1)
    chosen = jax.random.randint(second_key, (), 0, PAGES)
    return jnp.where(jnp.arange(PAGES) == chosen, LSLOT, drawn).astype(jnp.int32)


def plant(values, stream_key, smallest, high):
    index_at = [jax.random.randint(jax.random.fold_in(stream_key, axis), (), 0, length) for axis, length in enumerate(values.shape)]
    widest = values.shape.index(max(values.shape))
    next_to = index_at[:widest] + [(index_at[widest] + 1) % values.shape[widest]] + index_at[widest + 1:]
    return values.at[tuple(index_at)].set(smallest).at[tuple(next_to)].set(high)


def block_scale(rng, extent, cuts, low, high):
    loudness, own = 1.0, jax.random.fold_in(rng, 6)
    for dim, shards_of in cuts:
        draws = jnp.exp(jax.random.uniform(jax.random.fold_in(own, dim), (shards_of,), jnp.float32, low / len(cuts), high / len(cuts)))
        loudness = loudness * jnp.repeat(draws, extent[dim] // shards_of).reshape([-1 if axis == dim else 1 for axis in range(len(extent))])
    return loudness


def scatter_about(own_key, shape, width, reach, cuts=(), kind=jnp.bfloat16):
    values = width * jax.random.normal(own_key, shape, jnp.float32)
    if cuts:
        values = values * block_scale(own_key, shape, cuts, -0.22, 0.18)
    return jnp.clip(values, -reach, reach).astype(kind)


def setup_inputs(seed: int = 0) -> dict:
    keys = jax.random.split(jax.random.key(seed), 15)
    return {
        "hidden": scatter_about(keys[0], (TOKENS, D), 1.0, 6.0, ((0, 32),), jnp.float32),
        "memory": scatter_about(keys[1], (MEMORY_ROWS, D), 1.0, 6.0, ((0, 32),)),
        "lengths": draw_lengths(jax.random.fold_in(keys[14], 71), 0),
        "page_class": plant(jax.random.randint(keys[3], (PAGES,), 0, 2), jax.random.fold_in(keys[3], 1), 0, 1).astype(jnp.int32),
        "cotangent": scatter_about(keys[4], (TOKENS, D), 1.0, 6.0, ((0, 32),), jnp.float32),
        "w_self_qkv": scatter_about(keys[5], (D, 3 * D), D ** -0.5, 0.1875, ((0, 32),)),
        "w_self_out": scatter_about(keys[6], (D, D), (max(D // 256, 1)) ** -0.5, 3.0, ((0, 32),)),
        "w_cross_q": scatter_about(keys[7], (D, D), D ** -0.5, 0.1875, ((0, 32),)),
        "w_cross_kv": scatter_about(keys[8], (D, 2 * D), D ** -0.5, 0.1875, ((0, 32),)),
        "w_cross_out": scatter_about(keys[9], (D, D), (max(D // 256, 1)) ** -0.5, 3.0, ((0, 32),)),
        "w_fc1": scatter_about(keys[10], (D, FF), D ** -0.5, 0.1875, ((0, 32),)),
        "w_fc2": scatter_about(keys[11], (FF, D), FF ** -0.5, 0.09375, ((0, 32),)),
        "norm_gains": jnp.clip(1.0 + 0.1 * jax.random.normal(keys[12], (3, D), jnp.float32), 0.5, 1.5).astype(jnp.bfloat16),
        "norm_biases": scatter_about(keys[13], (3, D), 0.3, 1.75, ((1, 32),)),
    }


@jax.custom_vjp
def low(v):
    return lax.optimization_barrier(v.astype(jnp.bfloat16)).astype(jnp.float32)

@jax.custom_vjp
def low_back(v):
    return v

def low_keep(v):
    return (low(v), None)

def low_pass(kept, grad):
    return (grad,)

def back_keep(v):
    return (v, None)

def back_low(kept, grad):
    return (low(grad),)
low.defvjp(low_keep, low_pass)
low_back.defvjp(back_keep, back_low)

def layer_norm(v, gain_row, bias_row):
    center = v - lax.optimization_barrier(jnp.mean(v, -1, keepdims=True))
    variance = lax.optimization_barrier(jnp.mean(center * center, -1, keepdims=True))
    return center * lax.rsqrt(variance + 1e-05) * gain_row + bias_row

def product(a, b):
    return jnp.dot(a, b, precision=lax.Precision.HIGHEST)

def page_attend(query, key_rows, values, allowed):
    head_size = query.shape[1] // HEADS
    query_heads = query.reshape(query.shape[0], HEADS, head_size)
    key_heads = key_rows.reshape(key_rows.shape[0], HEADS, head_size)
    value_heads = values.reshape(values.shape[0], HEADS, head_size)
    scores = jnp.einsum('qhd,khd->hqk', query_heads, key_heads, precision=lax.Precision.HIGHEST) * head_size ** (-0.5)
    scores = jnp.where(allowed[None], low_back(scores), -1e+30)
    row_top = lax.optimization_barrier(jnp.max(scores, -1, keepdims=True))
    expd = jnp.exp(scores - row_top)
    probs = low(expd / lax.optimization_barrier(jnp.sum(expd, -1, keepdims=True)))
    mixed = jnp.einsum('hqk,khd->qhd', probs, value_heads, precision=lax.Precision.HIGHEST)
    return mixed.reshape(query.shape[0], -1)

def self_page(entry):
    query, key_rows, values, length = entry
    position = jnp.arange(LSLOT)
    allowed = (position[None, :] <= position[:, None]) & (position[None, :] < length)
    return page_attend(query, key_rows, values, allowed)

def cross_page(entry):
    query, key_rows, values, slots_used = entry
    slots = jnp.arange(MEM_BIG)
    allowed = jnp.broadcast_to(slots[None, :] < slots_used, (LSLOT, MEM_BIG))
    return page_attend(query, key_rows, values, allowed)

def block(x, memory_rows, page_lens, classes, wqkv, wso, wcq, wckv, wco, wup, wdown, gains, biases):
    features = x.shape[1]
    page_total = page_lens.shape[0]
    h1 = low(layer_norm(x, gains[0], biases[0]))
    qkv = low(low_back(product(h1, wqkv)))
    queries = qkv[:, :features].reshape(page_total, LSLOT, features)
    key_rows = qkv[:, features:2 * features].reshape(page_total, LSLOT, features)
    values = qkv[:, 2 * features:].reshape(page_total, LSLOT, features)
    mixed = lax.map(jax.checkpoint(self_page), (queries, key_rows, values, page_lens)).reshape(-1, features)
    mixed = low(low_back(mixed))
    x1 = x + low_back(product(mixed, wso))
    h2 = low(layer_norm(x1, gains[1], biases[1]))
    cross_query = low(low_back(product(h2, wcq))).reshape(page_total, LSLOT, features)
    kvc = low(low_back(product(memory_rows, wckv)))
    cross_keys = kvc[:, :features].reshape(page_total, MEM_BIG, features)
    cross_values = kvc[:, features:].reshape(page_total, MEM_BIG, features)
    slots_used = jnp.where(classes == 0, MEM_BIG, MEM_BIG // 4)
    mixed_cross = lax.map(jax.checkpoint(cross_page), (cross_query, cross_keys, cross_values, slots_used)).reshape(-1, features)
    mixed_cross = low(low_back(mixed_cross))
    x2 = x1 + low_back(product(mixed_cross, wco))
    h3 = low(layer_norm(x2, gains[2], biases[2]))
    upper = low_back(product(h3, wup))
    activated = low(jax.nn.gelu(upper, approximate=False))
    return x2 + low_back(product(activated, wdown))

def reference(hidden, memory, lengths, page_class, cotangent, w_self_qkv, w_self_out, w_cross_q, w_cross_kv, w_cross_out, w_fc1, w_fc2, norm_gains, norm_biases):
    params = tuple((w.astype(jnp.float32) for w in (w_self_qkv, w_self_out, w_cross_q, w_cross_kv, w_cross_out, w_fc1, w_fc2, norm_gains, norm_biases)))
    group_rows = PAGES_DEV * LSLOT
    groups = hidden.shape[0] // group_rows
    features = hidden.shape[1]
    entries = (hidden.reshape(groups, group_rows, features), memory.astype(jnp.float32).reshape(groups, PAGES_DEV * MEM_BIG, features), lengths.reshape(groups, PAGES_DEV), page_class.reshape(groups, PAGES_DEV), cotangent.reshape(groups, group_rows, features))

    def advance(summed, entry):
        x, memory_rows, page_lens, classes, cotan = entry

        def forward(x, memory_rows, *weights):
            return block(x, memory_rows, page_lens, classes, *weights)
        output, pullback = jax.vjp(forward, x, memory_rows, *params)
        valid = (jnp.arange(LSLOT)[None, :] < page_lens[:, None]).reshape(-1)
        grads = pullback(cotan * valid[:, None].astype(cotan.dtype))
        return (tuple((a + b for a, b in zip(summed, grads[2:]))), (output, grads[0], grads[1]))
    zeros_start = tuple((jnp.zeros_like(w) for w in params))
    summed, (output, grad_x, grad_m) = lax.scan(advance, zeros_start, entries)
    return (output.reshape(-1, features), grad_x.reshape(-1, features), grad_m.reshape(-1, features), summed[0], summed[1], summed[2], summed[3], summed[4], summed[5], summed[6], summed[7], summed[8])
```

```python
import functools

import jax
import jax.numpy as jnp
from jax import lax
from jax.experimental import pallas as pl
from jax.experimental.pallas import tpu as pltpu
from jax.sharding import PartitionSpec as P

HEADS = 16
MEM_BIG = 588
ALL = ("gx", "gy")
BF = jnp.bfloat16
F32 = jnp.float32
PAIR = 128


def dot(a, b):
    return jnp.dot(a, b, preferred_element_type=F32)


def dot_nt(a, b):
    return lax.dot_general(a, b, (((1,), (1,)), ((), ())), preferred_element_type=F32)


def dot_tn(a, b):
    return lax.dot_general(a, b, (((0,), (0,)), ((), ())), preferred_element_type=F32)


def allowed_t(key_count, q0, q1, limit, causal):
    key_at = lax.broadcasted_iota(jnp.int32, (key_count, q1 - q0), 0)
    ok = key_at < limit
    if causal:
        query_at = lax.broadcasted_iota(jnp.int32, (key_count, q1 - q0), 1) + q0
        ok = ok & (key_at <= query_at)
    return ok


def half_mask(width, half):
    lane = lax.broadcasted_iota(jnp.int32, (1, width), 1)
    return ((lane // (width // 2)) == half).astype(F32).astype(BF)


def attn_fwd_kernel(spans, causal, limit_ref, q_ref, k_ref, v_ref, o_ref, lse_ref):
    width = q_ref.shape[1]
    half = width // 2
    limit = limit_ref[0]
    scale = BF(half**-0.5)
    v_t = v_ref[...].T
    for q0, q1, keys in spans:
        query = q_ref[q0:q1, :] * scale
        ok = allowed_t(keys, q0, q1, limit, causal)
        outs = []
        for h in range(2):
            s = dot_nt(k_ref[:keys, :], query * half_mask(width, h))
            s = jnp.where(ok, s, -1e30)
            top = jnp.max(s, axis=0, keepdims=True)
            e = jnp.exp(s - top)
            total = jnp.sum(e, axis=0, keepdims=True)
            outs.append(dot(v_t[h * half : (h + 1) * half, :keys], e.astype(BF)) / total)
            lse_ref[0, h : h + 1, q0:q1] = top + jnp.log(total)
        o_ref[q0:q1, :] = jnp.concatenate(outs, axis=0).T.astype(BF)


def attn_bwd_kernel(
    spans, causal, limit_ref, q_ref, k_ref, v_ref, o_ref, do_ref, lse_ref, dq_ref, dk_ref, dv_ref
):
    width = q_ref.shape[1]
    half = width // 2
    limit = limit_ref[0]
    scale = BF(half**-0.5)
    k_t = k_ref[...].T * scale
    dk_ref_val = [None]
    total_k = k_ref.shape[0]
    dk = jnp.zeros((total_k, width), F32)
    dv = jnp.zeros((total_k, width), F32)
    del dk_ref_val
    for q0, q1, keys in spans:
        query = q_ref[q0:q1, :] * scale
        grad_o = do_ref[q0:q1, :]
        ok = allowed_t(keys, q0, q1, limit, causal)
        both = (grad_o.astype(F32) * o_ref[q0:q1, :].astype(F32)).T
        outs = []
        dk_part = jnp.zeros((keys, width), F32)
        dv_part = jnp.zeros((keys, width), F32)
        for h in range(2):
            mask = half_mask(width, h)
            query_h = query * mask
            grad_h = grad_o * mask
            inner = jnp.sum(both[h * half : (h + 1) * half], axis=0, keepdims=True)
            s = dot_nt(k_ref[:keys, :], query_h)
            p = jnp.where(ok, jnp.exp(s - lse_ref[0, h : h + 1, q0:q1]), 0.0)
            dv_part += dot(p.astype(BF), grad_h)
            dp = dot_nt(v_ref[:keys, :], grad_h)
            ds = (p * (dp - inner)).astype(BF)
            dk_part += dot(ds, query_h)
            outs.append(dot(k_t[h * half : (h + 1) * half, :keys], ds))
        dq_ref[q0:q1, :] = jnp.concatenate(outs, axis=0).T.astype(BF)
        if keys < total_k:
            pad = jnp.zeros((total_k - keys, width), F32)
            dk_part = jnp.concatenate([dk_part, pad], axis=0)
            dv_part = jnp.concatenate([dv_part, pad], axis=0)
        dk += dk_part
        dv += dv_part
    dk_ref[...] = dk.astype(BF)
    dv_ref[...] = dv.astype(BF)


def make_spans(queries, keys, causal):
    step = 256
    return tuple(
        (q, q + step, min(q + step, keys) if causal else keys) for q in range(0, queries, step)
    )


def attn_params():
    return pltpu.CompilerParams(
        dimension_semantics=("arbitrary",), vmem_limit_bytes=40 * 1024 * 1024
    )


def attn_fwd(q, kv, k_at, v_at, limit, causal):
    q_arr, q_at = q
    queries, keys = q_arr.shape[0], kv.shape[0]
    pairs = HEADS // 2
    return pl.pallas_call(
        functools.partial(attn_fwd_kernel, make_spans(queries, keys, causal), causal),
        grid_spec=pltpu.PrefetchScalarGridSpec(
            num_scalar_prefetch=1,
            grid=(pairs,),
            in_specs=[
                pl.BlockSpec((queries, PAIR), lambda p, _: (0, q_at + p)),
                pl.BlockSpec((keys, PAIR), lambda p, _: (0, k_at + p)),
                pl.BlockSpec((keys, PAIR), lambda p, _: (0, v_at + p)),
            ],
            out_specs=[
                pl.BlockSpec((queries, PAIR), lambda p, _: (0, p)),
                pl.BlockSpec((1, 2, queries), lambda p, _: (p, 0, 0)),
            ],
        ),
        out_shape=[
            jax.ShapeDtypeStruct((queries, pairs * PAIR), BF),
            jax.ShapeDtypeStruct((pairs, 2, queries), F32),
        ],
        compiler_params=attn_params(),
        cost_estimate=pl.CostEstimate(
            flops=16 * queries * keys * 256 * 4,
            bytes_accessed=8 * queries * 1024,
            transcendentals=16 * queries * keys,
        ),
        name="attn_fwd",
    )(limit, q_arr, kv, kv)


def attn_bwd(q, kv, k_at, v_at, o, do, lse, limit, causal):
    q_arr, q_at = q
    queries, keys = q_arr.shape[0], kv.shape[0]
    pairs = HEADS // 2
    q_block = pl.BlockSpec((queries, PAIR), lambda p, _: (0, p))
    k_block = pl.BlockSpec((keys, PAIR), lambda p, _: (0, p))
    return pl.pallas_call(
        functools.partial(attn_bwd_kernel, make_spans(queries, keys, causal), causal),
        grid_spec=pltpu.PrefetchScalarGridSpec(
            num_scalar_prefetch=1,
            grid=(pairs,),
            in_specs=[
                pl.BlockSpec((queries, PAIR), lambda p, _: (0, q_at + p)),
                pl.BlockSpec((keys, PAIR), lambda p, _: (0, k_at + p)),
                pl.BlockSpec((keys, PAIR), lambda p, _: (0, v_at + p)),
                q_block,
                q_block,
                pl.BlockSpec((1, 2, queries), lambda p, _: (p, 0, 0)),
            ],
            out_specs=[q_block, k_block, k_block],
        ),
        out_shape=[
            jax.ShapeDtypeStruct((queries, pairs * PAIR), BF),
            jax.ShapeDtypeStruct((keys, pairs * PAIR), BF),
            jax.ShapeDtypeStruct((keys, pairs * PAIR), BF),
        ],
        compiler_params=attn_params(),
        cost_estimate=pl.CostEstimate(
            flops=16 * queries * keys * 256 * 10,
            bytes_accessed=16 * queries * 1024,
            transcendentals=16 * queries * keys,
        ),
        name="attn_bwd",
    )(limit, q_arr, kv, kv, o, do, lse)


def norm_parts(v):
    center = v - jnp.mean(v, -1, keepdims=True)
    inverse = lax.rsqrt(jnp.mean(center * center, -1, keepdims=True) + 1e-05)
    return center * inverse, inverse


def norm_back(grad, unit, inverse, gain):
    gain_grad = jnp.sum(grad * unit, axis=0)
    bias_grad = jnp.sum(grad, axis=0)
    scaled = grad * gain
    mean_a = jnp.mean(scaled, -1, keepdims=True)
    mean_b = jnp.mean(scaled * unit, -1, keepdims=True)
    return inverse * (scaled - mean_a - unit * mean_b), gain_grad, bias_grad


def gather_rows(w):
    return lax.all_gather(w, ALL, axis=0, tiled=True)


def scatter_rows(g):
    part = lax.psum_scatter(g, "gy", scatter_dimension=0, tiled=True)
    return lax.psum_scatter(part, "gx", scatter_dimension=0, tiled=True)


def shards(
    hidden,
    memory,
    lengths,
    page_class,
    cotangent,
    w_self_qkv,
    w_self_out,
    w_cross_q,
    w_cross_kv,
    w_cross_out,
    w_fc1,
    w_fc2,
    norm_gains,
    norm_biases,
    *,
    nx,
    ny,
):
    n = nx * ny
    tokens, d = hidden.shape
    rows = w_fc1.shape[0]
    ff = w_fc1.shape[1]
    cuts = w_fc2.shape[0] // rows
    mem_rows = -(-memory.shape[0] // 16) * 16
    slots_used = jnp.where(page_class == 0, MEM_BIG, MEM_BIG // 4).astype(jnp.int32)

    norm_cols = jnp.concatenate([norm_gains, norm_biases], axis=0).T
    norm_cols = jnp.pad(norm_cols, ((0, 0), (0, 128 - norm_cols.shape[1])))
    first = jnp.concatenate([w_self_qkv, w_cross_kv, norm_cols], axis=1)
    second = jnp.concatenate([w_self_out, w_cross_q, w_cross_out], axis=1)
    up_local = (
        w_fc1.reshape(rows, nx, ny, cuts, rows).transpose(0, 3, 2, 1, 4).reshape(rows, ff)
    )
    down_local = jnp.concatenate(
        [w_fc2[c * rows : (c + 1) * rows] for c in range(cuts)], axis=1
    )
    w_first = gather_rows(first)
    w_second = gather_rows(second)
    wup = gather_rows(up_local)
    wdown = lax.all_gather(down_local, ("gy", "gx"), axis=0, tiled=True)

    wqkv = w_first[:, : 3 * d]
    wckv = w_first[:, 3 * d : 5 * d]
    norms = w_first[:, 5 * d : 5 * d + 6].T.astype(F32)
    gains, biases = norms[:3], norms[3:]
    wso, wcq, wco = w_second[:, :d], w_second[:, d : 2 * d], w_second[:, 2 * d :]

    place = jnp.arange(d)
    source = place % rows + ((place // rows) % nx * ny + place // (rows * nx)) * rows
    select = (source[:, None] == place[None, :]).astype(BF)

    def turned(a):
        return dot_nt(select, a).astype(BF)

    unit1, inv1 = norm_parts(hidden)
    h1 = (unit1 * gains[0] + biases[0]).astype(BF)
    qkv = dot(h1, wqkv).astype(BF)
    blocks = d // PAIR
    o, lse = attn_fwd((qkv, 0), qkv, blocks, 2 * blocks, lengths, True)
    x1 = hidden + dot(o, wso)
    unit2, inv2 = norm_parts(x1)
    h2 = (unit2 * gains[1] + biases[1]).astype(BF)
    qc = dot(h2, wcq).astype(BF)
    memory_pad = jnp.pad(memory, ((0, mem_rows - memory.shape[0]), (0, 0)))
    kvc = dot(memory_pad, wckv).astype(BF)
    o2, lse2 = attn_fwd((qc, 0), kvc, 0, blocks, slots_used, False)
    x2 = x1 + dot(o2, wco)
    unit3, inv3 = norm_parts(x2)
    h3 = (unit3 * gains[2] + biases[2]).astype(BF)
    u = dot(h3, wup)
    cdf = 0.5 * (1.0 + lax.erf(u * (0.5**0.5)))
    g = (u * cdf).astype(BF)
    slope = (cdf + u * (jnp.exp(-0.5 * u * u) * 0.3989422804014327)).astype(BF)
    result = x2
    for c in range(cuts):
        result = result + dot(g[:, c * d : (c + 1) * d], wdown[:, c * d : (c + 1) * d])

    valid = (jnp.arange(tokens) < lengths[0])[:, None].astype(F32)
    dout = cotangent * valid
    dy3 = dout.astype(BF)
    grad_down = jnp.concatenate(
        [dot_tn(g[:, c * d : (c + 1) * d], dy3).astype(BF) for c in range(cuts)], axis=1
    )
    own_down = scatter_rows(grad_down)
    dg = jnp.concatenate(
        [dot_nt(dy3, wdown[:, c * d : (c + 1) * d]) for c in range(cuts)], axis=1
    )
    du = (dg * slope.astype(F32)).astype(BF)
    grad_up = dot(turned(h3), du).astype(BF)
    own_up = scatter_rows(grad_up)
    dh3 = dot_nt(du, wup)
    back3, gain3, bias3 = norm_back(dh3, unit3, inv3, gains[2])
    dx2 = dout + back3
    dy2 = dx2.astype(BF)
    do2 = dot_nt(dy2, wco).astype(BF)
    dqc, dkc, dvc = attn_bwd((qc, 0), kvc, 0, blocks, o2, do2, lse2, slots_used, False)
    dkvc = jnp.concatenate([dkc, dvc], axis=1)
    mem_turned = turned(memory_pad)
    grad_mid = jnp.concatenate(
        [
            dot(turned(o2), dy2).astype(BF),
            dot(turned(h2), dqc).astype(BF),
            dot(mem_turned, dkvc).astype(BF),
        ],
        axis=1,
    )
    own_mid = scatter_rows(grad_mid)
    grad_memory = dot_nt(dkvc, wckv)[: memory.shape[0]]
    dh2 = dot_nt(dqc, wcq)
    back2, gain2, bias2 = norm_back(dh2, unit2, inv2, gains[1])
    dx1 = dx2 + back2
    dy1 = dx1.astype(BF)
    do = dot_nt(dy1, wso).astype(BF)
    dq, dk, dv = attn_bwd((qkv, 0), qkv, blocks, 2 * blocks, o, do, lse, lengths, True)
    dqkv = jnp.concatenate([dq, dk, dv], axis=1)
    dh1 = dot_nt(dqkv, wqkv)
    back1, gain1, bias1 = norm_back(dh1, unit1, inv1, gains[0])
    grad_hidden = dx1 + back1
    norm_grads = jnp.stack([gain1, gain2, gain3, bias1, bias2, bias3])
    norm_grads = jnp.pad(norm_grads, ((0, 122), (0, 0))).astype(BF)
    grad_last = jnp.concatenate(
        [
            dot(turned(o), dy1).astype(BF),
            dot(turned(h1), dqkv).astype(BF),
            turned(norm_grads),
        ],
        axis=1,
    )
    own_last = scatter_rows(grad_last)

    own_up = (
        own_up.reshape(rows, cuts, ny, nx, rows).transpose(0, 3, 2, 1, 4).reshape(rows, ff)
    )
    own_down = jnp.concatenate(
        [own_down[:, c * d : (c + 1) * d] for c in range(cuts)], axis=0
    )
    own_norms = own_last[:, 4 * d : 4 * d + 6].T.astype(F32)
    return (
        result,
        grad_hidden,
        grad_memory,
        own_last[:, d : 4 * d].astype(F32),
        own_last[:, :d].astype(F32),
        own_mid[:, d : 2 * d].astype(F32),
        own_mid[:, 2 * d :].astype(F32),
        own_mid[:, :d].astype(F32),
        own_up.astype(F32),
        own_down.astype(F32),
        own_norms[:3],
        own_norms[3:],
    )


def solution(mesh):
    row = P(ALL, None)
    col = P(None, ALL)
    return jax.shard_map(
        functools.partial(shards, nx=mesh.shape["gx"], ny=mesh.shape["gy"]),
        mesh=mesh,
        in_specs=(row, row, P(ALL), P(ALL), row) + (row,) * 7 + (col, col),
        out_specs=(row,) * 10 + (col, col),
        check_vma=False,
    )
```

```python
import functools

import jax
import jax.numpy as jnp
from jax import lax
from jax.experimental import pallas as pl
from jax.experimental.pallas import tpu as pltpu
from jax.sharding import PartitionSpec as P

HEADS = 16
MEM_BIG = 588
ALL = ("gx", "gy")
BF = jnp.bfloat16
F32 = jnp.float32
PAIR = 128


def dot(a, b):
    return jnp.dot(a, b, preferred_element_type=F32)


def dot_nt(a, b):
    return lax.dot_general(a, b, (((1,), (1,)), ((), ())), preferred_element_type=F32)


def dot_tn(a, b):
    return lax.dot_general(a, b, (((0,), (0,)), ((), ())), preferred_element_type=F32)


def run(kernel, grid, ins, outs, prefetch=(), scratch=(), deps=(), cost=None, name=None):
    count = len(prefetch) + len(ins)

    def body(*refs):
        return kernel(*refs[:count], *refs[count + len(deps) :])

    result = pl.pallas_call(
        body,
        grid_spec=pltpu.PrefetchScalarGridSpec(
            num_scalar_prefetch=len(prefetch),
            grid=grid,
            in_specs=[spec for _, spec in ins] + [pl.BlockSpec(memory_space=pl.ANY)] * len(deps),
            out_specs=[spec for _, spec in outs],
            scratch_shapes=scratch,
        ),
        out_shape=[shape for shape, _ in outs],
        compiler_params=pltpu.CompilerParams(
            dimension_semantics=("arbitrary",) * len(grid), vmem_limit_bytes=48 * 1024 * 1024
        ),
        cost_estimate=cost,
        name=name,
    )(*prefetch, *[a for a, _ in ins], *deps)
    return result if len(outs) > 1 else result[0]


def costs(flops, nbytes, transcendentals=0):
    return pl.CostEstimate(
        flops=flops, bytes_accessed=nbytes, transcendentals=transcendentals
    )


def shaped(shape, dtype):
    return jax.ShapeDtypeStruct(shape, dtype)


def allowed_t(key_count, q0, q1, limit, causal):
    key_at = lax.broadcasted_iota(jnp.int32, (key_count, q1 - q0), 0)
    ok = key_at < limit
    if causal:
        query_at = lax.broadcasted_iota(jnp.int32, (key_count, q1 - q0), 1) + q0
        ok = ok & (key_at <= query_at)
    return ok


def half_mask(width, half):
    lane = lax.broadcasted_iota(jnp.int32, (1, width), 1)
    return ((lane // (width // 2)) == half).astype(F32).astype(BF)


def attn_fwd_kernel(spans, causal, limit_ref, q_ref, k_ref, v_ref, o_ref, lse_ref):
    width = q_ref.shape[1]
    half = width // 2
    limit = limit_ref[0]
    scale = BF(half**-0.5)
    v_t = v_ref[...].T
    for q0, q1, keys in spans:
        query = q_ref[q0:q1, :] * scale
        ok = allowed_t(keys, q0, q1, limit, causal)
        outs = []
        for h in range(2):
            s = dot_nt(k_ref[:keys, :], query * half_mask(width, h))
            s = jnp.where(ok, s, -1e30)
            top = jnp.max(s, axis=0, keepdims=True)
            e = jnp.exp(s - top)
            total = jnp.sum(e, axis=0, keepdims=True)
            outs.append(dot(v_t[h * half : (h + 1) * half, :keys], e.astype(BF)) / total)
            lse_ref[0, h : h + 1, q0:q1] = top + jnp.log(total)
        o_ref[q0:q1, :] = jnp.concatenate(outs, axis=0).T.astype(BF)


def attn_bwd_kernel(
    spans, causal, limit_ref, q_ref, k_ref, v_ref, o_ref, do_ref, lse_ref, dq_ref, dk_ref, dv_ref
):
    width = q_ref.shape[1]
    half = width // 2
    limit = limit_ref[0]
    scale = BF(half**-0.5)
    k_t = k_ref[...].T * scale
    total_k = k_ref.shape[0]
    dk = jnp.zeros((total_k, width), F32)
    dv = jnp.zeros((total_k, width), F32)
    for q0, q1, keys in spans:
        query = q_ref[q0:q1, :] * scale
        grad_o = do_ref[q0:q1, :]
        ok = allowed_t(keys, q0, q1, limit, causal)
        both = (grad_o.astype(F32) * o_ref[q0:q1, :].astype(F32)).T
        outs = []
        dk_part = jnp.zeros((keys, width), F32)
        dv_part = jnp.zeros((keys, width), F32)
        for h in range(2):
            mask = half_mask(width, h)
            query_h = query * mask
            grad_h = grad_o * mask
            inner = jnp.sum(both[h * half : (h + 1) * half], axis=0, keepdims=True)
            s = dot_nt(k_ref[:keys, :], query_h)
            p = jnp.where(ok, jnp.exp(s - lse_ref[0, h : h + 1, q0:q1]), 0.0)
            dv_part += dot(p.astype(BF), grad_h)
            dp = dot_nt(v_ref[:keys, :], grad_h)
            ds = (p * (dp - inner)).astype(BF)
            dk_part += dot(ds, query_h)
            outs.append(dot(k_t[h * half : (h + 1) * half, :keys], ds))
        dq_ref[q0:q1, :] = jnp.concatenate(outs, axis=0).T.astype(BF)
        if keys < total_k:
            pad = jnp.zeros((total_k - keys, width), F32)
            dk_part = jnp.concatenate([dk_part, pad], axis=0)
            dv_part = jnp.concatenate([dv_part, pad], axis=0)
        dk += dk_part
        dv += dv_part
    dk_ref[...] = dk.astype(BF)
    dv_ref[...] = dv.astype(BF)


def make_spans(queries, keys, causal):
    step = 256
    return tuple(
        (q, q + step, min(q + step, keys) if causal else keys) for q in range(0, queries, step)
    )


def attn_fwd(q, kv, k_at, v_at, limit, causal, deps=()):
    q_arr, q_at = q
    queries, keys = q_arr.shape[0], kv.shape[0]
    pairs = HEADS // 2
    return run(
        functools.partial(attn_fwd_kernel, make_spans(queries, keys, causal), causal),
        (pairs,),
        [
            (q_arr, pl.BlockSpec((queries, PAIR), lambda p, _: (0, q_at + p))),
            (kv, pl.BlockSpec((keys, PAIR), lambda p, _: (0, k_at + p))),
            (kv, pl.BlockSpec((keys, PAIR), lambda p, _: (0, v_at + p))),
        ],
        [
            (
                shaped((queries, pairs * PAIR), BF),
                pl.BlockSpec((queries, PAIR), lambda p, _: (0, p)),
            ),
            (
                shaped((pairs, 2, queries), F32),
                pl.BlockSpec((1, 2, queries), lambda p, _: (p, 0, 0)),
            ),
        ],
        prefetch=(limit,),
        deps=deps,
        cost=costs(16 * queries * keys * 1024, 8 * queries * 1024, 16 * queries * keys),
        name="attn_fwd",
    )


def attn_bwd(q, kv, k_at, v_at, o, do, lse, limit, causal, deps=()):
    q_arr, q_at = q
    queries, keys = q_arr.shape[0], kv.shape[0]
    pairs = HEADS // 2
    q_block = pl.BlockSpec((queries, PAIR), lambda p, _: (0, p))
    k_block = pl.BlockSpec((keys, PAIR), lambda p, _: (0, p))
    return run(
        functools.partial(attn_bwd_kernel, make_spans(queries, keys, causal), causal),
        (pairs,),
        [
            (q_arr, pl.BlockSpec((queries, PAIR), lambda p, _: (0, q_at + p))),
            (kv, pl.BlockSpec((keys, PAIR), lambda p, _: (0, k_at + p))),
            (kv, pl.BlockSpec((keys, PAIR), lambda p, _: (0, v_at + p))),
            (o, q_block),
            (do, q_block),
            (lse, pl.BlockSpec((1, 2, queries), lambda p, _: (p, 0, 0))),
        ],
        [
            (shaped((queries, pairs * PAIR), BF), q_block),
            (shaped((keys, pairs * PAIR), BF), k_block),
            (shaped((keys, pairs * PAIR), BF), k_block),
        ],
        prefetch=(limit,),
        deps=deps,
        cost=costs(16 * queries * keys * 2560, 16 * queries * 1024, 16 * queries * keys),
        name="attn_bwd",
    )


def norm_parts(v):
    center = v - jnp.mean(v, -1, keepdims=True)
    inverse = lax.rsqrt(jnp.mean(center * center, -1, keepdims=True) + 1e-05)
    return center * inverse, inverse


def norm_back(grad, unit, inverse, gain):
    gain_grad = jnp.sum(grad * unit, axis=0)
    bias_grad = jnp.sum(grad, axis=0)
    scaled = grad * gain
    mean_a = jnp.mean(scaled, -1, keepdims=True)
    mean_b = jnp.mean(scaled * unit, -1, keepdims=True)
    return inverse * (scaled - mean_a - unit * mean_b), gain_grad, bias_grad


def gather_rows(w):
    return lax.all_gather(w, ALL, axis=0, tiled=True)


def scatter_rows(g):
    part = lax.psum_scatter(g, "gy", scatter_dimension=0, tiled=True)
    return lax.psum_scatter(part, "gx", scatter_dimension=0, tiled=True)


def shards_any(
    hidden,
    memory,
    lengths,
    page_class,
    cotangent,
    w_self_qkv,
    w_self_out,
    w_cross_q,
    w_cross_kv,
    w_cross_out,
    w_fc1,
    w_fc2,
    norm_gains,
    norm_biases,
    *,
    nx,
    ny,
):
    n = nx * ny
    tokens, d = hidden.shape
    rows = w_fc1.shape[0]
    ff = w_fc1.shape[1]
    cuts = w_fc2.shape[0] // rows
    mem_rows = -(-memory.shape[0] // 16) * 16
    slots_used = jnp.where(page_class == 0, MEM_BIG, MEM_BIG // 4).astype(jnp.int32)

    norm_cols = jnp.concatenate([norm_gains, norm_biases], axis=0).T
    norm_cols = jnp.pad(norm_cols, ((0, 0), (0, 128 - norm_cols.shape[1])))
    first = jnp.concatenate([w_self_qkv, w_cross_kv, norm_cols], axis=1)
    second = jnp.concatenate([w_self_out, w_cross_q, w_cross_out], axis=1)
    up_local = (
        w_fc1.reshape(rows, nx, ny, cuts, rows).transpose(0, 3, 2, 1, 4).reshape(rows, ff)
    )
    down_local = jnp.concatenate(
        [w_fc2[c * rows : (c + 1) * rows] for c in range(cuts)], axis=1
    )
    w_first = gather_rows(first)
    w_second = gather_rows(second)
    wup = gather_rows(up_local)
    wdown = lax.all_gather(down_local, ("gy", "gx"), axis=0, tiled=True)

    wqkv = w_first[:, : 3 * d]
    wckv = w_first[:, 3 * d : 5 * d]
    norms = w_first[:, 5 * d : 5 * d + 6].T.astype(F32)
    gains, biases = norms[:3], norms[3:]
    wso, wcq, wco = w_second[:, :d], w_second[:, d : 2 * d], w_second[:, 2 * d :]

    place = jnp.arange(d)
    source = place % rows + ((place // rows) % nx * ny + place // (rows * nx)) * rows
    select = (source[:, None] == place[None, :]).astype(BF)

    def turned(a):
        return dot_nt(select, a).astype(BF)

    unit1, inv1 = norm_parts(hidden)
    h1 = (unit1 * gains[0] + biases[0]).astype(BF)
    qkv = dot(h1, wqkv).astype(BF)
    blocks = d // PAIR
    o, lse = attn_fwd((qkv, 0), qkv, blocks, 2 * blocks, lengths, True)
    x1 = hidden + dot(o, wso)
    unit2, inv2 = norm_parts(x1)
    h2 = (unit2 * gains[1] + biases[1]).astype(BF)
    qc = dot(h2, wcq).astype(BF)
    memory_pad = jnp.pad(memory, ((0, mem_rows - memory.shape[0]), (0, 0)))
    kvc = dot(memory_pad, wckv).astype(BF)
    o2, lse2 = attn_fwd((qc, 0), kvc, 0, blocks, slots_used, False)
    x2 = x1 + dot(o2, wco)
    unit3, inv3 = norm_parts(x2)
    h3 = (unit3 * gains[2] + biases[2]).astype(BF)
    u = dot(h3, wup)
    cdf = 0.5 * (1.0 + lax.erf(u * (0.5**0.5)))
    g = (u * cdf).astype(BF)
    slope = (cdf + u * (jnp.exp(-0.5 * u * u) * 0.3989422804014327)).astype(BF)
    result = x2
    for c in range(cuts):
        result = result + dot(g[:, c * d : (c + 1) * d], wdown[:, c * d : (c + 1) * d])

    valid = (jnp.arange(tokens) < lengths[0])[:, None].astype(F32)
    dout = cotangent * valid
    dy3 = dout.astype(BF)
    grad_down = jnp.concatenate(
        [dot_tn(g[:, c * d : (c + 1) * d], dy3).astype(BF) for c in range(cuts)], axis=1
    )
    own_down = scatter_rows(grad_down)
    dg = jnp.concatenate(
        [dot_nt(dy3, wdown[:, c * d : (c + 1) * d]) for c in range(cuts)], axis=1
    )
    du = (dg * slope.astype(F32)).astype(BF)
    grad_up = dot(turned(h3), du).astype(BF)
    own_up = scatter_rows(grad_up)
    dh3 = dot_nt(du, wup)
    back3, gain3, bias3 = norm_back(dh3, unit3, inv3, gains[2])
    dx2 = dout + back3
    dy2 = dx2.astype(BF)
    do2 = dot_nt(dy2, wco).astype(BF)
    dqc, dkc, dvc = attn_bwd((qc, 0), kvc, 0, blocks, o2, do2, lse2, slots_used, False)
    dkvc = jnp.concatenate([dkc, dvc], axis=1)
    mem_turned = turned(memory_pad)
    grad_mid = jnp.concatenate(
        [
            dot(turned(o2), dy2).astype(BF),
            dot(turned(h2), dqc).astype(BF),
            dot(mem_turned, dkvc).astype(BF),
        ],
        axis=1,
    )
    own_mid = scatter_rows(grad_mid)
    grad_memory = dot_nt(dkvc, wckv)[: memory.shape[0]]
    dh2 = dot_nt(dqc, wcq)
    back2, gain2, bias2 = norm_back(dh2, unit2, inv2, gains[1])
    dx1 = dx2 + back2
    dy1 = dx1.astype(BF)
    do = dot_nt(dy1, wso).astype(BF)
    dq, dk, dv = attn_bwd((qkv, 0), qkv, blocks, 2 * blocks, o, do, lse, lengths, True)
    dqkv = jnp.concatenate([dq, dk, dv], axis=1)
    dh1 = dot_nt(dqkv, wqkv)
    back1, gain1, bias1 = norm_back(dh1, unit1, inv1, gains[0])
    grad_hidden = dx1 + back1
    norm_grads = jnp.stack([gain1, gain2, gain3, bias1, bias2, bias3])
    norm_grads = jnp.pad(norm_grads, ((0, 122), (0, 0))).astype(BF)
    grad_last = jnp.concatenate(
        [
            dot(turned(o), dy1).astype(BF),
            dot(turned(h1), dqkv).astype(BF),
            turned(norm_grads),
        ],
        axis=1,
    )
    own_last = scatter_rows(grad_last)

    own_up = (
        own_up.reshape(rows, cuts, ny, nx, rows).transpose(0, 3, 2, 1, 4).reshape(rows, ff)
    )
    own_down = jnp.concatenate(
        [own_down[:, c * d : (c + 1) * d] for c in range(cuts)], axis=0
    )
    own_norms = own_last[:, 4 * d : 4 * d + 6].T.astype(F32)
    return (
        result,
        grad_hidden,
        grad_memory,
        own_last[:, d : 4 * d].astype(F32),
        own_last[:, :d].astype(F32),
        own_mid[:, d : 2 * d].astype(F32),
        own_mid[:, 2 * d :].astype(F32),
        own_mid[:, :d].astype(F32),
        own_up.astype(F32),
        own_down.astype(F32),
        own_norms[:3],
        own_norms[3:],
    )


CORE, XBIT, YBIT = 1, 2, 4


def swap(a, bit):
    return lax.ppermute(a, ALL, [(i, i ^ bit) for i in range(32)])


def part_kernel(lo, src, out):
    out[...] = src[lo : lo + 2]


def part_of(piece, lo, deps):
    _, rows, columns = piece.shape
    block = 640 if columns % 640 == 0 else 1024
    return run(
        functools.partial(part_kernel, lo),
        (columns // block,),
        [(piece, pl.BlockSpec((4, rows, block), lambda j: (0, 0, j)))],
        [(shaped((2, rows, columns), BF), pl.BlockSpec((2, rows, block), lambda j: (0, 0, j)))],
        deps=deps,
        cost=costs(0, 12 * rows * columns),
        name="part_of",
    )


def gather_start(w):
    here = lax.all_gather(w, "gx", axis=0)
    return here, swap(here, XBIT), swap(here, YBIT)


def gather_end(pieces, deps=()):
    here, from_x, from_y = pieces
    if deps:
        low, high = part_of(from_y, 0, deps), part_of(from_x, 2, deps)
    else:
        low, high = from_y[:2], from_x[2:]
    own = [here, from_x, from_y, swap(low, XBIT), swap(high, YBIT)]
    return own + [swap(p, CORE) for p in own]


def place_kernel(by_core, bits_ref, *refs):
    out = refs[-1]
    x, y, core = bits_ref[0], bits_ref[1], bits_ref[2]
    for k in range(10):
        at_core = core if k < 5 else 1 - core
        at_x = x if k % 5 in (0, 2) else 1 - x
        at_y = y if k % 5 in (0, 1) else 1 - y
        z0, z1 = {3: (0, 2), 4: (2, 4)}.get(k % 5, (0, 4))
        if by_core:
            out[at_core * 4 + at_y * 2 + at_x, z0:z1] = refs[k][...]
        else:
            out[z0:z1, at_y * 4 + at_x * 2 + at_core] = refs[k][...]


def place(pieces, start, width, bits, by_core=False, deps=()):
    rows = pieces[0].shape[1]
    block = min(width, 512)
    lead = (8, 4) if by_core else (4, 8)
    out = run(
        functools.partial(place_kernel, by_core),
        (width // block,),
        [
            (p, pl.BlockSpec((p.shape[0], rows, block), lambda j, _: (0, 0, start // block + j)))
            for p in pieces
        ],
        [
            (
                shaped(lead + (rows, width), BF),
                pl.BlockSpec(lead + (rows, block), lambda j, _: (0, 0, 0, j)),
            )
        ],
        prefetch=(bits,),
        deps=deps,
        cost=costs(0, 4 * 32 * rows * width),
        name="place",
    )
    return out.reshape(32 * rows, width)


def wgrad_kernel(starts, *refs):
    out = refs[-1]
    j = pl.program_id(0)
    for s in range(len(starts) - 1):
        a, a2, g, g2 = refs[4 * s : 4 * s + 4]

        @pl.when((j >= starts[s]) & (j < starts[s + 1]))
        def _(a=a, a2=a2, g=g, g2=g2):
            out[...] = (dot(a[...], g[...]) + dot(a2[...], g2[...])).astype(BF)


def wgrad(segments, deps=(), block=512):
    starts, ins = [0], []
    for a, a2, g, g2 in segments:
        per = g.shape[2] // block
        count, start = g.shape[0] * per, starts[-1]

        def at(j, start=start, count=count, per=per):
            k = jnp.clip(j - start, 0, count - 1)
            return (k // per, 0, k % per)

        whole = pl.BlockSpec(a.shape, lambda j: (0, 0))
        grads = pl.BlockSpec((None, g.shape[1], block), at)
        ins += [(a, whole), (a2, whole), (g, grads), (g2, grads)]
        starts.append(start + count)
    rows = segments[0][0].shape[0]
    columns = starts[-1] * block
    return run(
        functools.partial(wgrad_kernel, tuple(starts)),
        (starts[-1],),
        ins,
        [(shaped((rows, columns), BF), pl.BlockSpec((rows, block), lambda j: (0, j)))],
        deps=deps,
        cost=costs(2 * rows * 1024 * columns, 4 * 512 * columns + 2 * rows * columns),
        name="wgrad",
    )


def wgrad_down_kernel(bits_ref, *refs):
    blocks, other, dy, dy2, out = refs[:4], refs[4:8], refs[8], refs[9], refs[10]
    mine = jnp.concatenate([r[...].T for r in blocks], axis=0)
    theirs = jnp.concatenate([r[...].T for r in other], axis=0)
    out[...] = (dot(mine, dy[...]) + dot(theirs, dy2[...])).astype(BF)


def wgrad_down(bits, g, g_other, dy, dy_other, cuts):
    tokens, d = dy.shape

    def spec(rel, whole):
        def at(b, bits_ref):
            x = bits_ref[0] ^ (rel & 1)
            y = bits_ref[1] ^ (rel >> 1)
            block = b * 4 + y * 2 + x
            return (0, bits_ref[2] * 4 * cuts + block if whole else block)

        return pl.BlockSpec((tokens, 128), at)

    rows = pl.BlockSpec((tokens, d), lambda b, _: (0, 0))
    return run(
        wgrad_down_kernel,
        (cuts,),
        [(g, spec(r, True)) for r in range(4)]
        + [(g_other, spec(r, False)) for r in range(4)]
        + [(dy, rows), (dy_other, rows)],
        [(shaped((512, cuts * d), BF), pl.BlockSpec((512, d), lambda b, _: (0, b)))],
        prefetch=(bits,),
        cost=costs(2 * 512 * 1024 * cuts * d, 16 * tokens * d),
        name="wgrad_down",
    )


def up_kernel(h_ref, w_ref, g_ref, slope_ref):
    u = dot(h_ref[...], w_ref[...])
    cdf = 0.5 * (1.0 + lax.erf(u * (0.5**0.5)))
    g_ref[...] = (u * cdf).astype(BF)
    slope_ref[...] = (cdf + u * (jnp.exp(-0.5 * u * u) * 0.3989422804014327)).astype(BF)


def feed_up(h, w, block=512):
    tokens, d = h.shape
    ff = w.shape[1]
    out = (shaped((tokens, ff), BF), pl.BlockSpec((tokens, block), lambda j: (0, j)))
    return run(
        up_kernel,
        (ff // block,),
        [
            (h, pl.BlockSpec((tokens, d), lambda j: (0, 0))),
            (w, pl.BlockSpec((d, block), lambda j: (0, j))),
        ],
        [out, out],
        cost=costs(2 * tokens * d * ff, 2 * d * ff + 4 * tokens * ff, 2 * tokens * ff),
        name="feed_up",
    )


def down_kernel(g_ref, w_ref, x_ref, out_ref):
    @pl.when(pl.program_id(0) == 0)
    def _():
        out_ref[...] = x_ref[...]

    out_ref[...] += dot(g_ref[...], w_ref[...])


def feed_down(g, w, x, cuts, deps=()):
    tokens, d = x.shape
    block = d // 2
    whole = pl.BlockSpec((tokens, d), lambda j: (0, 0))
    return run(
        down_kernel,
        (2 * cuts,),
        [
            (g, pl.BlockSpec((tokens, block), lambda j: (0, j))),
            (w, pl.BlockSpec((block, d), lambda j: (j // cuts, j % cuts))),
            (x, whole),
        ],
        [(shaped((tokens, d), F32), whole)],
        deps=deps,
        cost=costs(2 * tokens * d * d * cuts, 2 * d * d * cuts + 10 * tokens * d),
        name="feed_down",
    )


def norm_back_store(dh, x_ref, gain_ref, res_ref, dx_ref, low_ref, sums_ref):
    x = x_ref[...]
    center = x - jnp.mean(x, -1, keepdims=True)
    inverse = lax.rsqrt(jnp.mean(center * center, -1, keepdims=True) + 1e-05)
    unit = center * inverse
    sums_ref[0:1, :] = jnp.sum(dh * unit, axis=0, keepdims=True)
    sums_ref[1:2, :] = jnp.sum(dh, axis=0, keepdims=True)
    scaled = dh * gain_ref[...]
    mean_a = jnp.mean(scaled, -1, keepdims=True)
    mean_b = jnp.mean(scaled * unit, -1, keepdims=True)
    dx = res_ref[...] + inverse * (scaled - mean_a - unit * mean_b)
    dx_ref[...] = dx
    if low_ref is not None:
        low_ref[...] = dx.astype(BF)


def accumulate(acc, part):
    j = pl.program_id(0)

    @pl.when(j == 0)
    def _():
        acc[...] = part

    @pl.when(j > 0)
    def _():
        acc[...] += part


def feed_back_kernel(
    dy_ref, w2_ref, slope_ref, w1_ref, x_ref, gain_ref, res_ref, du_ref, dx_ref, low_ref, sums_ref, acc
):
    du = (dot_nt(dy_ref[...], w2_ref[...]) * slope_ref[...].astype(F32)).astype(BF)
    du_ref[...] = du
    accumulate(acc, dot_nt(du, w1_ref[...]))

    @pl.when(pl.program_id(0) == pl.num_programs(0) - 1)
    def _():
        norm_back_store(acc[...], x_ref, gain_ref, res_ref, dx_ref, low_ref, sums_ref)


def feed_back(dy, w2, slope, w1, x, gain, res, cuts, deps=()):
    tokens, d = x.shape
    block = d // 2
    ff = w1.shape[1]
    whole = pl.BlockSpec((tokens, d), lambda j: (0, 0))
    part = pl.BlockSpec((tokens, block), lambda j: (0, j))
    return run(
        feed_back_kernel,
        (2 * cuts,),
        [
            (dy, whole),
            (w2, pl.BlockSpec((block, d), lambda j: (j // cuts, j % cuts))),
            (slope, part),
            (w1, pl.BlockSpec((d, block), lambda j: (0, j))),
            (x, whole),
            (gain, pl.BlockSpec((1, d), lambda j: (0, 0))),
            (res, whole),
        ],
        [
            (shaped((tokens, ff), BF), part),
            (shaped((tokens, d), F32), whole),
            (shaped((tokens, d), BF), whole),
            (shaped((2, d), F32), pl.BlockSpec((2, d), lambda j: (0, 0))),
        ],
        scratch=[pltpu.VMEM((tokens, d), F32)],
        deps=deps,
        cost=costs(4 * tokens * d * ff, 4 * d * ff + 4 * tokens * ff + 16 * tokens * d),
        name="feed_back",
    )


def norm_back_kernel(g_ref, w_ref, x_ref, gain_ref, res_ref, *refs):
    dx_ref, sums_ref, acc = refs[0], refs[-2], refs[-1]
    low_ref = refs[1] if len(refs) == 4 else None
    accumulate(acc, dot_nt(g_ref[...], w_ref[...]))

    @pl.when(pl.program_id(0) == pl.num_programs(0) - 1)
    def _():
        norm_back_store(acc[...], x_ref, gain_ref, res_ref, dx_ref, low_ref, sums_ref)


def through_norm(g, w, x, gain, res, low=True, deps=()):
    tokens, d = x.shape
    block = 512
    per = g.shape[2] // block
    count = g.shape[0] * per
    whole = pl.BlockSpec((tokens, d), lambda j: (0, 0))
    outs = [(shaped((tokens, d), F32), whole)]
    if low:
        outs.append((shaped((tokens, d), BF), whole))
    outs.append((shaped((2, d), F32), pl.BlockSpec((2, d), lambda j: (0, 0))))
    return run(
        norm_back_kernel,
        (count,),
        [
            (g, pl.BlockSpec((None, tokens, block), lambda j: (j // per, 0, j % per))),
            (w, pl.BlockSpec((d, block), lambda j: (0, j))),
            (x, whole),
            (gain, pl.BlockSpec((1, d), lambda j: (0, 0))),
            (res, whole),
        ],
        outs,
        scratch=[pltpu.VMEM((tokens, d), F32)],
        deps=deps,
        cost=costs(2 * tokens * d * block * count, 2 * d * block * count + 16 * tokens * d),
        name="through_norm",
    )


def scatter_diag(grad, rows):
    parts = grad.reshape(4, 4, rows, grad.shape[1])
    from_x, from_y = swap(parts[3, :2], XBIT), swap(parts[3, 2:], YBIT)
    to_x = jnp.concatenate([parts[1, :2], parts[1, 2:] + from_y], axis=0)
    to_y = jnp.concatenate([parts[2, :2] + from_x, parts[2, 2:]], axis=0)
    return parts[0], to_x, to_y


def scatter_plane(stage):
    here, to_x, to_y = stage
    got_x, got_y = swap(to_x, XBIT), swap(to_y, YBIT)
    total = here.astype(F32) + got_x.astype(F32) + got_y.astype(F32)
    return total.astype(BF).reshape(-1, here.shape[2])


def scatter_line(total):
    return lax.psum_scatter(total, "gx", scatter_dimension=0, tiled=True)


def shards_plane(
    hidden,
    memory,
    lengths,
    page_class,
    cotangent,
    w_self_qkv,
    w_self_out,
    w_cross_q,
    w_cross_kv,
    w_cross_out,
    w_fc1,
    w_fc2,
    norm_gains,
    norm_biases,
):
    tokens, d = hidden.shape
    rows, ff = w_fc1.shape
    cuts = w_fc2.shape[0] // rows
    mem_rows = -(-memory.shape[0] // 16) * 16
    slots_used = jnp.where(page_class == 0, MEM_BIG, MEM_BIG // 4).astype(jnp.int32)
    along = lax.axis_index("gy")
    x_at, y_at, core = (along // 2) % 2, along // 4, along % 2
    bits = jnp.stack([x_at, y_at, core]).astype(jnp.int32)

    norm_cols = jnp.concatenate([norm_gains, norm_biases], axis=0).T
    norm_cols = jnp.pad(norm_cols, ((0, 0), (0, 128 - norm_cols.shape[1])))
    up_local = (
        w_fc1.reshape(rows, 4, 2, 2, 2, cuts, rows)
        .transpose(0, 4, 5, 2, 3, 1, 6)
        .reshape(rows, ff)
    )
    down_local = jnp.concatenate(
        [w_fc2[c * rows : (c + 1) * rows] for c in range(cuts)], axis=1
    )
    first = gather_start(jnp.concatenate([w_self_qkv, norm_cols], axis=1))
    second = gather_start(
        jnp.concatenate([w_cross_kv, w_self_out, w_cross_q, w_cross_out], axis=1)
    )
    third = gather_start(up_local)
    fourth = gather_start(down_local)

    place_at = jnp.arange(d)
    r = place_at % rows
    z = (place_at // rows) % 4
    rel = (place_at // (4 * rows)) % 4
    source_core = core ^ (place_at // (16 * rows))
    device = z * 8 + (y_at ^ (rel // 2)) * 4 + (x_at ^ (rel % 2)) * 2 + source_core
    select = ((device * rows + r)[:, None] == place_at[None, :]).astype(BF)
    half = d // 2

    def turned(a):
        t = dot_nt(select, a).astype(BF)
        return t[:half], swap(t[half:], CORE)

    first = gather_end(first)
    wqkv = place(first, 0, 3 * d, bits)
    norms = place(first, 3 * d, 128, bits)[:, :6].T.astype(F32)
    gains, biases = norms[:3], norms[3:]
    unit1, _ = norm_parts(hidden)
    h1 = (unit1 * gains[0] + biases[0]).astype(BF)
    qkv = dot(h1, wqkv).astype(BF)
    blocks = d // PAIR
    o, lse = attn_fwd((qkv, 0), qkv, blocks, 2 * blocks, lengths, True)
    second = gather_end(second, (qkv,))
    wckv = place(second, 0, 2 * d, bits, deps=(o,))
    wso, wcq, wco = (place(second, k * d, d, bits, deps=(o,)) for k in (2, 3, 4))
    x1 = hidden + dot(o, wso)
    unit2, _ = norm_parts(x1)
    h2 = (unit2 * gains[1] + biases[1]).astype(BF)
    qc = dot(h2, wcq).astype(BF)
    third = gather_end(third, (qc,))
    memory_pad = jnp.pad(memory, ((0, mem_rows - memory.shape[0]), (0, 0)))
    kvc = dot(memory_pad, wckv).astype(BF)
    o2, lse2 = attn_fwd((qc, 0), kvc, 0, blocks, slots_used, False)
    x2 = x1 + dot(o2, wco)
    unit3, _ = norm_parts(x2)
    h3 = (unit3 * gains[2] + biases[2]).astype(BF)
    fourth = gather_end(fourth, (h3,))
    wup = place(third, 0, ff, bits, deps=(o2,))
    g, slope = feed_up(h3, wup)
    h1_t, o_t, h2_t, o2_t, h3_t = turned(h1), turned(o), turned(h2), turned(o2), turned(h3)
    mem_t = turned(memory_pad)

    valid = (jnp.arange(tokens) < lengths[0])[:, None].astype(F32)
    dout = cotangent * valid
    dy3 = dout.astype(BF)
    g_other = swap(lax.dynamic_slice_in_dim(g, (1 - core) * (ff // 2), ff // 2, 1), CORE)
    dy3_other = swap(dy3, CORE)
    grad_down = wgrad_down(bits, g, g_other, dy3, dy3_other, cuts)
    wdown = place(fourth, 0, cuts * d, bits, True, deps=(grad_down,))
    stage1 = scatter_diag(grad_down, rows)
    du, dx2, dy2, sums3 = feed_back(dy3, wdown, slope, wup, x2, gains[2:3], dout, cuts)
    do2 = dot_nt(dy2, wco).astype(BF)
    dqc, dkc, dvc = attn_bwd(
        (qc, 0), kvc, 0, blocks, o2, do2, lse2, slots_used, False, deps=stage1[1:]
    )
    dkvc = jnp.stack([dkc, dvc])
    grad_up = wgrad([h3_t + (du[None], swap(du, CORE)[None])], deps=(dqc,))
    stage2 = scatter_diag(grad_up, rows)
    dx1, dy1, sums2 = through_norm(
        dqc[None], wcq, x1, gains[1:2], dx2, deps=(grad_up,)
    )
    total1 = scatter_plane(stage1)
    own_down = scatter_line(total1)
    grad_mid = wgrad(
        [
            o2_t + (dy2[None], swap(dy2, CORE)[None]),
            h2_t + (dqc[None], swap(dqc, CORE)[None]),
            mem_t + (dkvc, swap(dkvc, CORE)),
        ],
        deps=(total1, dy1),
    )
    stage3 = scatter_diag(grad_mid, rows)
    do = dot_nt(dy1, wso).astype(BF)
    dqkv = jnp.stack(
        attn_bwd(
            (qkv, 0), qkv, blocks, 2 * blocks, o, do, lse, lengths, True,
            deps=stage2[1:] + (grad_mid,),
        )
    )
    total2 = scatter_plane(stage2)
    own_up = scatter_line(total2)
    grad_hidden, sums1 = through_norm(dqkv, wqkv, hidden, gains[0:1], dx1, low=False)
    sums = jnp.concatenate([sums1, sums2, sums3], axis=0)
    sums = jnp.pad(sums, ((0, 122), (0, 0))).astype(BF)
    sums_t, sums_other = turned(sums)
    grad_last = jnp.concatenate(
        [
            wgrad(
                [
                    o_t + (dy1[None], swap(dy1, CORE)[None]),
                    h1_t + (dqkv, swap(dqkv, CORE)),
                ],
                deps=stage3[1:] + (total2,),
            ),
            (sums_t.astype(F32) + sums_other.astype(F32)).astype(BF),
        ],
        axis=1,
    )
    own_mid = scatter_line(scatter_plane(stage3))
    stage4 = scatter_diag(grad_last, rows)
    result = feed_down(g, wdown, x2, cuts, deps=(grad_last,))
    own_last = scatter_line(scatter_plane(stage4))
    grad_memory = (dot_nt(dkc, wckv[:, :d]) + dot_nt(dvc, wckv[:, d:]))[: memory.shape[0]]

    own_up = (
        own_up.reshape(rows, 2, cuts, 2, 2, 4, rows)
        .transpose(0, 5, 3, 4, 1, 2, 6)
        .reshape(rows, ff)
    )
    own_down = jnp.concatenate(
        [own_down[:, c * d : (c + 1) * d] for c in range(cuts)], axis=0
    )
    own_sums = own_last[:, 4 * d : 4 * d + 6].T.astype(F32)
    return (
        result,
        grad_hidden,
        grad_memory,
        own_last[:, d : 4 * d].astype(F32),
        own_last[:, :d].astype(F32),
        own_mid[:, d : 2 * d].astype(F32),
        own_mid[:, 2 * d :].astype(F32),
        own_mid[:, :d].astype(F32),
        own_up.astype(F32),
        own_down.astype(F32),
        own_sums[0::2],
        own_sums[1::2],
    )


def solution(mesh):
    row = P(ALL, None)
    col = P(None, ALL)
    nx, ny = mesh.shape["gx"], mesh.shape["gy"]
    body = shards_plane if (nx, ny) == (4, 8) else functools.partial(shards_any, nx=nx, ny=ny)
    return jax.shard_map(
        body,
        mesh=mesh,
        in_specs=(row, row, P(ALL), P(ALL), row) + (row,) * 7 + (col, col),
        out_specs=(row,) * 10 + (col, col),
        check_vma=False,
    )
```

```python
import functools

import jax
import jax.numpy as jnp
from jax import lax
from jax.experimental import pallas as pl
from jax.experimental.pallas import tpu as pltpu
from jax.sharding import PartitionSpec as P

HEADS = 16
MEM_BIG = 588
ALL = ("gx", "gy")
BF = jnp.bfloat16
F32 = jnp.float32
PAIR = 128


def dot(a, b):
    return jnp.dot(a, b, preferred_element_type=F32)


def dot_nt(a, b):
    return lax.dot_general(a, b, (((1,), (1,)), ((), ())), preferred_element_type=F32)


def dot_tn(a, b):
    return lax.dot_general(a, b, (((0,), (0,)), ((), ())), preferred_element_type=F32)


def run(
    kernel, grid, ins, outs, prefetch=(), scratch=(), deps=(), cost=None, name=None, vmem=30
):
    count = len(prefetch) + len(ins)

    def body(*refs):
        return kernel(*refs[:count], *refs[count + len(deps) :])

    result = pl.pallas_call(
        body,
        grid_spec=pltpu.PrefetchScalarGridSpec(
            num_scalar_prefetch=len(prefetch),
            grid=grid,
            in_specs=[spec for _, spec in ins] + [pl.BlockSpec(memory_space=pl.ANY)] * len(deps),
            out_specs=[spec for _, spec in outs],
            scratch_shapes=scratch,
        ),
        out_shape=[shape for shape, _ in outs],
        compiler_params=pltpu.CompilerParams(
            dimension_semantics=("arbitrary",) * len(grid), vmem_limit_bytes=vmem * 1024 * 1024
        ),
        cost_estimate=cost,
        name=name,
    )(*prefetch, *[a for a, _ in ins], *deps)
    return result if len(outs) > 1 else result[0]


def costs(flops, nbytes, transcendentals=0):
    return pl.CostEstimate(
        flops=flops, bytes_accessed=nbytes, transcendentals=transcendentals
    )


def shaped(shape, dtype):
    return jax.ShapeDtypeStruct(shape, dtype)


def allowed_t(key_count, q0, q1, limit, causal):
    key_at = lax.broadcasted_iota(jnp.int32, (key_count, q1 - q0), 0)
    ok = key_at < limit
    if causal:
        query_at = lax.broadcasted_iota(jnp.int32, (key_count, q1 - q0), 1) + q0
        ok = ok & (key_at <= query_at)
    return ok


def half_mask(width, half):
    lane = lax.broadcasted_iota(jnp.int32, (1, width), 1)
    return ((lane // (width // 2)) == half).astype(F32).astype(BF)


def attn_fwd_kernel(spans, causal, limit_ref, q_ref, k_ref, v_ref, o_ref, lse_ref):
    width = q_ref.shape[1]
    half = width // 2
    limit = limit_ref[0]
    scale = BF(half**-0.5)
    v_t = v_ref[...].T
    for q0, q1, keys in spans:
        query = q_ref[q0:q1, :] * scale
        ok = allowed_t(keys, q0, q1, limit, causal)
        outs = []
        for h in range(2):
            s = dot_nt(k_ref[:keys, :], query * half_mask(width, h))
            s = jnp.where(ok, s, -1e30)
            top = jnp.max(s, axis=0, keepdims=True)
            e = jnp.exp(s - top)
            total = jnp.sum(e, axis=0, keepdims=True)
            outs.append(dot(v_t[h * half : (h + 1) * half, :keys], e.astype(BF)) / total)
            lse_ref[0, h : h + 1, q0:q1] = top + jnp.log(total)
        o_ref[q0:q1, :] = jnp.concatenate(outs, axis=0).T.astype(BF)


def attn_bwd_kernel(
    spans, causal, limit_ref, q_ref, k_ref, v_ref, o_ref, do_ref, lse_ref, *outs_ref
):
    dq_ref = outs_ref[0].at[0]
    dk_ref, dv_ref = (outs_ref[-1].at[k - 2 + outs_ref[-1].shape[0]] for k in range(2))
    width = q_ref.shape[1]
    half = width // 2
    limit = limit_ref[0]
    scale = BF(half**-0.5)
    k_t = k_ref[...].T * scale
    total_k = k_ref.shape[0]
    dk = jnp.zeros((total_k, width), F32)
    dv = jnp.zeros((total_k, width), F32)
    for q0, q1, keys in spans:
        query = q_ref[q0:q1, :] * scale
        grad_o = do_ref[q0:q1, :]
        ok = allowed_t(keys, q0, q1, limit, causal)
        both = (grad_o.astype(F32) * o_ref[q0:q1, :].astype(F32)).T
        outs = []
        dk_part = jnp.zeros((keys, width), F32)
        dv_part = jnp.zeros((keys, width), F32)
        for h in range(2):
            mask = half_mask(width, h)
            query_h = query * mask
            grad_h = grad_o * mask
            inner = jnp.sum(both[h * half : (h + 1) * half], axis=0, keepdims=True)
            s = dot_nt(k_ref[:keys, :], query_h)
            p = jnp.where(ok, jnp.exp(s - lse_ref[0, h : h + 1, q0:q1]), 0.0)
            dv_part += dot(p.astype(BF), grad_h)
            dp = dot_nt(v_ref[:keys, :], grad_h)
            ds = (p * (dp - inner)).astype(BF)
            dk_part += dot(ds, query_h)
            outs.append(dot(k_t[h * half : (h + 1) * half, :keys], ds))
        dq_ref[q0:q1, :] = jnp.concatenate(outs, axis=0).T.astype(BF)
        if keys < total_k:
            pad = jnp.zeros((total_k - keys, width), F32)
            dk_part = jnp.concatenate([dk_part, pad], axis=0)
            dv_part = jnp.concatenate([dv_part, pad], axis=0)
        dk += dk_part
        dv += dv_part
    dk_ref[...] = dk.astype(BF)
    dv_ref[...] = dv.astype(BF)


def make_spans(queries, keys, causal):
    step = 256
    return tuple(
        (q, q + step, min(q + step, keys) if causal else keys) for q in range(0, queries, step)
    )


def attn_fwd(q, kv, k_at, v_at, limit, causal, deps=()):
    q_arr, q_at = q
    queries, keys = q_arr.shape[0], kv.shape[0]
    pairs = HEADS // 2
    return run(
        functools.partial(attn_fwd_kernel, make_spans(queries, keys, causal), causal),
        (pairs,),
        [
            (q_arr, pl.BlockSpec((queries, PAIR), lambda p, _: (0, q_at + p))),
            (kv, pl.BlockSpec((keys, PAIR), lambda p, _: (0, k_at + p))),
            (kv, pl.BlockSpec((keys, PAIR), lambda p, _: (0, v_at + p))),
        ],
        [
            (
                shaped((queries, pairs * PAIR), BF),
                pl.BlockSpec((queries, PAIR), lambda p, _: (0, p)),
            ),
            (
                shaped((pairs, 2, queries), F32),
                pl.BlockSpec((1, 2, queries), lambda p, _: (p, 0, 0)),
            ),
        ],
        prefetch=(limit,),
        deps=deps,
        cost=costs(16 * queries * keys * 1024, 8 * queries * 1024, 16 * queries * keys),
        name="attn_fwd",
    )


def attn_bwd(q, kv, k_at, v_at, o, do, lse, limit, causal, deps=()):
    q_arr, q_at = q
    queries, keys = q_arr.shape[0], kv.shape[0]
    pairs = HEADS // 2
    q_block = pl.BlockSpec((queries, PAIR), lambda p, _: (0, p))

    def stacked(count, rows):
        return (
            shaped((count, rows, pairs * PAIR), BF),
            pl.BlockSpec((count, rows, PAIR), lambda p, _: (0, 0, p)),
        )

    return run(
        functools.partial(attn_bwd_kernel, make_spans(queries, keys, causal), causal),
        (pairs,),
        [
            (q_arr, pl.BlockSpec((queries, PAIR), lambda p, _: (0, q_at + p))),
            (kv, pl.BlockSpec((keys, PAIR), lambda p, _: (0, k_at + p))),
            (kv, pl.BlockSpec((keys, PAIR), lambda p, _: (0, v_at + p))),
            (o, q_block),
            (do, q_block),
            (lse, pl.BlockSpec((1, 2, queries), lambda p, _: (p, 0, 0))),
        ],
        [stacked(3, queries)] if queries == keys else [stacked(1, queries), stacked(2, keys)],
        prefetch=(limit,),
        deps=deps,
        cost=costs(16 * queries * keys * 2560, 16 * queries * 1024, 16 * queries * keys),
        name="attn_bwd",
    )


def norm_parts(v):
    center = v - jnp.mean(v, -1, keepdims=True)
    inverse = lax.rsqrt(jnp.mean(center * center, -1, keepdims=True) + 1e-05)
    return center * inverse, inverse


def norm_back(grad, unit, inverse, gain):
    gain_grad = jnp.sum(grad * unit, axis=0)
    bias_grad = jnp.sum(grad, axis=0)
    scaled = grad * gain
    mean_a = jnp.mean(scaled, -1, keepdims=True)
    mean_b = jnp.mean(scaled * unit, -1, keepdims=True)
    return inverse * (scaled - mean_a - unit * mean_b), gain_grad, bias_grad


def gather_rows(w):
    return lax.all_gather(w, ALL, axis=0, tiled=True)


def scatter_rows(g):
    part = lax.psum_scatter(g, "gy", scatter_dimension=0, tiled=True)
    return lax.psum_scatter(part, "gx", scatter_dimension=0, tiled=True)


def shards_any(
    hidden,
    memory,
    lengths,
    page_class,
    cotangent,
    w_self_qkv,
    w_self_out,
    w_cross_q,
    w_cross_kv,
    w_cross_out,
    w_fc1,
    w_fc2,
    norm_gains,
    norm_biases,
    *,
    nx,
    ny,
):
    n = nx * ny
    tokens, d = hidden.shape
    rows = w_fc1.shape[0]
    ff = w_fc1.shape[1]
    cuts = w_fc2.shape[0] // rows
    mem_rows = -(-memory.shape[0] // 16) * 16
    slots_used = jnp.where(page_class == 0, MEM_BIG, MEM_BIG // 4).astype(jnp.int32)

    norm_cols = jnp.concatenate([norm_gains, norm_biases], axis=0).T
    norm_cols = jnp.pad(norm_cols, ((0, 0), (0, 128 - norm_cols.shape[1])))
    first = jnp.concatenate([w_self_qkv, w_cross_kv, norm_cols], axis=1)
    second = jnp.concatenate([w_self_out, w_cross_q, w_cross_out], axis=1)
    up_local = (
        w_fc1.reshape(rows, nx, ny, cuts, rows).transpose(0, 3, 2, 1, 4).reshape(rows, ff)
    )
    down_local = jnp.concatenate(
        [w_fc2[c * rows : (c + 1) * rows] for c in range(cuts)], axis=1
    )
    w_first = gather_rows(first)
    w_second = gather_rows(second)
    wup = gather_rows(up_local)
    wdown = lax.all_gather(down_local, ("gy", "gx"), axis=0, tiled=True)

    wqkv = w_first[:, : 3 * d]
    wckv = w_first[:, 3 * d : 5 * d]
    norms = w_first[:, 5 * d : 5 * d + 6].T.astype(F32)
    gains, biases = norms[:3], norms[3:]
    wso, wcq, wco = w_second[:, :d], w_second[:, d : 2 * d], w_second[:, 2 * d :]

    place = jnp.arange(d)
    source = place % rows + ((place // rows) % nx * ny + place // (rows * nx)) * rows
    select = (source[:, None] == place[None, :]).astype(BF)

    def turned(a):
        return dot_nt(select, a).astype(BF)

    unit1, inv1 = norm_parts(hidden)
    h1 = (unit1 * gains[0] + biases[0]).astype(BF)
    qkv = dot(h1, wqkv).astype(BF)
    blocks = d // PAIR
    o, lse = attn_fwd((qkv, 0), qkv, blocks, 2 * blocks, lengths, True)
    x1 = hidden + dot(o, wso)
    unit2, inv2 = norm_parts(x1)
    h2 = (unit2 * gains[1] + biases[1]).astype(BF)
    qc = dot(h2, wcq).astype(BF)
    memory_pad = jnp.pad(memory, ((0, mem_rows - memory.shape[0]), (0, 0)))
    kvc = dot(memory_pad, wckv).astype(BF)
    o2, lse2 = attn_fwd((qc, 0), kvc, 0, blocks, slots_used, False)
    x2 = x1 + dot(o2, wco)
    unit3, inv3 = norm_parts(x2)
    h3 = (unit3 * gains[2] + biases[2]).astype(BF)
    u = dot(h3, wup)
    cdf = 0.5 * (1.0 + lax.erf(u * (0.5**0.5)))
    g = (u * cdf).astype(BF)
    slope = (cdf + u * (jnp.exp(-0.5 * u * u) * 0.3989422804014327)).astype(BF)
    result = x2
    for c in range(cuts):
        result = result + dot(g[:, c * d : (c + 1) * d], wdown[:, c * d : (c + 1) * d])

    valid = (jnp.arange(tokens) < lengths[0])[:, None].astype(F32)
    dout = cotangent * valid
    dy3 = dout.astype(BF)
    grad_down = jnp.concatenate(
        [dot_tn(g[:, c * d : (c + 1) * d], dy3).astype(BF) for c in range(cuts)], axis=1
    )
    own_down = scatter_rows(grad_down)
    dg = jnp.concatenate(
        [dot_nt(dy3, wdown[:, c * d : (c + 1) * d]) for c in range(cuts)], axis=1
    )
    du = (dg * slope.astype(F32)).astype(BF)
    grad_up = dot(turned(h3), du).astype(BF)
    own_up = scatter_rows(grad_up)
    dh3 = dot_nt(du, wup)
    back3, gain3, bias3 = norm_back(dh3, unit3, inv3, gains[2])
    dx2 = dout + back3
    dy2 = dx2.astype(BF)
    do2 = dot_nt(dy2, wco).astype(BF)
    dqc, dkv = attn_bwd((qc, 0), kvc, 0, blocks, o2, do2, lse2, slots_used, False)
    dqc = dqc[0]
    dkvc = jnp.concatenate([dkv[0], dkv[1]], axis=1)
    mem_turned = turned(memory_pad)
    grad_mid = jnp.concatenate(
        [
            dot(turned(o2), dy2).astype(BF),
            dot(turned(h2), dqc).astype(BF),
            dot(mem_turned, dkvc).astype(BF),
        ],
        axis=1,
    )
    own_mid = scatter_rows(grad_mid)
    grad_memory = dot_nt(dkvc, wckv)[: memory.shape[0]]
    dh2 = dot_nt(dqc, wcq)
    back2, gain2, bias2 = norm_back(dh2, unit2, inv2, gains[1])
    dx1 = dx2 + back2
    dy1 = dx1.astype(BF)
    do = dot_nt(dy1, wso).astype(BF)
    dqkv = attn_bwd((qkv, 0), qkv, blocks, 2 * blocks, o, do, lse, lengths, True)
    dqkv = jnp.concatenate([dqkv[0], dqkv[1], dqkv[2]], axis=1)
    dh1 = dot_nt(dqkv, wqkv)
    back1, gain1, bias1 = norm_back(dh1, unit1, inv1, gains[0])
    grad_hidden = dx1 + back1
    norm_grads = jnp.stack([gain1, gain2, gain3, bias1, bias2, bias3])
    norm_grads = jnp.pad(norm_grads, ((0, 122), (0, 0))).astype(BF)
    grad_last = jnp.concatenate(
        [
            dot(turned(o), dy1).astype(BF),
            dot(turned(h1), dqkv).astype(BF),
            turned(norm_grads),
        ],
        axis=1,
    )
    own_last = scatter_rows(grad_last)

    own_up = (
        own_up.reshape(rows, cuts, ny, nx, rows).transpose(0, 3, 2, 1, 4).reshape(rows, ff)
    )
    own_down = jnp.concatenate(
        [own_down[:, c * d : (c + 1) * d] for c in range(cuts)], axis=0
    )
    own_norms = own_last[:, 4 * d : 4 * d + 6].T.astype(F32)
    return (
        result,
        grad_hidden,
        grad_memory,
        own_last[:, d : 4 * d].astype(F32),
        own_last[:, :d].astype(F32),
        own_mid[:, d : 2 * d].astype(F32),
        own_mid[:, 2 * d :].astype(F32),
        own_mid[:, :d].astype(F32),
        own_up.astype(F32),
        own_down.astype(F32),
        own_norms[:3],
        own_norms[3:],
    )


CORE, XBIT, YBIT = 1, 2, 4


def swap(a, bit):
    return lax.ppermute(a, ALL, [(i, i ^ bit) for i in range(32)])


def fence(*values):
    return lax.optimization_barrier(values)


def gather_line(w):
    return lax.all_gather(w, "gx", axis=0)


def gather_near(here):
    return here, swap(here, XBIT), swap(here, YBIT)


def gather_far(near):
    return swap(near[2][:2], XBIT), swap(near[1][2:], YBIT)


def swap_cores(pieces):
    return tuple(swap(p, CORE) for p in pieces)


def put_pieces(bits_ref, pieces, out):
    x, y, core = bits_ref[0], bits_ref[1], bits_ref[2]
    for k in range(10):
        at_core = core if k < 5 else 1 - core
        at_x = x if k % 5 in (0, 2) else 1 - x
        at_y = y if k % 5 in (0, 1) else 1 - y
        z0, z1 = {3: (0, 2), 4: (2, 4)}.get(k % 5, (0, 4))
        out[z0:z1, at_y * 4 + at_x * 2 + at_core] = pieces[k][...]


def place_kernel(bits_ref, *refs):
    put_pieces(bits_ref, refs[:10], refs[-1])


def place_dot_kernel(bits_ref, *refs):
    a, w, y = refs[10], refs[11], refs[12]
    put_pieces(bits_ref, refs[:10], w)
    whole = w[...].reshape(a.shape[1], w.shape[3])
    y[...] = dot(a[...], whole).astype(y.dtype)


def piece_specs(pieces, start, block):
    rows = pieces[0].shape[1]
    return [
        (p, pl.BlockSpec((p.shape[0], rows, block), lambda j, _: (0, 0, start // block + j)))
        for p in pieces
    ]


def place_out(rows, width, block):
    return (
        shaped((4, 8, rows, width), BF),
        pl.BlockSpec((4, 8, rows, block), lambda j, _: (0, 0, 0, j)),
    )


def place(pieces, start, width, bits, deps=()):
    rows = pieces[0].shape[1]
    block = min(width, 512)
    out = run(
        place_kernel,
        (width // block,),
        piece_specs(pieces, start, block),
        [place_out(rows, width, block)],
        prefetch=(bits,),
        deps=deps,
        cost=costs(0, 4 * 32 * rows * width),
        name="place",
    )
    return out.reshape(32 * rows, width)


def place_dot(pieces, start, width, bits, a, dtype, deps=()):
    rows, block = pieces[0].shape[1], 512
    whole = pl.BlockSpec(a.shape, lambda j, _: (0, 0))
    w, y = run(
        place_dot_kernel,
        (width // block,),
        piece_specs(pieces, start, block) + [(a, whole)],
        [
            place_out(rows, width, block),
            (
                shaped((a.shape[0], width), dtype),
                pl.BlockSpec((a.shape[0], block), lambda j, _: (0, j)),
            ),
        ],
        prefetch=(bits,),
        deps=deps,
        cost=costs(2 * a.shape[0] * 32 * rows * width, 4 * 32 * rows * width),
        name="place_dot",
    )
    return w.reshape(32 * rows, width), y


def store_rows(value, outs):
    near = outs[0].shape[0]
    half = outs[1].shape[0]
    columns = value.shape[1]
    outs[0][:, :columns] = value[:near]
    outs[1][:, :columns] = value[near : near + half]
    outs[2][:, :columns] = value[near + half :]


def row_outs(rows, columns, block):
    return [
        (shaped((r, columns), BF), pl.BlockSpec((r, block), lambda j, *_: (0, j)))
        for r in (rows * 3 // 4, rows // 8, rows // 8)
    ]


def wgrad_kernel(starts, extra, *refs):
    outs = refs[-3:]
    j = pl.program_id(0)
    for s in range(len(starts) - 1):
        a, a2, g, g2 = refs[4 * s : 4 * s + 4]

        @pl.when((j >= starts[s]) & (j < starts[s + 1]))
        def _(a=a, a2=a2, g=g, g2=g2):
            store_rows((dot(a[...], g[...]) + dot(a2[...], g2[...])).astype(BF), outs)

    if extra:

        @pl.when(j == starts[-1])
        def _():
            mine, theirs = refs[-5], refs[-4]
            store_rows((mine[...].astype(F32) + theirs[...].astype(F32)).astype(BF), outs)


def wgrad(segments, extra=(), deps=(), block=1024):
    starts, ins = [0], []
    for a, a2, g, g2 in segments:
        per = g.shape[2] // block
        count, start = g.shape[0] * per, starts[-1]

        def at(j, start=start, count=count, per=per):
            k = jnp.clip(j - start, 0, count - 1)
            return (k // per, 0, k % per)

        whole = pl.BlockSpec(a.shape, lambda j: (0, 0))
        grads = pl.BlockSpec((None, g.shape[1], block), at)
        ins += [(a, whole), (a2, whole), (g, grads), (g2, grads)]
        starts.append(start + count)
    rows = segments[0][0].shape[0]
    columns = starts[-1] * block
    steps = starts[-1]
    if extra:
        ins += [(e, pl.BlockSpec(e.shape, lambda j: (0, 0))) for e in extra]
        columns += extra[0].shape[1]
        steps += 1
    return run(
        functools.partial(wgrad_kernel, tuple(starts), bool(extra)),
        (steps,),
        ins,
        row_outs(rows, columns, block),
        deps=deps,
        cost=costs(2 * rows * 1024 * columns, 4 * 512 * columns + 2 * rows * columns),
        name="wgrad",
        vmem=30 if len(segments) > 1 else 16,
    )


def wgrad_down_kernel(bits_ref, *refs):
    blocks, other, dy, dy2 = refs[:4], refs[4:8], refs[8], refs[9]
    mine = jnp.concatenate([r[...].T for r in blocks], axis=0)
    theirs = jnp.concatenate([r[...].T for r in other], axis=0)
    store_rows((dot(mine, dy[...]) + dot(theirs, dy2[...])).astype(BF), refs[10:])


def wgrad_down(bits, g, g_other, dy, dy_other, cuts):
    tokens, d = dy.shape

    def spec(rel, whole):
        def at(b, bits_ref):
            x = bits_ref[0] ^ (rel & 1)
            y = bits_ref[1] ^ (rel >> 1)
            block = b * 4 + y * 2 + x
            return (0, block * 2 + bits_ref[2] if whole else block)

        return pl.BlockSpec((tokens, 128), at)

    rows = pl.BlockSpec((tokens, d), lambda b, _: (0, 0))
    return run(
        wgrad_down_kernel,
        (cuts,),
        [(g, spec(r, True)) for r in range(4)]
        + [(g_other, spec(r, False)) for r in range(4)]
        + [(dy, rows), (dy_other, rows)],
        row_outs(512, cuts * d, d),
        prefetch=(bits,),
        cost=costs(2 * 512 * 1024 * cuts * d, 16 * tokens * d),
        name="wgrad_down",
    )


def up_kernel(bits_ref, *refs):
    h_ref, w_ref, g_ref, slope_ref, send_ref = refs[10:]
    put_pieces(bits_ref, refs[:10], w_ref)
    u = dot(h_ref[...], w_ref[...].reshape(h_ref.shape[1], w_ref.shape[3]))
    cdf = 0.5 * (1.0 + lax.erf(u * (0.5**0.5)))
    g = (u * cdf).astype(BF)
    g_ref[...] = g
    slope_ref[...] = (cdf + u * (jnp.exp(-0.5 * u * u) * 0.3989422804014327)).astype(BF)
    core = bits_ref[2]
    for k in range(0, g.shape[1], 256):
        send_ref[:, k // 2 : k // 2 + 128] = jnp.where(
            core == 0, g[:, k + 128 : k + 256], g[:, k : k + 128]
        )


def feed_up(bits, h, pieces, ff, deps=(), block=512):
    tokens, d = h.shape
    rows = pieces[0].shape[1]
    out = (shaped((tokens, ff), BF), pl.BlockSpec((tokens, block), lambda j, _: (0, j)))
    w, *rest = run(
        up_kernel,
        (ff // block,),
        piece_specs(pieces, 0, block) + [(h, pl.BlockSpec((tokens, d), lambda j, _: (0, 0)))],
        [
            place_out(rows, ff, block),
            out,
            out,
            (
                shaped((tokens, ff // 2), BF),
                pl.BlockSpec((tokens, block // 2), lambda j, _: (0, j)),
            ),
        ],
        prefetch=(bits,),
        deps=deps,
        cost=costs(2 * tokens * d * ff, 4 * d * ff + 4 * tokens * ff, 2 * tokens * ff),
        name="feed_up",
    )
    return w.reshape(d, ff), *rest


def down_kernel(g_ref, w_ref, x_ref, out_ref):
    @pl.when(pl.program_id(0) == 0)
    def _():
        out_ref[...] = x_ref[...]

    out_ref[...] += dot(g_ref[...], w_ref[...])


def feed_down(g, w, x, cuts, deps=()):
    tokens, d = x.shape
    block = d // 2
    whole = pl.BlockSpec((tokens, d), lambda j: (0, 0))
    return run(
        down_kernel,
        (2 * cuts,),
        [
            (g, pl.BlockSpec((tokens, block), lambda j: (0, j))),
            (w, pl.BlockSpec((block, d), lambda j: (j % 2, j // 2))),
            (x, whole),
        ],
        [(shaped((tokens, d), F32), whole)],
        deps=deps,
        cost=costs(2 * tokens * d * d * cuts, 2 * d * d * cuts + 10 * tokens * d),
        name="feed_down",
    )


def norm_back_store(acc, x_ref, gain_ref, res_ref, dx_ref, low_ref, sums_ref):
    gain_grad, bias_grad = 0.0, 0.0
    step = 128
    for r in range(0, x_ref.shape[0], step):
        part = slice(r, r + step)
        x, dh = x_ref[part, :], acc[part, :]
        center = x - jnp.mean(x, -1, keepdims=True)
        inverse = lax.rsqrt(jnp.mean(center * center, -1, keepdims=True) + 1e-05)
        unit = center * inverse
        gain_grad += jnp.sum(dh * unit, axis=0, keepdims=True)
        bias_grad += jnp.sum(dh, axis=0, keepdims=True)
        scaled = dh * gain_ref[...]
        mean_a = jnp.mean(scaled, -1, keepdims=True)
        mean_b = jnp.mean(scaled * unit, -1, keepdims=True)
        dx = res_ref[part, :] + inverse * (scaled - mean_a - unit * mean_b)
        dx_ref[part, :] = dx
        if low_ref is not None:
            low_ref[part, :] = dx.astype(BF)
    sums_ref[0:1, :] = gain_grad
    sums_ref[1:2, :] = bias_grad


def accumulate(acc, part):
    j = pl.program_id(0)

    @pl.when(j == 0)
    def _():
        acc[...] = part

    @pl.when(j > 0)
    def _():
        acc[...] += part


def feed_back_kernel(
    dy_ref, w2_ref, slope_ref, w1_ref, x_ref, gain_ref, res_ref, du_ref, dx_ref, low_ref, sums_ref, acc
):
    du = (dot_nt(dy_ref[...], w2_ref[...]) * slope_ref[...].astype(F32)).astype(BF)
    du_ref[...] = du
    accumulate(acc, dot_nt(du, w1_ref[...]))

    @pl.when(pl.program_id(0) == pl.num_programs(0) - 1)
    def _():
        norm_back_store(acc, x_ref, gain_ref, res_ref, dx_ref, low_ref, sums_ref)


def feed_back(dy, w2, slope, w1, x, gain, res, cuts, deps=()):
    tokens, d = x.shape
    block = d // 2
    ff = w1.shape[1]
    whole = pl.BlockSpec((tokens, d), lambda j: (0, 0), pipeline_mode=pl.Buffered(1))
    part = pl.BlockSpec((tokens, block), lambda j: (0, j))
    return run(
        feed_back_kernel,
        (2 * cuts,),
        [
            (dy, whole),
            (w2, pl.BlockSpec((block, d), lambda j: (j % 2, j // 2))),
            (slope, part),
            (w1, pl.BlockSpec((d, block), lambda j: (0, j))),
            (x, whole),
            (gain, pl.BlockSpec((1, d), lambda j: (0, 0))),
            (res, whole),
        ],
        [
            (shaped((tokens, ff), BF), part),
            (shaped((tokens, d), F32), whole),
            (shaped((tokens, d), BF), whole),
            (shaped((2, d), F32), pl.BlockSpec((2, d), lambda j: (0, 0))),
        ],
        scratch=[pltpu.VMEM((tokens, d), F32)],
        deps=deps,
        cost=costs(4 * tokens * d * ff, 4 * d * ff + 4 * tokens * ff + 16 * tokens * d),
        name="feed_back",
        vmem=30,
    )


def norm_back_kernel(g_ref, w_ref, x_ref, gain_ref, res_ref, *refs):
    dx_ref, sums_ref, acc = refs[0], refs[-2], refs[-1]
    low_ref = refs[1] if len(refs) == 4 else None
    accumulate(acc, dot_nt(g_ref[...], w_ref[...]))

    @pl.when(pl.program_id(0) == pl.num_programs(0) - 1)
    def _():
        norm_back_store(acc, x_ref, gain_ref, res_ref, dx_ref, low_ref, sums_ref)


def through_norm(g, w, x, gain, res, low=True, deps=()):
    tokens, d = x.shape
    block = 512
    per = g.shape[2] // block
    count = g.shape[0] * per
    whole = pl.BlockSpec((tokens, d), lambda j: (0, 0), pipeline_mode=pl.Buffered(1))
    outs = [(shaped((tokens, d), F32), whole)]
    if low:
        outs.append((shaped((tokens, d), BF), whole))
    outs.append((shaped((2, d), F32), pl.BlockSpec((2, d), lambda j: (0, 0))))
    return run(
        norm_back_kernel,
        (count,),
        [
            (g, pl.BlockSpec((None, tokens, block), lambda j: (j // per, 0, j % per))),
            (w, pl.BlockSpec((d, block), lambda j: (0, j))),
            (x, whole),
            (gain, pl.BlockSpec((1, d), lambda j: (0, 0))),
            (res, whole),
        ],
        outs,
        scratch=[pltpu.VMEM((tokens, d), F32)],
        deps=deps,
        cost=costs(2 * tokens * d * block * count, 2 * d * block * count + 16 * tokens * d),
        name="through_norm",
    )


def scatter_far(grads):
    return swap(grads[1], XBIT), swap(grads[2], YBIT)


def scatter_near(near, far, rows):
    parts = near.reshape(3, 4, rows, near.shape[1])
    from_x, from_y = (f.reshape(2, rows, -1) for f in far)
    to_x = jnp.concatenate([parts[1, :2], parts[1, 2:] + from_y], axis=0)
    to_y = jnp.concatenate([parts[2, :2] + from_x, parts[2, 2:]], axis=0)
    return swap(to_x, XBIT), swap(to_y, YBIT)


def scatter_line(near, got, rows):
    here = near[: 4 * rows].reshape(4, rows, -1)
    total = here.astype(F32) + got[0].astype(F32) + got[1].astype(F32)
    flat = total.astype(BF).reshape(4 * rows, -1)
    return lax.psum_scatter(flat, "gx", scatter_dimension=0, tiled=True)


def shards_plane(
    hidden,
    memory,
    lengths,
    page_class,
    cotangent,
    w_self_qkv,
    w_self_out,
    w_cross_q,
    w_cross_kv,
    w_cross_out,
    w_fc1,
    w_fc2,
    norm_gains,
    norm_biases,
):
    tokens, d = hidden.shape
    rows, ff = w_fc1.shape
    cuts = w_fc2.shape[0] // rows
    mem_rows = -(-memory.shape[0] // 16) * 16
    slots_used = jnp.where(page_class == 0, MEM_BIG, MEM_BIG // 4).astype(jnp.int32)
    along = lax.axis_index("gy")
    x_at, y_at, core = (along // 2) % 2, along // 4, along % 2
    bits = jnp.stack([x_at, y_at, core, lax.axis_index("gx")]).astype(jnp.int32)

    norm_cols = jnp.concatenate([norm_gains, norm_biases], axis=0).T
    norm_cols = jnp.pad(norm_cols, ((0, 0), (0, 128 - norm_cols.shape[1])))
    up_local = (
        w_fc1.reshape(rows, 4, 2, 2, 2, cuts, rows)
        .transpose(0, 5, 2, 3, 4, 1, 6)
        .reshape(rows, ff)
    )
    down_local = jnp.concatenate(
        [w_fc2[c * rows : (c + 1) * rows] for c in range(cuts)], axis=1
    )
    place_at = jnp.arange(d)
    r = place_at % rows
    z = (place_at // rows) % 4
    rel = (place_at // (4 * rows)) % 4
    source_core = core ^ (place_at // (16 * rows))
    device = z * 8 + (y_at ^ (rel // 2)) * 4 + (x_at ^ (rel % 2)) * 2 + source_core
    select = ((device * rows + r)[:, None] == place_at[None, :]).astype(BF)
    half = d // 2

    def turned(a):
        t = dot_nt(select, a).astype(BF)
        return t[:half], swap(t[half:], CORE)

    pack1 = jnp.concatenate([w_self_qkv, norm_cols], axis=1)
    pack2 = jnp.concatenate([w_cross_kv, w_self_out, w_cross_q, w_cross_out], axis=1)
    blocks = d // PAIR
    memory_pad = jnp.pad(memory, ((0, mem_rows - memory.shape[0]), (0, 0)))

    line1, pack2, memory_pad, hidden = fence(gather_line(pack1), pack2, memory_pad, hidden)

    line2 = gather_line(pack2)
    near1 = gather_near(line1)
    mem_t = turned(memory_pad)
    unit1, _ = norm_parts(hidden)
    near1, mem_t, unit1 = fence(near1, mem_t, unit1)

    near1, far1, cores1, line2, pack3 = fence(
        near1, gather_far(near1), swap_cores(near1), line2, up_local
    )

    line3 = gather_line(pack3)
    near2 = gather_near(line2)
    first = near1 + far1 + cores1 + swap_cores(far1)
    norms = place(first, 3 * d, 128, bits)[:, :6].T.astype(F32)
    gains, biases = norms[:3], norms[3:]
    h1 = (unit1 * gains[0] + biases[0]).astype(BF)
    wqkv, qkv = place_dot(first, 0, 3 * d, bits, h1, BF)
    o, lse = attn_fwd((qkv, 0), qkv, blocks, 2 * blocks, lengths, True)
    near2, o, h1, gains, biases = fence(near2, o, h1, gains, biases)

    near2, far2, cores2, h1, o, line3, pack4 = fence(
        near2, gather_far(near2), swap_cores(near2), h1, o, line3, down_local
    )

    wdown = lax.all_gather(pack4, ("gy", "gx"), axis=0, tiled=True)
    near3 = gather_near(line3)
    second = near2 + far2 + cores2 + swap_cores(far2)
    wso, y1 = place_dot(second, 2 * d, d, bits, o, F32)
    x1 = hidden + y1
    unit2, _ = norm_parts(x1)
    h2 = (unit2 * gains[1] + biases[1]).astype(BF)
    wcq, qc = place_dot(second, 3 * d, d, bits, h2, BF)
    wckv, kvc = place_dot(second, 0, 2 * d, bits, memory_pad, BF)
    h1_t, o_t = turned(h1), turned(o)
    near3, second, qc, kvc, h2, x1, h1_t, o_t = fence(
        near3, second, qc, kvc, h2, x1, h1_t, o_t
    )

    far3, cores3 = gather_far(near3), swap_cores(near3)
    o2, lse2 = attn_fwd((qc, 0), kvc, 0, blocks, slots_used, False)
    near3, far3, cores3, o2, h2, cotangent = fence(near3, far3, cores3, o2, h2, cotangent)

    third = near3 + far3 + cores3 + swap_cores(far3)
    wco, y2 = place_dot(second, 4 * d, d, bits, o2, F32)
    x2 = x1 + y2
    unit3, _ = norm_parts(x2)
    h3 = (unit3 * gains[2] + biases[2]).astype(BF)
    valid = (jnp.arange(tokens) < lengths[0])[:, None].astype(F32)
    dout = cotangent * valid
    dy3 = dout.astype(BF)
    dy3_other = swap(dy3, CORE)
    third, h3, x2, o2, dout, dy3, dy3_other = fence(third, h3, x2, o2, dout, dy3, dy3_other)

    wup, g, slope, g_send = feed_up(bits, h3, third, ff)
    wup, g, slope, g_send, h3, o2 = fence(wup, g, slope, g_send, h3, o2)

    h2_t, h3_t, o2_t = turned(h2), turned(h3), turned(o2)
    g_other, h2_t, h3_t, o2_t, g = fence(swap(g_send, CORE), h2_t, h3_t, o2_t, g)

    grad_down = wgrad_down(bits, g, g_other, dy3, dy3_other, cuts)
    grad_down, dy3, slope, wdown = fence(grad_down, dy3, slope, wdown)

    du, dx2, dy2, sums3 = feed_back(dy3, wdown, slope, wup, x2, gains[2:3], dout, cuts)
    far1, du, dx2, dy2, g = fence(scatter_far(grad_down), du, dx2, dy2, g)

    got1 = scatter_near(grad_down[0], far1, rows)
    result = feed_down(g, wdown, x2, cuts)
    do2 = dot_nt(dy2, wco).astype(BF)
    du_other, result, do2, du = fence(swap(du, CORE), result, do2, du)

    grad_up = wgrad([h3_t + (du[None], du_other[None])])
    grad_up, do2, dy2 = fence(grad_up, do2, dy2)

    dqc, dkvc = attn_bwd((qc, 0), kvc, 0, blocks, o2, do2, lse2, slots_used, False)
    far2, got1, dqc, dkvc, dy2_other, dx2 = fence(
        scatter_far(grad_up), got1, dqc, dkvc, swap(dy2, CORE), dx2
    )

    own_down = scatter_line(grad_down[0], got1, rows)
    got2 = scatter_near(grad_up[0], far2, rows)
    dx1, dy1, sums2 = through_norm(dqc, wcq, x1, gains[1:2], dx2)
    do = dot_nt(dy1, wso).astype(BF)
    dqc_other, dkvc_other, dx1, dy1, do, dqc, dkvc = fence(
        swap(dqc, CORE), swap(dkvc, CORE), dx1, dy1, do, dqc, dkvc
    )

    grad_mid = wgrad(
        [
            o2_t + (dy2[None], dy2_other[None]),
            h2_t + (dqc, dqc_other),
            mem_t + (dkvc, dkvc_other),
        ]
    )
    grad_mid, do, dy1 = fence(grad_mid, do, dy1)

    dqkv = attn_bwd((qkv, 0), qkv, blocks, 2 * blocks, o, do, lse, lengths, True)
    far3, dy1_other, dqkv, got2, dx1 = fence(
        scatter_far(grad_mid), swap(dy1, CORE), dqkv, got2, dx1
    )

    own_up = scatter_line(grad_up[0], got2, rows)
    got3 = scatter_near(grad_mid[0], far3, rows)
    grad_hidden, sums1 = through_norm(dqkv, wqkv, hidden, gains[0:1], dx1, low=False)
    sums = jnp.concatenate([sums1, sums2, sums3], axis=0)
    sums = jnp.pad(sums, ((0, 122), (0, 0))).astype(BF)
    dqkv_other, grad_hidden, sums_t = fence(swap(dqkv, CORE), grad_hidden, turned(sums))

    grad_last = wgrad(
        [o_t + (dy1[None], dy1_other[None]), h1_t + (dqkv, dqkv_other)], extra=sums_t
    )
    grad_last, got3, dkvc, own_down = fence(grad_last, got3, dkvc, own_down)

    own_mid = scatter_line(grad_mid[0], got3, rows)
    grad_memory = (dot_nt(dkvc[0], wckv[:, :d]) + dot_nt(dkvc[1], wckv[:, d:]))[
        : memory.shape[0]
    ]
    far4, grad_memory, own_up = fence(scatter_far(grad_last), grad_memory, own_up)

    got4 = scatter_near(grad_last[0], far4, rows)
    own_last = scatter_line(grad_last[0], got4, rows)

    own_up = (
        own_up.reshape(rows, cuts, 2, 2, 2, 4, rows)
        .transpose(0, 5, 2, 3, 4, 1, 6)
        .reshape(rows, ff)
    )
    own_down = jnp.concatenate(
        [own_down[:, c * d : (c + 1) * d] for c in range(cuts)], axis=0
    )
    own_sums = own_last[:, 4 * d : 4 * d + 6].T.astype(F32)
    return (
        result,
        grad_hidden,
        grad_memory,
        own_last[:, d : 4 * d].astype(F32),
        own_last[:, :d].astype(F32),
        own_mid[:, d : 2 * d].astype(F32),
        own_mid[:, 2 * d :].astype(F32),
        own_mid[:, :d].astype(F32),
        own_up.astype(F32),
        own_down.astype(F32),
        own_sums[0::2],
        own_sums[1::2],
    )


def solution(mesh):
    row = P(ALL, None)
    col = P(None, ALL)
    nx, ny = mesh.shape["gx"], mesh.shape["gy"]
    body = shards_plane if (nx, ny) == (4, 8) else functools.partial(shards_any, nx=nx, ny=ny)
    return jax.shard_map(
        body,
        mesh=mesh,
        in_specs=(row, row, P(ALL), P(ALL), row) + (row,) * 7 + (col, col),
        out_specs=(row,) * 10 + (col, col),
        check_vma=False,
    )
```

```python
import functools

import jax
import jax.numpy as jnp
from jax import lax
from jax.experimental import pallas as pl
from jax.experimental.pallas import tpu as pltpu
from jax.sharding import PartitionSpec as P

HEADS = 16
MEM_BIG = 588
ALL = ("gx", "gy")
BF = jnp.bfloat16
F32 = jnp.float32
PAIR = 128
LIMITS = {'feed_back': 50, 'pass_on': 8, 'plane_sum': 8, 'place': 8, 'hidden_order': 8, 'memory_grad': 12, 'turn': 12, 'wgrad': 44, 'wgrad_down': 44}
FAR_OUTS = {'wgrad': (0, 1, 2), 'wgrad_down': (0, 1, 2), 'feed_up': (0, 1, 2), 'place_dot': (0,), 'feed_back': (0, 1)}
FAR_INS = {'pass_on': (0, 1, 2, 3), 'plane_sum': (0, 1, 2)}


def dot(a, b):
    return jnp.dot(a, b, preferred_element_type=F32)


def dot_nt(a, b):
    return lax.dot_general(a, b, (((1,), (1,)), ((), ())), preferred_element_type=F32)


def dot_tn(a, b):
    return lax.dot_general(a, b, (((0,), (0,)), ((), ())), preferred_element_type=F32)


def run(
    kernel, grid, ins, outs, prefetch=(), scratch=(), deps=(), cost=None, name=None
):
    count = len(prefetch) + len(ins)

    def body(*refs):
        return kernel(*refs[:count], *refs[count + len(deps) :])

    result = pl.pallas_call(
        body,
        grid_spec=pltpu.PrefetchScalarGridSpec(
            num_scalar_prefetch=len(prefetch),
            grid=grid,
            in_specs=[spec for _, spec in ins] + [pl.BlockSpec(memory_space=pl.ANY)] * len(deps),
            out_specs=[spec for _, spec in outs],
            scratch_shapes=scratch,
        ),
        out_shape=[
            pltpu.HBM(shape.shape, shape.dtype) if k in FAR_OUTS.get(name, ()) else shape
            for k, (shape, _) in enumerate(outs)
        ],
        compiler_params=pltpu.CompilerParams(
            dimension_semantics=("arbitrary",) * len(grid), vmem_limit_bytes=LIMITS.get(name, 30) * 1024 * 1024
        ),
        cost_estimate=cost,
        name=name,
    )(
        *prefetch,
        *[
            pltpu.with_memory_space_constraint(a, pltpu.HBM)
            if k in FAR_INS.get(name, ())
            else a
            for k, (a, _) in enumerate(ins)
        ],
        *deps,
    )
    return result if len(outs) > 1 else result[0]


def costs(flops, nbytes, transcendentals=0):
    return pl.CostEstimate(
        flops=flops, bytes_accessed=nbytes, transcendentals=transcendentals
    )


def shaped(shape, dtype):
    return jax.ShapeDtypeStruct(shape, dtype)


def allowed_t(key_count, q0, q1, limit, causal):
    key_at = lax.broadcasted_iota(jnp.int32, (key_count, q1 - q0), 0)
    ok = key_at < limit
    if causal:
        query_at = lax.broadcasted_iota(jnp.int32, (key_count, q1 - q0), 1) + q0
        ok = ok & (key_at <= query_at)
    return ok


def half_mask(width, half):
    lane = lax.broadcasted_iota(jnp.int32, (1, width), 1)
    return ((lane // (width // 2)) == half).astype(F32).astype(BF)


def attn_fwd_kernel(spans, causal, limit_ref, q_ref, k_ref, v_ref, o_ref, lse_ref):
    width = q_ref.shape[1]
    half = width // 2
    limit = limit_ref[0]
    scale = BF(half**-0.5)
    v_t = v_ref[...].T
    for q0, q1, keys in spans:
        query = q_ref[q0:q1, :] * scale
        ok = allowed_t(keys, q0, q1, limit, causal)
        outs = []
        for h in range(2):
            s = dot_nt(k_ref[:keys, :], query * half_mask(width, h))
            s = jnp.where(ok, s, -1e30)
            top = jnp.max(s, axis=0, keepdims=True)
            e = jnp.exp(s - top)
            total = jnp.sum(e, axis=0, keepdims=True)
            outs.append(dot(v_t[h * half : (h + 1) * half, :keys], e.astype(BF)) / total)
            lse_ref[0, h : h + 1, q0:q1] = top + jnp.log(total)
        o_ref[q0:q1, :] = jnp.concatenate(outs, axis=0).T.astype(BF)


def attn_bwd_kernel(
    spans, causal, limit_ref, q_ref, k_ref, v_ref, o_ref, do_ref, lse_ref, *outs_ref
):
    dq_ref = outs_ref[0].at[0]
    dk_ref, dv_ref = (outs_ref[-1].at[k - 2 + outs_ref[-1].shape[0]] for k in range(2))
    width = q_ref.shape[1]
    half = width // 2
    limit = limit_ref[0]
    scale = BF(half**-0.5)
    k_t = k_ref[...].T * scale
    total_k = k_ref.shape[0]
    dk = jnp.zeros((total_k, width), F32)
    dv = jnp.zeros((total_k, width), F32)
    for q0, q1, keys in spans:
        query = q_ref[q0:q1, :] * scale
        grad_o = do_ref[q0:q1, :]
        ok = allowed_t(keys, q0, q1, limit, causal)
        both = (grad_o.astype(F32) * o_ref[q0:q1, :].astype(F32)).T
        outs = []
        dk_part = jnp.zeros((keys, width), F32)
        dv_part = jnp.zeros((keys, width), F32)
        for h in range(2):
            mask = half_mask(width, h)
            query_h = query * mask
            grad_h = grad_o * mask
            inner = jnp.sum(both[h * half : (h + 1) * half], axis=0, keepdims=True)
            s = dot_nt(k_ref[:keys, :], query_h)
            p = jnp.where(ok, jnp.exp(s - lse_ref[0, h : h + 1, q0:q1]), 0.0)
            dv_part += dot(p.astype(BF), grad_h)
            dp = dot_nt(v_ref[:keys, :], grad_h)
            ds = (p * (dp - inner)).astype(BF)
            dk_part += dot(ds, query_h)
            outs.append(dot(k_t[h * half : (h + 1) * half, :keys], ds))
        dq_ref[q0:q1, :] = jnp.concatenate(outs, axis=0).T.astype(BF)
        if keys < total_k:
            pad = jnp.zeros((total_k - keys, width), F32)
            dk_part = jnp.concatenate([dk_part, pad], axis=0)
            dv_part = jnp.concatenate([dv_part, pad], axis=0)
        dk += dk_part
        dv += dv_part
    dk_ref[...] = dk.astype(BF)
    dv_ref[...] = dv.astype(BF)


def make_spans(queries, keys, causal):
    step = 256
    return tuple(
        (q, q + step, min(q + step, keys) if causal else keys) for q in range(0, queries, step)
    )


def attn_fwd(q, kv, k_at, v_at, limit, causal, deps=()):
    q_arr, q_at = q
    queries, keys = q_arr.shape[0], kv.shape[0]
    pairs = HEADS // 2
    return run(
        functools.partial(attn_fwd_kernel, make_spans(queries, keys, causal), causal),
        (pairs,),
        [
            (q_arr, pl.BlockSpec((queries, PAIR), lambda p, _: (0, q_at + p))),
            (kv, pl.BlockSpec((keys, PAIR), lambda p, _: (0, k_at + p))),
            (kv, pl.BlockSpec((keys, PAIR), lambda p, _: (0, v_at + p))),
        ],
        [
            (
                shaped((queries, pairs * PAIR), BF),
                pl.BlockSpec((queries, PAIR), lambda p, _: (0, p)),
            ),
            (
                shaped((pairs, 2, queries), F32),
                pl.BlockSpec((1, 2, queries), lambda p, _: (p, 0, 0)),
            ),
        ],
        prefetch=(limit,),
        deps=deps,
        cost=costs(16 * queries * keys * 1024, 8 * queries * 1024, 16 * queries * keys),
        name="attn_fwd",
    )


def attn_bwd(q, kv, k_at, v_at, o, do, lse, limit, causal, deps=()):
    q_arr, q_at = q
    queries, keys = q_arr.shape[0], kv.shape[0]
    pairs = HEADS // 2
    q_block = pl.BlockSpec((queries, PAIR), lambda p, _: (0, p))

    def stacked(count, rows):
        return (
            shaped((count, rows, pairs * PAIR), BF),
            pl.BlockSpec((count, rows, PAIR), lambda p, _: (0, 0, p)),
        )

    return run(
        functools.partial(attn_bwd_kernel, make_spans(queries, keys, causal), causal),
        (pairs,),
        [
            (q_arr, pl.BlockSpec((queries, PAIR), lambda p, _: (0, q_at + p))),
            (kv, pl.BlockSpec((keys, PAIR), lambda p, _: (0, k_at + p))),
            (kv, pl.BlockSpec((keys, PAIR), lambda p, _: (0, v_at + p))),
            (o, q_block),
            (do, q_block),
            (lse, pl.BlockSpec((1, 2, queries), lambda p, _: (p, 0, 0))),
        ],
        [stacked(3, queries)] if queries == keys else [stacked(1, queries), stacked(2, keys)],
        prefetch=(limit,),
        deps=deps,
        cost=costs(16 * queries * keys * 2560, 16 * queries * 1024, 16 * queries * keys),
        name="attn_bwd",
    )


def norm_parts(v):
    center = v - jnp.mean(v, -1, keepdims=True)
    inverse = lax.rsqrt(jnp.mean(center * center, -1, keepdims=True) + 1e-05)
    return center * inverse, inverse


def norm_back(grad, unit, inverse, gain):
    gain_grad = jnp.sum(grad * unit, axis=0)
    bias_grad = jnp.sum(grad, axis=0)
    scaled = grad * gain
    mean_a = jnp.mean(scaled, -1, keepdims=True)
    mean_b = jnp.mean(scaled * unit, -1, keepdims=True)
    return inverse * (scaled - mean_a - unit * mean_b), gain_grad, bias_grad


def gather_rows(w):
    return lax.all_gather(w, ALL, axis=0, tiled=True)


def scatter_rows(g):
    part = lax.psum_scatter(g, "gy", scatter_dimension=0, tiled=True)
    return lax.psum_scatter(part, "gx", scatter_dimension=0, tiled=True)


def shards_any(
    hidden,
    memory,
    lengths,
    page_class,
    cotangent,
    w_self_qkv,
    w_self_out,
    w_cross_q,
    w_cross_kv,
    w_cross_out,
    w_fc1,
    w_fc2,
    norm_gains,
    norm_biases,
    *,
    nx,
    ny,
):
    n = nx * ny
    tokens, d = hidden.shape
    rows = w_fc1.shape[0]
    ff = w_fc1.shape[1]
    cuts = w_fc2.shape[0] // rows
    mem_rows = -(-memory.shape[0] // 16) * 16
    slots_used = jnp.where(page_class == 0, MEM_BIG, MEM_BIG // 4).astype(jnp.int32)

    norm_cols = jnp.concatenate([norm_gains, norm_biases], axis=0).T
    norm_cols = jnp.pad(norm_cols, ((0, 0), (0, 128 - norm_cols.shape[1])))
    first = jnp.concatenate([w_self_qkv, w_cross_kv, norm_cols], axis=1)
    second = jnp.concatenate([w_self_out, w_cross_q, w_cross_out], axis=1)
    up_local = (
        w_fc1.reshape(rows, nx, ny, cuts, rows).transpose(0, 3, 2, 1, 4).reshape(rows, ff)
    )
    down_local = jnp.concatenate(
        [w_fc2[c * rows : (c + 1) * rows] for c in range(cuts)], axis=1
    )
    w_first = gather_rows(first)
    w_second = gather_rows(second)
    wup = gather_rows(up_local)
    wdown = lax.all_gather(down_local, ("gy", "gx"), axis=0, tiled=True)

    wqkv = w_first[:, : 3 * d]
    wckv = w_first[:, 3 * d : 5 * d]
    norms = w_first[:, 5 * d : 5 * d + 6].T.astype(F32)
    gains, biases = norms[:3], norms[3:]
    wso, wcq, wco = w_second[:, :d], w_second[:, d : 2 * d], w_second[:, 2 * d :]

    place = jnp.arange(d)
    source = place % rows + ((place // rows) % nx * ny + place // (rows * nx)) * rows
    select = (source[:, None] == place[None, :]).astype(BF)

    def turned(a):
        return dot_nt(select, a).astype(BF)

    unit1, inv1 = norm_parts(hidden)
    h1 = (unit1 * gains[0] + biases[0]).astype(BF)
    qkv = dot(h1, wqkv).astype(BF)
    blocks = d // PAIR
    o, lse = attn_fwd((qkv, 0), qkv, blocks, 2 * blocks, lengths, True)
    x1 = hidden + dot(o, wso)
    unit2, inv2 = norm_parts(x1)
    h2 = (unit2 * gains[1] + biases[1]).astype(BF)
    qc = dot(h2, wcq).astype(BF)
    memory_pad = jnp.pad(memory, ((0, mem_rows - memory.shape[0]), (0, 0)))
    kvc = dot(memory_pad, wckv).astype(BF)
    o2, lse2 = attn_fwd((qc, 0), kvc, 0, blocks, slots_used, False)
    x2 = x1 + dot(o2, wco)
    unit3, inv3 = norm_parts(x2)
    h3 = (unit3 * gains[2] + biases[2]).astype(BF)
    u = dot(h3, wup)
    cdf = 0.5 * (1.0 + lax.erf(u * (0.5**0.5)))
    g = (u * cdf).astype(BF)
    slope = (cdf + u * (jnp.exp(-0.5 * u * u) * 0.3989422804014327)).astype(BF)
    result = x2
    for c in range(cuts):
        result = result + dot(g[:, c * d : (c + 1) * d], wdown[:, c * d : (c + 1) * d])

    valid = (jnp.arange(tokens) < lengths[0])[:, None].astype(F32)
    dout = cotangent * valid
    dy3 = dout.astype(BF)
    grad_down = jnp.concatenate(
        [dot_tn(g[:, c * d : (c + 1) * d], dy3).astype(BF) for c in range(cuts)], axis=1
    )
    own_down = scatter_rows(grad_down)
    dg = jnp.concatenate(
        [dot_nt(dy3, wdown[:, c * d : (c + 1) * d]) for c in range(cuts)], axis=1
    )
    du = (dg * slope.astype(F32)).astype(BF)
    grad_up = dot(turned(h3), du).astype(BF)
    own_up = scatter_rows(grad_up)
    dh3 = dot_nt(du, wup)
    back3, gain3, bias3 = norm_back(dh3, unit3, inv3, gains[2])
    dx2 = dout + back3
    dy2 = dx2.astype(BF)
    do2 = dot_nt(dy2, wco).astype(BF)
    dqc, dkv = attn_bwd((qc, 0), kvc, 0, blocks, o2, do2, lse2, slots_used, False)
    dqc = dqc[0]
    dkvc = jnp.concatenate([dkv[0], dkv[1]], axis=1)
    mem_turned = turned(memory_pad)
    grad_mid = jnp.concatenate(
        [
            dot(turned(o2), dy2).astype(BF),
            dot(turned(h2), dqc).astype(BF),
            dot(mem_turned, dkvc).astype(BF),
        ],
        axis=1,
    )
    own_mid = scatter_rows(grad_mid)
    grad_memory = dot_nt(dkvc, wckv)[: memory.shape[0]]
    dh2 = dot_nt(dqc, wcq)
    back2, gain2, bias2 = norm_back(dh2, unit2, inv2, gains[1])
    dx1 = dx2 + back2
    dy1 = dx1.astype(BF)
    do = dot_nt(dy1, wso).astype(BF)
    dqkv = attn_bwd((qkv, 0), qkv, blocks, 2 * blocks, o, do, lse, lengths, True)
    dqkv = jnp.concatenate([dqkv[0], dqkv[1], dqkv[2]], axis=1)
    dh1 = dot_nt(dqkv, wqkv)
    back1, gain1, bias1 = norm_back(dh1, unit1, inv1, gains[0])
    grad_hidden = dx1 + back1
    norm_grads = jnp.stack([gain1, gain2, gain3, bias1, bias2, bias3])
    norm_grads = jnp.pad(norm_grads, ((0, 122), (0, 0))).astype(BF)
    grad_last = jnp.concatenate(
        [
            dot(turned(o), dy1).astype(BF),
            dot(turned(h1), dqkv).astype(BF),
            turned(norm_grads),
        ],
        axis=1,
    )
    own_last = scatter_rows(grad_last)

    own_up = (
        own_up.reshape(rows, cuts, ny, nx, rows).transpose(0, 3, 2, 1, 4).reshape(rows, ff)
    )
    own_down = jnp.concatenate(
        [own_down[:, c * d : (c + 1) * d] for c in range(cuts)], axis=0
    )
    own_norms = own_last[:, 4 * d : 4 * d + 6].T.astype(F32)
    return (
        result,
        grad_hidden,
        grad_memory,
        own_last[:, d : 4 * d].astype(F32),
        own_last[:, :d].astype(F32),
        own_mid[:, d : 2 * d].astype(F32),
        own_mid[:, 2 * d :].astype(F32),
        own_mid[:, :d].astype(F32),
        own_up.astype(F32),
        own_down.astype(F32),
        own_norms[:3],
        own_norms[3:],
    )


CORE, XBIT, YBIT = 1, 2, 4


def swap(a, bit):
    return lax.ppermute(a, ALL, [(i, i ^ bit) for i in range(32)])


def fence(*values):
    return lax.optimization_barrier(values)


def gather_line(w):
    return lax.all_gather(w, "gx", axis=0)


def gather_near(here):
    return here, swap(here, XBIT), swap(here, YBIT)


def gather_far(near):
    return swap(near[2][:2], XBIT), swap(near[1][2:], YBIT)


def swap_cores(pieces):
    return tuple(swap(p, CORE) for p in pieces)


def put_pieces(bits_ref, pieces, out):
    x, y, core = bits_ref[0], bits_ref[1], bits_ref[2]
    for k in range(10):
        at_core = core if k < 5 else 1 - core
        at_x = x if k % 5 in (0, 2) else 1 - x
        at_y = y if k % 5 in (0, 1) else 1 - y
        z0, z1 = {3: (0, 2), 4: (2, 4)}.get(k % 5, (0, 4))
        out[z0:z1, at_y * 4 + at_x * 2 + at_core] = pieces[k][...]


def place_kernel(bits_ref, *refs):
    put_pieces(bits_ref, refs[:10], refs[-1])


def place_dot_kernel(bits_ref, *refs):
    a, w, y = refs[10], refs[11], refs[12]
    put_pieces(bits_ref, refs[:10], w)
    whole = w[...].reshape(a.shape[1], w.shape[3])
    y[...] = dot(a[...], whole).astype(y.dtype)


def piece_specs(pieces, start, block):
    rows = pieces[0].shape[1]
    return [
        (p, pl.BlockSpec((p.shape[0], rows, block), lambda j, _: (0, 0, start // block + j)))
        for p in pieces
    ]


def place_out(rows, width, block):
    return (
        shaped((4, 8, rows, width), BF),
        pl.BlockSpec((4, 8, rows, block), lambda j, _: (0, 0, 0, j)),
    )


def place(pieces, start, width, bits, deps=()):
    rows = pieces[0].shape[1]
    block = min(width, 512)
    out = run(
        place_kernel,
        (width // block,),
        piece_specs(pieces, start, block),
        [place_out(rows, width, block)],
        prefetch=(bits,),
        deps=deps,
        cost=costs(0, 4 * 32 * rows * width),
        name="place",
    )
    return out.reshape(32 * rows, width)


def place_dot(pieces, start, width, bits, a, dtype, deps=()):
    rows, block = pieces[0].shape[1], 512
    whole = pl.BlockSpec(a.shape, lambda j, _: (0, 0))
    w, y = run(
        place_dot_kernel,
        (width // block,),
        piece_specs(pieces, start, block) + [(a, whole)],
        [
            place_out(rows, width, block),
            (
                shaped((a.shape[0], width), dtype),
                pl.BlockSpec((a.shape[0], block), lambda j, _: (0, j)),
            ),
        ],
        prefetch=(bits,),
        deps=deps,
        cost=costs(2 * a.shape[0] * 32 * rows * width, 4 * 32 * rows * width),
        name="place_dot",
    )
    return w.reshape(32 * rows, width), y


def store_rows(value, outs):
    near = outs[0].shape[0]
    half = outs[1].shape[0]
    columns = value.shape[1]
    outs[0][:, :columns] = value[:near]
    outs[1][:, :columns] = value[near : near + half]
    outs[2][:, :columns] = value[near + half :]


def row_outs(rows, columns, block):
    return [
        (shaped((r, columns), BF), pl.BlockSpec((r, block), lambda j, *_: (0, j)))
        for r in (rows * 3 // 4, rows // 8, rows // 8)
    ]


def wgrad_kernel(starts, extra, *refs):
    outs = refs[-3:]
    j = pl.program_id(0)
    for s in range(len(starts) - 1):
        a, a2, g, g2 = refs[4 * s : 4 * s + 4]

        @pl.when((j >= starts[s]) & (j < starts[s + 1]))
        def _(a=a, a2=a2, g=g, g2=g2):
            store_rows((dot(a[...], g[...]) + dot(a2[...], g2[...])).astype(BF), outs)

    if extra:

        @pl.when(j == starts[-1])
        def _():
            mine, theirs = refs[-5], refs[-4]
            store_rows((mine[...].astype(F32) + theirs[...].astype(F32)).astype(BF), outs)


def wgrad(segments, extra=(), deps=(), block=1024):
    starts, ins = [0], []
    for a, a2, g, g2, *span in segments:
        per = g.shape[2] // block
        first, end = span or (0, g.shape[0] * per)
        count, start = end - first, starts[-1]

        def at(j, start=start, count=count, per=per, first=first):
            k = first + jnp.clip(j - start, 0, count - 1)
            return (k // per, 0, k % per)

        whole = pl.BlockSpec(a.shape, lambda j: (0, 0))
        grads = pl.BlockSpec((None, g.shape[1], block), at)
        ins += [(a, whole), (a2, whole), (g, grads), (g2, grads)]
        starts.append(start + count)
    rows = segments[0][0].shape[0]
    columns = starts[-1] * block
    steps = starts[-1]
    if extra:
        ins += [(e, pl.BlockSpec(e.shape, lambda j: (0, 0))) for e in extra]
        columns += extra[0].shape[1]
        steps += 1
    return run(
        functools.partial(wgrad_kernel, tuple(starts), bool(extra)),
        (steps,),
        ins,
        row_outs(rows, columns, block),
        deps=deps,
        cost=costs(2 * rows * 1024 * columns, 4 * 512 * columns + 2 * rows * columns),
        name="wgrad",
    )


def wgrad_down_kernel(bits_ref, *refs):
    blocks, other, dy, dy2 = refs[:4], refs[4:8], refs[8], refs[9]
    mine = jnp.concatenate([r[...].T for r in blocks], axis=0)
    theirs = jnp.concatenate([r[...].T for r in other], axis=0)
    store_rows((dot(mine, dy[...]) + dot(theirs, dy2[...])).astype(BF), refs[10:])


def wgrad_down(bits, g, g_other, dy, dy_other, cuts):
    tokens, d = dy.shape

    def spec(rel, whole):
        def at(b, bits_ref):
            x = bits_ref[0] ^ (rel & 1)
            y = bits_ref[1] ^ (rel >> 1)
            block = b * 4 + y * 2 + x
            return (0, block * 2 + bits_ref[2] if whole else block)

        return pl.BlockSpec((tokens, 128), at)

    rows = pl.BlockSpec((tokens, d), lambda b, _: (0, 0))
    return run(
        wgrad_down_kernel,
        (cuts,),
        [(g, spec(r, True)) for r in range(4)]
        + [(g_other, spec(r, False)) for r in range(4)]
        + [(dy, rows), (dy_other, rows)],
        row_outs(512, cuts * d, d),
        prefetch=(bits,),
        cost=costs(2 * 512 * 1024 * cuts * d, 16 * tokens * d),
        name="wgrad_down",
    )


def up_kernel(bits_ref, *refs):
    h_ref, w_ref, g_ref, slope_ref, send_ref = refs[10:]
    put_pieces(bits_ref, refs[:10], w_ref)
    u = dot(h_ref[...], w_ref[...].reshape(h_ref.shape[1], w_ref.shape[3]))
    cdf = 0.5 * (1.0 + lax.erf(u * (0.5**0.5)))
    g = (u * cdf).astype(BF)
    g_ref[...] = g
    slope_ref[...] = (cdf + u * (jnp.exp(-0.5 * u * u) * 0.3989422804014327)).astype(BF)
    core = bits_ref[2]
    for k in range(0, g.shape[1], 256):
        send_ref[:, k // 2 : k // 2 + 128] = jnp.where(
            core == 0, g[:, k + 128 : k + 256], g[:, k : k + 128]
        )


def feed_up(bits, h, pieces, ff, deps=(), block=512):
    tokens, d = h.shape
    rows = pieces[0].shape[1]
    out = (shaped((tokens, ff), BF), pl.BlockSpec((tokens, block), lambda j, _: (0, j)))
    w, *rest = run(
        up_kernel,
        (ff // block,),
        piece_specs(pieces, 0, block) + [(h, pl.BlockSpec((tokens, d), lambda j, _: (0, 0)))],
        [
            place_out(rows, ff, block),
            out,
            out,
            (
                shaped((tokens, ff // 2), BF),
                pl.BlockSpec((tokens, block // 2), lambda j, _: (0, j)),
            ),
        ],
        prefetch=(bits,),
        deps=deps,
        cost=costs(2 * tokens * d * ff, 4 * d * ff + 4 * tokens * ff, 2 * tokens * ff),
        name="feed_up",
    )
    return w.reshape(d, ff), *rest


def down_kernel(g_ref, w_ref, x_ref, out_ref):
    @pl.when(pl.program_id(0) == 0)
    def _():
        out_ref[...] = x_ref[...]

    out_ref[...] += dot(g_ref[...], w_ref[...])


def feed_down(g, w, x, cuts, deps=()):
    tokens, d = x.shape
    block = d // 2
    whole = pl.BlockSpec((tokens, d), lambda j: (0, 0))
    return run(
        down_kernel,
        (2 * cuts,),
        [
            (g, pl.BlockSpec((tokens, block), lambda j: (0, j))),
            (w, pl.BlockSpec((block, d), lambda j: (j % 2, j // 2))),
            (x, whole),
        ],
        [(shaped((tokens, d), F32), whole)],
        deps=deps,
        cost=costs(2 * tokens * d * d * cuts, 2 * d * d * cuts + 10 * tokens * d),
        name="feed_down",
    )


def norm_back_store(acc, x_ref, gain_ref, res_ref, dx_ref, low_ref, sums_ref):
    gain_grad, bias_grad = 0.0, 0.0
    step = 128
    for r in range(0, x_ref.shape[0], step):
        part = slice(r, r + step)
        x, dh = x_ref[part, :], acc[part, :]
        center = x - jnp.mean(x, -1, keepdims=True)
        inverse = lax.rsqrt(jnp.mean(center * center, -1, keepdims=True) + 1e-05)
        unit = center * inverse
        gain_grad += jnp.sum(dh * unit, axis=0, keepdims=True)
        bias_grad += jnp.sum(dh, axis=0, keepdims=True)
        scaled = dh * gain_ref[...]
        mean_a = jnp.mean(scaled, -1, keepdims=True)
        mean_b = jnp.mean(scaled * unit, -1, keepdims=True)
        dx = res_ref[part, :] + inverse * (scaled - mean_a - unit * mean_b)
        dx_ref[part, :] = dx
        if low_ref is not None:
            low_ref[part, :] = dx.astype(BF)
    sums_ref[0:1, :] = gain_grad
    sums_ref[1:2, :] = bias_grad


def accumulate(acc, part):
    j = pl.program_id(0)

    @pl.when(j == 0)
    def _():
        acc[...] = part

    @pl.when(j > 0)
    def _():
        acc[...] += part


def feed_back_kernel(
    dy_ref, w2_ref, slope_ref, w1_ref, x_ref, gain_ref, res_ref, du_ref, dx_ref, low_ref, sums_ref, acc
):
    du = (dot_nt(dy_ref[...], w2_ref[...]) * slope_ref[...].astype(F32)).astype(BF)
    du_ref[...] = du
    accumulate(acc, dot_nt(du, w1_ref[...]))

    @pl.when(pl.program_id(0) == pl.num_programs(0) - 1)
    def _():
        norm_back_store(acc, x_ref, gain_ref, res_ref, dx_ref, low_ref, sums_ref)


def feed_back(dy, w2, slope, w1, x, gain, res, cuts, deps=()):
    tokens, d = x.shape
    block = d // 2
    ff = w1.shape[1]
    whole = pl.BlockSpec((tokens, d), lambda j: (0, 0), pipeline_mode=pl.Buffered(1))
    part = pl.BlockSpec((tokens, block), lambda j: (0, j))
    return run(
        feed_back_kernel,
        (2 * cuts,),
        [
            (dy, whole),
            (w2, pl.BlockSpec((block, d), lambda j: (j % 2, j // 2))),
            (slope, part),
            (w1, pl.BlockSpec((d, block), lambda j: (0, j))),
            (x, whole),
            (gain, pl.BlockSpec((1, d), lambda j: (0, 0))),
            (res, whole),
        ],
        [
            (shaped((tokens, ff), BF), part),
            (shaped((tokens, d), F32), whole),
            (shaped((tokens, d), BF), whole),
            (shaped((2, d), F32), pl.BlockSpec((2, d), lambda j: (0, 0))),
        ],
        scratch=[pltpu.VMEM((tokens, d), F32)],
        deps=deps,
        cost=costs(4 * tokens * d * ff, 4 * d * ff + 4 * tokens * ff + 16 * tokens * d),
        name="feed_back",
    )


def norm_back_kernel(g_ref, w_ref, x_ref, gain_ref, res_ref, *refs):
    dx_ref, sums_ref, acc = refs[0], refs[-2], refs[-1]
    low_ref = refs[1] if len(refs) == 4 else None
    accumulate(acc, dot_nt(g_ref[...], w_ref[...]))

    @pl.when(pl.program_id(0) == pl.num_programs(0) - 1)
    def _():
        norm_back_store(acc, x_ref, gain_ref, res_ref, dx_ref, low_ref, sums_ref)


def through_norm(g, w, x, gain, res, low=True, deps=()):
    tokens, d = x.shape
    block = 512
    per = g.shape[2] // block
    count = g.shape[0] * per
    whole = pl.BlockSpec((tokens, d), lambda j: (0, 0), pipeline_mode=pl.Buffered(1))
    outs = [(shaped((tokens, d), F32), whole)]
    if low:
        outs.append((shaped((tokens, d), BF), whole))
    outs.append((shaped((2, d), F32), pl.BlockSpec((2, d), lambda j: (0, 0))))
    return run(
        norm_back_kernel,
        (count,),
        [
            (g, pl.BlockSpec((None, tokens, block), lambda j: (j // per, 0, j % per))),
            (w, pl.BlockSpec((d, block), lambda j: (0, j))),
            (x, whole),
            (gain, pl.BlockSpec((1, d), lambda j: (0, 0))),
            (res, whole),
        ],
        outs,
        scratch=[pltpu.VMEM((tokens, d), F32)],
        deps=deps,
        cost=costs(2 * tokens * d * block * count, 2 * d * block * count + 16 * tokens * d),
        name="through_norm",
    )


def scatter_far(grads):
    return swap(grads[1], XBIT), swap(grads[2], YBIT)


def pass_on_kernel(x_ref, y_ref, from_x, from_y, to_x, to_y):
    half = from_x.shape[0]
    to_x[:half] = x_ref[:half]
    to_x[half:] = x_ref[half:] + from_y[...]
    to_y[:half] = y_ref[:half] + from_x[...]
    to_y[half:] = y_ref[half:]


def sum_kernel(own, got_x, got_y, out):
    total = own[...].astype(F32) + got_x[...].astype(F32) + got_y[...].astype(F32)
    out[...] = total.astype(out.dtype)


def column_blocks(columns):
    return columns if columns <= 2304 else next(b for b in (2048, 1024, 640) if columns % b == 0)


def rows_spec(rows, block, at=0):
    return pl.BlockSpec((rows, block), lambda j: (at, j))


def scatter_near(near, far):
    rows, columns = near.shape[0] // 3, near.shape[1]
    block = column_blocks(columns)
    far_spec, out = rows_spec(rows // 2, block), (shaped((rows, columns), BF), rows_spec(rows, block))
    to_x, to_y = run(
        pass_on_kernel,
        (columns // block,),
        [
            (near, rows_spec(rows, block, 1)),
            (near, rows_spec(rows, block, 2)),
            (far[0], far_spec),
            (far[1], far_spec),
        ],
        [out, out],
        cost=costs(rows * columns, 10 * rows * columns),
        name="pass_on",
    )
    return swap(to_x, XBIT), swap(to_y, YBIT)


def plane_sum(near, got, dtype):
    rows, columns = got[0].shape
    block = column_blocks(columns)
    return run(
        sum_kernel,
        (columns // block,),
        [(a, rows_spec(rows, block)) for a in (near, *got)],
        [(shaped((rows, columns), dtype), rows_spec(rows, block))],
        cost=costs(2 * rows * columns, 8 * rows * columns),
        name="plane_sum",
    )


def scatter_line(near, got):
    total = plane_sum(near, got, BF)
    return lax.psum_scatter(total, "gx", scatter_dimension=0, tiled=True)


def scatter_line_direct(near, got, z):
    total = plane_sum(near, got, F32)
    total = total.reshape(4, -1, total.shape[1])
    low = total.astype(BF)
    own = lax.dynamic_index_in_dim(total, z, 0, keepdims=False)
    for step in (1, 2, 3):
        part = lax.dynamic_index_in_dim(low, (z + step) % 4, 0, keepdims=False)
        came = lax.ppermute(part, ALL, [(i, (i + 8 * step) % 32) for i in range(32)])
        own = own + came.astype(F32)
    return own


def turn_kernel(select_ref, a_ref, mine, theirs):
    rows = dot_nt(select_ref[...], a_ref[...]).astype(BF)
    half = pl.num_programs(0) // 2

    @pl.when(pl.program_id(0) < half)
    def _():
        mine[...] = rows

    @pl.when(pl.program_id(0) >= half)
    def _():
        theirs[...] = rows


def turn(select, a):
    tokens, d = a.shape
    steps = 4
    block, half = d // steps, steps // 2
    out = shaped((d // 2, tokens), BF)
    return run(
        turn_kernel,
        (steps,),
        [
            (select, pl.BlockSpec((block, d), lambda j: (j, 0))),
            (a, pl.BlockSpec((tokens, d), lambda j: (0, 0))),
        ],
        [
            (out, pl.BlockSpec((block, tokens), lambda j: (jnp.minimum(j, half - 1), 0))),
            (out, pl.BlockSpec((block, tokens), lambda j: (jnp.maximum(j - half, 0), 0))),
        ],
        cost=costs(2 * d * d * tokens, 2 * d * d + 4 * d * tokens),
        name="turn",
    )


def hidden_order_kernel(to_hidden, rows, cuts, src, out):
    lines = 4
    width = lines * cuts * rows
    at = lax.broadcasted_iota(jnp.int32, (width, width), 0)
    to = lax.broadcasted_iota(jnp.int32, (width, width), 1)
    first, second = (lines, cuts) if to_hidden else (cuts, lines)
    moved = (at // rows % second * first + at // (rows * second)) * rows + at % rows
    swap_two = (moved == to).astype(F32).astype(BF)
    for place_at in range(8):
        if to_hidden:
            step, parts, wide = cuts * rows, lines, cuts * rows
        else:
            step, parts, wide = lines * rows, cuts, lines * rows
        pieces = [
            src[:, (k * 8 + place_at) * step : (k * 8 + place_at) * step + wide]
            for k in range(parts)
        ]
        done = dot(jnp.concatenate(pieces, axis=1), swap_two)
        out_step = lines * rows if to_hidden else cuts * rows
        for k in range(cuts if to_hidden else lines):
            at_column = (k * 8 + place_at) * out_step
            out[:, at_column : at_column + out_step] = done[
                :, k * out_step : (k + 1) * out_step
            ].astype(out.dtype)


def hidden_order(a, to_hidden, cuts, dtype):
    rows, ff = a.shape
    whole = pl.BlockSpec((rows, ff), lambda j: (0, 0))
    return run(
        functools.partial(hidden_order_kernel, to_hidden, ff // 32 // cuts, cuts),
        (1,),
        [(a, whole)],
        [(shaped((rows, ff), dtype), whole)],
        cost=costs(2 * rows * ff * 512, 6 * rows * ff),
        name="hidden_order",
    )


def memory_grad_kernel(g_ref, w_ref, out_ref):
    part = dot_nt(g_ref[...], w_ref[...])[: out_ref.shape[0]]

    @pl.when(pl.program_id(0) == 0)
    def _():
        out_ref[...] = part

    @pl.when(pl.program_id(0) > 0)
    def _():
        out_ref[...] += part


def memory_grad(g, w, rows):
    _, padded, d = g.shape
    block = d // 2
    return run(
        memory_grad_kernel,
        (4,),
        [
            (g, pl.BlockSpec((None, padded, block), lambda j: (j // 2, 0, j % 2))),
            (w, pl.BlockSpec((d, block), lambda j: (0, j))),
        ],
        [(shaped((rows, d), F32), pl.BlockSpec((rows, d), lambda j: (0, 0)))],
        cost=costs(4 * padded * d * d, 8 * d * d + 4 * rows * d),
        name="memory_grad",
    )


def shards_plane(
    hidden,
    memory,
    lengths,
    page_class,
    cotangent,
    w_self_qkv,
    w_self_out,
    w_cross_q,
    w_cross_kv,
    w_cross_out,
    w_fc1,
    w_fc2,
    norm_gains,
    norm_biases,
):
    tokens, d = hidden.shape
    rows, ff = w_fc1.shape
    cuts = w_fc2.shape[0] // rows
    mem_rows = -(-memory.shape[0] // 16) * 16
    slots_used = jnp.where(page_class == 0, MEM_BIG, MEM_BIG // 4).astype(jnp.int32)
    along = lax.axis_index("gy")
    x_at, y_at, core = (along // 2) % 2, along // 4, along % 2
    z_at = lax.axis_index("gx")
    bits = jnp.stack([x_at, y_at, core]).astype(jnp.int32)

    norm_cols = jnp.concatenate([norm_gains, norm_biases], axis=0).T
    norm_cols = jnp.pad(norm_cols, ((0, 0), (0, 128 - norm_cols.shape[1])))
    up_local = hidden_order(w_fc1, True, cuts, BF)
    down_local = jnp.concatenate(
        [w_fc2[c * rows : (c + 1) * rows] for c in range(cuts)], axis=1
    )
    place_at = jnp.arange(d)
    r = place_at % rows
    z = (place_at // rows) % 4
    rel = (place_at // (4 * rows)) % 4
    source_core = core ^ (place_at // (16 * rows))
    device = z * 8 + (y_at ^ (rel // 2)) * 4 + (x_at ^ (rel % 2)) * 2 + source_core
    select = ((device * rows + r)[:, None] == place_at[None, :]).astype(BF)

    def turned(a):
        mine, theirs = turn(select, a)
        return mine, swap(theirs, CORE)

    pack1 = jnp.concatenate([w_self_qkv, norm_cols], axis=1)
    pack2 = jnp.concatenate([w_cross_kv, w_self_out, w_cross_q, w_cross_out], axis=1)
    blocks = d // PAIR
    memory_pad = jnp.pad(memory, ((0, mem_rows - memory.shape[0]), (0, 0)))

    line1, pack2, memory_pad, hidden = fence(gather_line(pack1), pack2, memory_pad, hidden)

    line2 = gather_line(pack2)
    near1 = gather_near(line1)
    mem_t = turned(memory_pad)
    unit1, _ = norm_parts(hidden)
    near1, mem_t, unit1 = fence(near1, mem_t, unit1)

    near1, far1, cores1, line2, pack3 = fence(
        near1, gather_far(near1), swap_cores(near1), line2, up_local
    )

    line3 = gather_line(pack3)
    near2 = gather_near(line2)
    first = near1 + far1 + cores1 + swap_cores(far1)
    norms = place(first, 3 * d, 128, bits)[:, :6].T.astype(F32)
    gains, biases = norms[:3], norms[3:]
    h1 = (unit1 * gains[0] + biases[0]).astype(BF)
    wqkv, qkv = place_dot(first, 0, 3 * d, bits, h1, BF)
    o, lse = attn_fwd((qkv, 0), qkv, blocks, 2 * blocks, lengths, True)
    near2, o, h1, gains, biases = fence(near2, o, h1, gains, biases)

    near2, far2, cores2, h1, o, line3, pack4 = fence(
        near2, gather_far(near2), swap_cores(near2), h1, o, line3, down_local
    )

    wdown = lax.all_gather(pack4, ("gy", "gx"), axis=0, tiled=True)
    near3 = gather_near(line3)
    second = near2 + far2 + cores2 + swap_cores(far2)
    wso, y1 = place_dot(second, 2 * d, d, bits, o, F32)
    x1 = hidden + y1
    unit2, _ = norm_parts(x1)
    h2 = (unit2 * gains[1] + biases[1]).astype(BF)
    wcq, qc = place_dot(second, 3 * d, d, bits, h2, BF)
    wckv, kvc = place_dot(second, 0, 2 * d, bits, memory_pad, BF)
    h1_t, o_t = turned(h1), turned(o)
    near3, second, qc, kvc, h2, x1, h1_t, o_t = fence(
        near3, second, qc, kvc, h2, x1, h1_t, o_t
    )

    far3, cores3 = gather_far(near3), swap_cores(near3)
    o2, lse2 = attn_fwd((qc, 0), kvc, 0, blocks, slots_used, False)
    near3, far3, cores3, o2, h2, cotangent = fence(near3, far3, cores3, o2, h2, cotangent)

    third = near3 + far3 + cores3 + swap_cores(far3)
    wco, y2 = place_dot(second, 4 * d, d, bits, o2, F32)
    x2 = x1 + y2
    unit3, _ = norm_parts(x2)
    h3 = (unit3 * gains[2] + biases[2]).astype(BF)
    valid = (jnp.arange(tokens) < lengths[0])[:, None].astype(F32)
    dout = cotangent * valid
    dy3 = dout.astype(BF)
    dy3_other = swap(dy3, CORE)
    third, h3, x2, o2, dout, dy3, dy3_other = fence(third, h3, x2, o2, dout, dy3, dy3_other)

    wup, g, slope, g_send = feed_up(bits, h3, third, ff)
    wup, g, slope, g_send, h3, o2 = fence(wup, g, slope, g_send, h3, o2)

    h2_t, h3_t, o2_t = turned(h2), turned(h3), turned(o2)
    g_other, h2_t, h3_t, o2_t, g = fence(swap(g_send, CORE), h2_t, h3_t, o2_t, g)

    grad_down = wgrad_down(bits, g, g_other, dy3, dy3_other, cuts)
    grad_down, dy3, slope, wdown = fence(grad_down, dy3, slope, wdown)

    du, dx2, dy2, sums3 = feed_back(dy3, wdown, slope, wup, x2, gains[2:3], dout, cuts)
    far1, du, dx2, dy2, g = fence(scatter_far(grad_down), du, dx2, dy2, g)

    got1 = scatter_near(grad_down[0], far1)
    do2 = dot_nt(dy2, wco).astype(BF)
    du_other, do2, du = fence(swap(du, CORE), do2, du)

    grad_up = wgrad([h3_t + (du[None], du_other[None])])
    grad_up, do2, dy2 = fence(grad_up, do2, dy2)

    dqc, dkvc = attn_bwd((qc, 0), kvc, 0, blocks, o2, do2, lse2, slots_used, False)
    far2, got1, dqc, dkvc, dy2_other, dx2 = fence(
        scatter_far(grad_up), got1, dqc, dkvc, swap(dy2, CORE), dx2
    )

    own_down = scatter_line(grad_down[0], got1)
    got2 = scatter_near(grad_up[0], far2)
    dx1, dy1, sums2 = through_norm(dqc, wcq, x1, gains[1:2], dx2)
    do = dot_nt(dy1, wso).astype(BF)
    dqc_other, dkvc_other, dx1, dy1, do, dqc, dkvc = fence(
        swap(dqc, CORE), swap(dkvc, CORE), dx1, dy1, do, dqc, dkvc
    )

    grad_mid = wgrad(
        [
            o2_t + (dy2[None], dy2_other[None]),
            h2_t + (dqc, dqc_other),
            mem_t + (dkvc, dkvc_other),
        ]
    )
    grad_mid, do, dy1 = fence(grad_mid, do, dy1)

    dqkv = attn_bwd((qkv, 0), qkv, blocks, 2 * blocks, o, do, lse, lengths, True)
    far3, dy1_other, dqkv, got2, dx1 = fence(
        scatter_far(grad_mid), swap(dy1, CORE), dqkv, got2, dx1
    )

    own_up = scatter_line(grad_up[0], got2)
    got3 = scatter_near(grad_mid[0], far3)
    grad_hidden, sums1 = through_norm(dqkv, wqkv, hidden, gains[0:1], dx1, low=False)
    sums = jnp.concatenate([sums1, sums2, sums3], axis=0)
    sums = jnp.pad(sums, ((0, 122), (0, 0))).astype(BF)
    dqkv_other, grad_hidden, sums_t = fence(swap(dqkv, CORE), grad_hidden, turned(sums))

    grad_a = wgrad(
        [o_t + (dy1[None], dy1_other[None]), h1_t + (dqkv, dqkv_other, 0, 1)]
    )
    grad_a, dqkv, dqkv_other, sums_t = fence(grad_a, dqkv, dqkv_other, sums_t)

    grad_b = wgrad([h1_t + (dqkv, dqkv_other, 1, 3)], extra=sums_t)
    far_a, grad_b, got3, dkvc, own_down = fence(
        scatter_far(grad_a), grad_b, got3, dkvc, own_down
    )

    got_a = scatter_near(grad_a[0], far_a)
    own_mid = scatter_line(grad_mid[0], got3)
    grad_memory = memory_grad(dkvc, wckv, memory.shape[0])
    far_b, got_a, grad_memory, own_up, g = fence(
        scatter_far(grad_b), got_a, grad_memory, own_up, g
    )

    got_b = scatter_near(grad_b[0], far_b)
    own_a = scatter_line_direct(grad_a[0], got_a, z_at)
    own_up = hidden_order(own_up, False, cuts, F32)
    result = feed_down(g, wdown, x2, cuts)
    got_b, own_a, own_up, result = fence(got_b, own_a, own_up, result)

    own_b = scatter_line_direct(grad_b[0], got_b, z_at)
    own_qkv = jnp.concatenate([own_a[:, d:], own_b[:, : 2 * d]], axis=1)
    own_down = jnp.concatenate(
        [own_down[:, c * d : (c + 1) * d] for c in range(cuts)], axis=0
    )
    own_sums = own_b[:, 2 * d : 2 * d + 6].T
    return (
        result,
        grad_hidden,
        grad_memory,
        own_qkv,
        own_a[:, :d],
        own_mid[:, d : 2 * d].astype(F32),
        own_mid[:, 2 * d :].astype(F32),
        own_mid[:, :d].astype(F32),
        own_up,
        own_down.astype(F32),
        own_sums[0::2],
        own_sums[1::2],
    )


def solution(mesh):
    row = P(ALL, None)
    col = P(None, ALL)
    nx, ny = mesh.shape["gx"], mesh.shape["gy"]
    body = shards_plane if (nx, ny) == (4, 8) else functools.partial(shards_any, nx=nx, ny=ny)
    return jax.shard_map(
        body,
        mesh=mesh,
        in_specs=(row, row, P(ALL), P(ALL), row) + (row,) * 7 + (col, col),
        out_specs=(row,) * 10 + (col, col),
        check_vma=False,
    )
```

```python
import functools

import jax
import jax.numpy as jnp
from jax import lax
from jax.experimental import pallas as pl
from jax.experimental.pallas import tpu as pltpu
from jax.sharding import PartitionSpec as P

HEADS = 16
MEM_BIG = 588
ALL = ("gx", "gy")
BF = jnp.bfloat16
F32 = jnp.float32
PAIR = 128
LIMITS = {'feed_back': 50, 'pass_on': 8, 'plane_sum': 8, 'place': 8, 'hidden_order': 8, 'memory_grad': 12, 'turn': 12, 'wgrad': 44, 'wgrad_down': 44, 'wgrad_mid': 44, 'finish': 12, 'line_parts': 12}
FAR_OUTS = {'wgrad': (0, 1, 2), 'wgrad_down': (0, 1, 2, 3, 4, 5, 6), 'feed_up': (0, 1, 2), 'place_dot': (0,), 'feed_back': (0, 1), 'turn': (0, 1), 'wgrad_mid': (0, 1, 2)}
FAR_INS = {'pass_on': (0, 1, 2, 3), 'plane_sum': (0, 1, 2), 'wgrad_mid': (0, 1, 2, 3, 4, 5, 6, 7, 8, 9, 10, 11), 'attn_bwd': (0, 1, 2, 3, 4)}


def dot(a, b):
    return jnp.dot(a, b, preferred_element_type=F32)


def dot_nt(a, b):
    return lax.dot_general(a, b, (((1,), (1,)), ((), ())), preferred_element_type=F32)


def dot_tn(a, b):
    return lax.dot_general(a, b, (((0,), (0,)), ((), ())), preferred_element_type=F32)


def run(
    kernel, grid, ins, outs, prefetch=(), scratch=(), deps=(), cost=None, name=None
):
    count = len(prefetch) + len(ins)

    def body(*refs):
        return kernel(*refs[:count], *refs[count + len(deps) :])

    result = pl.pallas_call(
        body,
        grid_spec=pltpu.PrefetchScalarGridSpec(
            num_scalar_prefetch=len(prefetch),
            grid=grid,
            in_specs=[spec for _, spec in ins] + [pl.BlockSpec(memory_space=pl.ANY)] * len(deps),
            out_specs=[spec for _, spec in outs],
            scratch_shapes=scratch,
        ),
        out_shape=[
            pltpu.HBM(shape.shape, shape.dtype) if k in FAR_OUTS.get(name, ()) else shape
            for k, (shape, _) in enumerate(outs)
        ],
        compiler_params=pltpu.CompilerParams(
            dimension_semantics=("arbitrary",) * len(grid), vmem_limit_bytes=LIMITS.get(name, 30) * 1024 * 1024
        ),
        cost_estimate=cost,
        name=name,
    )(
        *prefetch,
        *[
            pltpu.with_memory_space_constraint(a, pltpu.HBM)
            if k in FAR_INS.get(name, ())
            else a
            for k, (a, _) in enumerate(ins)
        ],
        *deps,
    )
    return result if len(outs) > 1 else result[0]


def costs(flops, nbytes, transcendentals=0):
    return pl.CostEstimate(
        flops=flops, bytes_accessed=nbytes, transcendentals=transcendentals
    )


def shaped(shape, dtype):
    return jax.ShapeDtypeStruct(shape, dtype)


def allowed_t(key_count, q0, q1, limit, causal):
    key_at = lax.broadcasted_iota(jnp.int32, (key_count, q1 - q0), 0)
    ok = key_at < limit
    if causal:
        query_at = lax.broadcasted_iota(jnp.int32, (key_count, q1 - q0), 1) + q0
        ok = ok & (key_at <= query_at)
    return ok


def half_mask(width, half):
    lane = lax.broadcasted_iota(jnp.int32, (1, width), 1)
    return ((lane // (width // 2)) == half).astype(F32).astype(BF)


def attn_fwd_kernel(spans, causal, limit_ref, q_ref, k_ref, v_ref, o_ref, lse_ref):
    width = q_ref.shape[1]
    half = width // 2
    limit = limit_ref[0]
    scale = BF(half**-0.5)
    v_t = v_ref[...].T
    work = [(q0, q1, keys, h) for q0, q1, keys in spans for h in range(2)]
    scores = [
        dot_nt(k_ref[:keys, :], q_ref[q0:q1, :] * scale * half_mask(width, h))
        for q0, q1, keys, h in work
    ]
    outs = {}
    for (q0, q1, keys, h), s in zip(work, scores, strict=True):
        s = jnp.where(allowed_t(keys, q0, q1, limit, causal), s, -1e30)
        top = jnp.max(s, axis=0, keepdims=True)
        e = jnp.exp(s - top)
        total = jnp.sum(e, axis=0, keepdims=True)
        outs[q0, h] = dot(v_t[h * half : (h + 1) * half, :keys], e.astype(BF)) / total
        lse_ref[0, h : h + 1, q0:q1] = top + jnp.log(total)
    for q0, q1, _ in spans:
        o_ref[q0:q1, :] = jnp.concatenate([outs[q0, 0], outs[q0, 1]], axis=0).T.astype(BF)


def attn_bwd_kernel(
    spans, causal, limit_ref, q_ref, k_ref, v_ref, o_ref, do_ref, lse_ref, *outs_ref
):
    dq_ref = outs_ref[0].at[0]
    dk_ref, dv_ref = (outs_ref[-1].at[k - 2 + outs_ref[-1].shape[0]] for k in range(2))
    width = q_ref.shape[1]
    half = width // 2
    limit = limit_ref[0]
    scale = BF(half**-0.5)
    k_t = k_ref[...].T * scale
    total_k = k_ref.shape[0]
    masks = [half_mask(width, h) for h in range(2)]
    dk = jnp.zeros((total_k, width), F32)
    dv = jnp.zeros((total_k, width), F32)
    for q0, q1, keys in spans:
        query = q_ref[q0:q1, :] * scale
        grad_o = do_ref[q0:q1, :]
        ok = allowed_t(keys, q0, q1, limit, causal)
        both = (grad_o.astype(F32) * o_ref[q0:q1, :].astype(F32)).T
        query_h = [query * m for m in masks]
        grad_h = [grad_o * m for m in masks]
        scores = [dot_nt(k_ref[:keys, :], a) for a in query_h]
        dps = [dot_nt(v_ref[:keys, :], a) for a in grad_h]
        probs, dss = [], []
        for h in range(2):
            inner = jnp.sum(both[h * half : (h + 1) * half], axis=0, keepdims=True)
            p = jnp.where(ok, jnp.exp(scores[h] - lse_ref[0, h : h + 1, q0:q1]), 0.0)
            probs.append(p.astype(BF))
            dss.append((p * (dps[h] - inner)).astype(BF))
        dv_part = dot(probs[0], grad_h[0]) + dot(probs[1], grad_h[1])
        dk_part = dot(dss[0], query_h[0]) + dot(dss[1], query_h[1])
        outs = [dot(k_t[h * half : (h + 1) * half, :keys], dss[h]) for h in range(2)]
        dq_ref[q0:q1, :] = jnp.concatenate(outs, axis=0).T.astype(BF)
        if keys < total_k:
            pad = jnp.zeros((total_k - keys, width), F32)
            dk_part = jnp.concatenate([dk_part, pad], axis=0)
            dv_part = jnp.concatenate([dv_part, pad], axis=0)
        dk += dk_part
        dv += dv_part
    dk_ref[...] = dk.astype(BF)
    dv_ref[...] = dv.astype(BF)


def make_spans(queries, keys, causal):
    step = 256
    return tuple(
        (q, q + step, min(q + step, keys) if causal else keys) for q in range(0, queries, step)
    )


def attn_fwd(q, kv, k_at, v_at, limit, causal, deps=()):
    q_arr, q_at = q
    queries, keys = q_arr.shape[0], kv.shape[0]
    pairs = HEADS // 2
    return run(
        functools.partial(attn_fwd_kernel, make_spans(queries, keys, causal), causal),
        (pairs,),
        [
            (q_arr, pl.BlockSpec((queries, PAIR), lambda p, _: (0, q_at + p))),
            (kv, pl.BlockSpec((keys, PAIR), lambda p, _: (0, k_at + p))),
            (kv, pl.BlockSpec((keys, PAIR), lambda p, _: (0, v_at + p))),
        ],
        [
            (
                shaped((queries, pairs * PAIR), BF),
                pl.BlockSpec((queries, PAIR), lambda p, _: (0, p)),
            ),
            (
                shaped((pairs, 2, queries), F32),
                pl.BlockSpec((1, 2, queries), lambda p, _: (p, 0, 0)),
            ),
        ],
        prefetch=(limit,),
        deps=deps,
        cost=costs(16 * queries * keys * 1024, 8 * queries * 1024, 16 * queries * keys),
        name="attn_fwd",
    )


def attn_bwd(q, kv, k_at, v_at, o, do, lse, limit, causal, deps=()):
    q_arr, q_at = q
    queries, keys = q_arr.shape[0], kv.shape[0]
    pairs = HEADS // 2
    q_block = pl.BlockSpec((queries, PAIR), lambda p, _: (0, p))

    def stacked(count, rows):
        return (
            shaped((count, rows, pairs * PAIR), BF),
            pl.BlockSpec((count, rows, PAIR), lambda p, _: (0, 0, p)),
        )

    return run(
        functools.partial(attn_bwd_kernel, make_spans(queries, keys, causal), causal),
        (pairs,),
        [
            (q_arr, pl.BlockSpec((queries, PAIR), lambda p, _: (0, q_at + p))),
            (kv, pl.BlockSpec((keys, PAIR), lambda p, _: (0, k_at + p))),
            (kv, pl.BlockSpec((keys, PAIR), lambda p, _: (0, v_at + p))),
            (o, q_block),
            (do, q_block),
            (lse, pl.BlockSpec((1, 2, queries), lambda p, _: (p, 0, 0))),
        ],
        [stacked(3, queries)] if queries == keys else [stacked(1, queries), stacked(2, keys)],
        prefetch=(limit,),
        deps=deps,
        cost=costs(16 * queries * keys * 2560, 16 * queries * 1024, 16 * queries * keys),
        name="attn_bwd",
    )


def norm_parts(v):
    center = v - jnp.mean(v, -1, keepdims=True)
    inverse = lax.rsqrt(jnp.mean(center * center, -1, keepdims=True) + 1e-05)
    return center * inverse, inverse


def norm_back(grad, unit, inverse, gain):
    gain_grad = jnp.sum(grad * unit, axis=0)
    bias_grad = jnp.sum(grad, axis=0)
    scaled = grad * gain
    mean_a = jnp.mean(scaled, -1, keepdims=True)
    mean_b = jnp.mean(scaled * unit, -1, keepdims=True)
    return inverse * (scaled - mean_a - unit * mean_b), gain_grad, bias_grad


def gather_rows(w):
    return lax.all_gather(w, ALL, axis=0, tiled=True)


def scatter_rows(g):
    part = lax.psum_scatter(g, "gy", scatter_dimension=0, tiled=True)
    return lax.psum_scatter(part, "gx", scatter_dimension=0, tiled=True)


def shards_any(
    hidden,
    memory,
    lengths,
    page_class,
    cotangent,
    w_self_qkv,
    w_self_out,
    w_cross_q,
    w_cross_kv,
    w_cross_out,
    w_fc1,
    w_fc2,
    norm_gains,
    norm_biases,
    *,
    nx,
    ny,
):
    n = nx * ny
    tokens, d = hidden.shape
    rows = w_fc1.shape[0]
    ff = w_fc1.shape[1]
    cuts = w_fc2.shape[0] // rows
    mem_rows = -(-memory.shape[0] // 16) * 16
    slots_used = jnp.where(page_class == 0, MEM_BIG, MEM_BIG // 4).astype(jnp.int32)

    norm_cols = jnp.concatenate([norm_gains, norm_biases], axis=0).T
    norm_cols = jnp.pad(norm_cols, ((0, 0), (0, 128 - norm_cols.shape[1])))
    first = jnp.concatenate([w_self_qkv, w_cross_kv, norm_cols], axis=1)
    second = jnp.concatenate([w_self_out, w_cross_q, w_cross_out], axis=1)
    up_local = (
        w_fc1.reshape(rows, nx, ny, cuts, rows).transpose(0, 3, 2, 1, 4).reshape(rows, ff)
    )
    down_local = jnp.concatenate(
        [w_fc2[c * rows : (c + 1) * rows] for c in range(cuts)], axis=1
    )
    w_first = gather_rows(first)
    w_second = gather_rows(second)
    wup = gather_rows(up_local)
    wdown = lax.all_gather(down_local, ("gy", "gx"), axis=0, tiled=True)

    wqkv = w_first[:, : 3 * d]
    wckv = w_first[:, 3 * d : 5 * d]
    norms = w_first[:, 5 * d : 5 * d + 6].T.astype(F32)
    gains, biases = norms[:3], norms[3:]
    wso, wcq, wco = w_second[:, :d], w_second[:, d : 2 * d], w_second[:, 2 * d :]

    place = jnp.arange(d)
    source = place % rows + ((place // rows) % nx * ny + place // (rows * nx)) * rows
    select = (source[:, None] == place[None, :]).astype(BF)

    def turned(a):
        return dot_nt(select, a).astype(BF)

    unit1, inv1 = norm_parts(hidden)
    h1 = (unit1 * gains[0] + biases[0]).astype(BF)
    qkv = dot(h1, wqkv).astype(BF)
    blocks = d // PAIR
    o, lse = attn_fwd((qkv, 0), qkv, blocks, 2 * blocks, lengths, True)
    x1 = hidden + dot(o, wso)
    unit2, inv2 = norm_parts(x1)
    h2 = (unit2 * gains[1] + biases[1]).astype(BF)
    qc = dot(h2, wcq).astype(BF)
    memory_pad = jnp.pad(memory, ((0, mem_rows - memory.shape[0]), (0, 0)))
    kvc = dot(memory_pad, wckv).astype(BF)
    o2, lse2 = attn_fwd((qc, 0), kvc, 0, blocks, slots_used, False)
    x2 = x1 + dot(o2, wco)
    unit3, inv3 = norm_parts(x2)
    h3 = (unit3 * gains[2] + biases[2]).astype(BF)
    u = dot(h3, wup)
    cdf = 0.5 * (1.0 + lax.erf(u * (0.5**0.5)))
    g = (u * cdf).astype(BF)
    slope = (cdf + u * (jnp.exp(-0.5 * u * u) * 0.3989422804014327)).astype(BF)
    result = x2
    for c in range(cuts):
        result = result + dot(g[:, c * d : (c + 1) * d], wdown[:, c * d : (c + 1) * d])

    valid = (jnp.arange(tokens) < lengths[0])[:, None].astype(F32)
    dout = cotangent * valid
    dy3 = dout.astype(BF)
    grad_down = jnp.concatenate(
        [dot_tn(g[:, c * d : (c + 1) * d], dy3).astype(BF) for c in range(cuts)], axis=1
    )
    own_down = scatter_rows(grad_down)
    dg = jnp.concatenate(
        [dot_nt(dy3, wdown[:, c * d : (c + 1) * d]) for c in range(cuts)], axis=1
    )
    du = (dg * slope.astype(F32)).astype(BF)
    grad_up = dot(turned(h3), du).astype(BF)
    own_up = scatter_rows(grad_up)
    dh3 = dot_nt(du, wup)
    back3, gain3, bias3 = norm_back(dh3, unit3, inv3, gains[2])
    dx2 = dout + back3
    dy2 = dx2.astype(BF)
    do2 = dot_nt(dy2, wco).astype(BF)
    dqc, dkv = attn_bwd((qc, 0), kvc, 0, blocks, o2, do2, lse2, slots_used, False)
    dqc = dqc[0]
    dkvc = jnp.concatenate([dkv[0], dkv[1]], axis=1)
    mem_turned = turned(memory_pad)
    grad_mid = jnp.concatenate(
        [
            dot(turned(o2), dy2).astype(BF),
            dot(turned(h2), dqc).astype(BF),
            dot(mem_turned, dkvc).astype(BF),
        ],
        axis=1,
    )
    own_mid = scatter_rows(grad_mid)
    grad_memory = dot_nt(dkvc, wckv)[: memory.shape[0]]
    dh2 = dot_nt(dqc, wcq)
    back2, gain2, bias2 = norm_back(dh2, unit2, inv2, gains[1])
    dx1 = dx2 + back2
    dy1 = dx1.astype(BF)
    do = dot_nt(dy1, wso).astype(BF)
    dqkv = attn_bwd((qkv, 0), qkv, blocks, 2 * blocks, o, do, lse, lengths, True)
    dqkv = jnp.concatenate([dqkv[0], dqkv[1], dqkv[2]], axis=1)
    dh1 = dot_nt(dqkv, wqkv)
    back1, gain1, bias1 = norm_back(dh1, unit1, inv1, gains[0])
    grad_hidden = dx1 + back1
    norm_grads = jnp.stack([gain1, gain2, gain3, bias1, bias2, bias3])
    norm_grads = jnp.pad(norm_grads, ((0, 122), (0, 0))).astype(BF)
    grad_last = jnp.concatenate(
        [
            dot(turned(o), dy1).astype(BF),
            dot(turned(h1), dqkv).astype(BF),
            turned(norm_grads),
        ],
        axis=1,
    )
    own_last = scatter_rows(grad_last)

    own_up = (
        own_up.reshape(rows, cuts, ny, nx, rows).transpose(0, 3, 2, 1, 4).reshape(rows, ff)
    )
    own_down = jnp.concatenate(
        [own_down[:, c * d : (c + 1) * d] for c in range(cuts)], axis=0
    )
    own_norms = own_last[:, 4 * d : 4 * d + 6].T.astype(F32)
    return (
        result,
        grad_hidden,
        grad_memory,
        own_last[:, d : 4 * d].astype(F32),
        own_last[:, :d].astype(F32),
        own_mid[:, d : 2 * d].astype(F32),
        own_mid[:, 2 * d :].astype(F32),
        own_mid[:, :d].astype(F32),
        own_up.astype(F32),
        own_down.astype(F32),
        own_norms[:3],
        own_norms[3:],
    )


CORE, XBIT, YBIT = 1, 2, 4


def swap(a, bit):
    return lax.ppermute(a, ALL, [(i, i ^ bit) for i in range(32)])


def fence(*values):
    return lax.optimization_barrier(values)


def gather_line(w):
    return lax.all_gather(w, "gx", axis=0)


def gather_near(here):
    return here, swap(here, XBIT), swap(here, YBIT)


def gather_far(near):
    return swap(near[2][:2], XBIT), swap(near[1][2:], YBIT)


def swap_cores(pieces):
    return tuple(swap(p, CORE) for p in pieces)


def put_pieces(bits_ref, pieces, out):
    x, y, core = bits_ref[0], bits_ref[1], bits_ref[2]
    for k in range(10):
        at_core = core if k < 5 else 1 - core
        at_x = x if k % 5 in (0, 2) else 1 - x
        at_y = y if k % 5 in (0, 1) else 1 - y
        z0, z1 = {3: (0, 2), 4: (2, 4)}.get(k % 5, (0, 4))
        out[z0:z1, at_y * 4 + at_x * 2 + at_core] = pieces[k][...]


def place_kernel(bits_ref, *refs):
    put_pieces(bits_ref, refs[:10], refs[-1])


def place_dot_kernel(bits_ref, *refs):
    a, w, y = refs[10], refs[11], refs[12]
    put_pieces(bits_ref, refs[:10], w)
    whole = w[...].reshape(a.shape[1], w.shape[3])
    y[...] = dot(a[...], whole).astype(y.dtype)


def piece_specs(pieces, start, block):
    rows = pieces[0].shape[1]
    return [
        (p, pl.BlockSpec((p.shape[0], rows, block), lambda j, _: (0, 0, start // block + j)))
        for p in pieces
    ]


def place_out(rows, width, block):
    return (
        shaped((4, 8, rows, width), BF),
        pl.BlockSpec((4, 8, rows, block), lambda j, _: (0, 0, 0, j)),
    )


def place(pieces, start, width, bits, deps=()):
    rows = pieces[0].shape[1]
    block = min(width, 512)
    out = run(
        place_kernel,
        (width // block,),
        piece_specs(pieces, start, block),
        [place_out(rows, width, block)],
        prefetch=(bits,),
        deps=deps,
        cost=costs(0, 4 * 32 * rows * width),
        name="place",
    )
    return out.reshape(32 * rows, width)


def place_dot(pieces, start, width, bits, a, dtype, deps=()):
    rows, block = pieces[0].shape[1], 512
    whole = pl.BlockSpec(a.shape, lambda j, _: (0, 0))
    w, y = run(
        place_dot_kernel,
        (width // block,),
        piece_specs(pieces, start, block) + [(a, whole)],
        [
            place_out(rows, width, block),
            (
                shaped((a.shape[0], width), dtype),
                pl.BlockSpec((a.shape[0], block), lambda j, _: (0, j)),
            ),
        ],
        prefetch=(bits,),
        deps=deps,
        cost=costs(2 * a.shape[0] * 32 * rows * width, 4 * 32 * rows * width),
        name="place_dot",
    )
    return w.reshape(32 * rows, width), y


def store_rows(value, outs):
    at = 0
    for out in outs:
        out[:, : value.shape[1]] = value[at : at + out.shape[0]]
        at += out.shape[0]


def row_outs(rows, columns, block):
    return [
        (shaped((r, columns), BF), pl.BlockSpec((r, block), lambda j, *_: (0, j)))
        for r in (rows * 3 // 4, rows // 8, rows // 8)
    ]


def half_outs(rows, columns, block):
    return [
        (shaped((r, columns), BF), pl.BlockSpec((r, block), lambda j, *_: (0, j)))
        for r in (rows // 4,) + (rows // 8,) * 6
    ]


def wgrad_kernel(starts, extra, *refs):
    outs = refs[-3:]
    j = pl.program_id(0)
    for s in range(len(starts) - 1):
        a, a2, g, g2 = refs[4 * s : 4 * s + 4]

        @pl.when((j >= starts[s]) & (j < starts[s + 1]))
        def _(a=a, a2=a2, g=g, g2=g2):
            tokens = g.shape[0]
            part = dot(a[...][:, :tokens], g[...]) + dot(a2[...][:, :tokens], g2[...])
            store_rows(part.astype(BF), outs)

    if extra:

        @pl.when(j == starts[-1])
        def _():
            mine, theirs = refs[-5], refs[-4]
            store_rows((mine[...].astype(F32) + theirs[...].astype(F32)).astype(BF), outs)


def wgrad(segments, extra=(), deps=(), block=1024, name="wgrad"):
    starts, ins = [0], []
    for a, a2, g, g2, *span in segments:
        per = g.shape[2] // block
        first, end = span or (0, g.shape[0] * per)
        count, start = end - first, starts[-1]

        def at(j, start=start, count=count, per=per, first=first):
            k = first + jnp.clip(j - start, 0, count - 1)
            return (k // per, 0, k % per)

        whole = pl.BlockSpec(a.shape, lambda j: (0, 0))
        grads = pl.BlockSpec((None, g.shape[1], block), at)
        ins += [(a, whole), (a2, whole), (g, grads), (g2, grads)]
        starts.append(start + count)
    rows = segments[0][0].shape[0]
    columns = starts[-1] * block
    steps = starts[-1]
    if extra:
        ins += [(e, pl.BlockSpec(e.shape, lambda j: (0, 0))) for e in extra]
        columns += extra[0].shape[1]
        steps += 1
    return run(
        functools.partial(wgrad_kernel, tuple(starts), bool(extra)),
        (steps,),
        ins,
        row_outs(rows, columns, block),
        deps=deps,
        cost=costs(2 * rows * 1024 * columns, 4 * 512 * columns + 2 * rows * columns),
        name=name,
    )


def wgrad_down_kernel(bits_ref, *refs):
    blocks, other, dy, dy2 = refs[:4], refs[4:8], refs[8], refs[9]
    mine = jnp.concatenate([r[...].T for r in blocks], axis=0)
    theirs = jnp.concatenate([r[...].T for r in other], axis=0)
    store_rows((dot(mine, dy[...]) + dot(theirs, dy2[...])).astype(BF), refs[10:])


def wgrad_down(bits, g, g_other, dy, dy_other, cuts):
    tokens, d = dy.shape

    def spec(rel, whole):
        def at(b, bits_ref):
            x = bits_ref[0] ^ (rel & 1)
            y = bits_ref[1] ^ (rel >> 1)
            block = b * 4 + y * 2 + x
            return (0, block * 2 + bits_ref[2] if whole else block)

        return pl.BlockSpec((tokens, 128), at)

    rows = pl.BlockSpec((tokens, d), lambda b, _: (0, 0))
    return run(
        wgrad_down_kernel,
        (cuts,),
        [(g, spec(r, True)) for r in range(4)]
        + [(g_other, spec(r, False)) for r in range(4)]
        + [(dy, rows), (dy_other, rows)],
        half_outs(512, cuts * d, d),
        prefetch=(bits,),
        cost=costs(2 * 512 * 1024 * cuts * d, 16 * tokens * d),
        name="wgrad_down",
    )


def up_kernel(bits_ref, *refs):
    h_ref, w_ref, g_ref, slope_ref, send_ref = refs[10:]
    put_pieces(bits_ref, refs[:10], w_ref)
    u = dot(h_ref[...], w_ref[...].reshape(h_ref.shape[1], w_ref.shape[3]))
    cdf = 0.5 * (1.0 + lax.erf(u * (0.5**0.5)))
    g = (u * cdf).astype(BF)
    g_ref[...] = g
    slope_ref[...] = (cdf + u * (jnp.exp(-0.5 * u * u) * 0.3989422804014327)).astype(BF)
    core = bits_ref[2]
    for k in range(0, g.shape[1], 256):
        send_ref[:, k // 2 : k // 2 + 128] = jnp.where(
            core == 0, g[:, k + 128 : k + 256], g[:, k : k + 128]
        )


def feed_up(bits, h, pieces, ff, deps=(), block=512):
    tokens, d = h.shape
    rows = pieces[0].shape[1]
    out = (shaped((tokens, ff), BF), pl.BlockSpec((tokens, block), lambda j, _: (0, j)))
    w, *rest = run(
        up_kernel,
        (ff // block,),
        piece_specs(pieces, 0, block) + [(h, pl.BlockSpec((tokens, d), lambda j, _: (0, 0)))],
        [
            place_out(rows, ff, block),
            out,
            out,
            (
                shaped((tokens, ff // 2), BF),
                pl.BlockSpec((tokens, block // 2), lambda j, _: (0, j)),
            ),
        ],
        prefetch=(bits,),
        deps=deps,
        cost=costs(2 * tokens * d * ff, 4 * d * ff + 4 * tokens * ff, 2 * tokens * ff),
        name="feed_up",
    )
    return w.reshape(d, ff), *rest


def down_kernel(g_ref, w_ref, x_ref, out_ref):
    @pl.when(pl.program_id(0) == 0)
    def _():
        out_ref[...] = x_ref[...]

    out_ref[...] += dot(g_ref[...], w_ref[...])


def feed_down(g, w, x, cuts, deps=()):
    tokens, d = x.shape
    block = d // 2
    whole = pl.BlockSpec((tokens, d), lambda j: (0, 0))
    return run(
        down_kernel,
        (2 * cuts,),
        [
            (g, pl.BlockSpec((tokens, block), lambda j: (0, j))),
            (w, pl.BlockSpec((block, d), lambda j: (j % 2, j // 2))),
            (x, whole),
        ],
        [(shaped((tokens, d), F32), whole)],
        deps=deps,
        cost=costs(2 * tokens * d * d * cuts, 2 * d * d * cuts + 10 * tokens * d),
        name="feed_down",
    )


def norm_back_store(acc, x_ref, gain_ref, res_ref, dx_ref, low_ref, sums_ref):
    gain_grad, bias_grad = 0.0, 0.0
    step = 128
    for r in range(0, x_ref.shape[0], step):
        part = slice(r, r + step)
        x, dh = x_ref[part, :], acc[part, :]
        center = x - jnp.mean(x, -1, keepdims=True)
        inverse = lax.rsqrt(jnp.mean(center * center, -1, keepdims=True) + 1e-05)
        unit = center * inverse
        gain_grad += jnp.sum(dh * unit, axis=0, keepdims=True)
        bias_grad += jnp.sum(dh, axis=0, keepdims=True)
        scaled = dh * gain_ref[...]
        mean_a = jnp.mean(scaled, -1, keepdims=True)
        mean_b = jnp.mean(scaled * unit, -1, keepdims=True)
        dx = res_ref[part, :] + inverse * (scaled - mean_a - unit * mean_b)
        dx_ref[part, :] = dx
        if low_ref is not None:
            low_ref[part, :] = dx.astype(BF)
    sums_ref[0:1, :] = gain_grad
    sums_ref[1:2, :] = bias_grad


def accumulate(acc, part):
    j = pl.program_id(0)

    @pl.when(j == 0)
    def _():
        acc[...] = part

    @pl.when(j > 0)
    def _():
        acc[...] += part


def feed_back_kernel(
    dy_ref, w2_ref, slope_ref, w1_ref, x_ref, gain_ref, res_ref, du_ref, dx_ref, low_ref, sums_ref, acc
):
    du = (dot_nt(dy_ref[...], w2_ref[...]) * slope_ref[...].astype(F32)).astype(BF)
    du_ref[...] = du
    accumulate(acc, dot_nt(du, w1_ref[...]))

    @pl.when(pl.program_id(0) == pl.num_programs(0) - 1)
    def _():
        norm_back_store(acc, x_ref, gain_ref, res_ref, dx_ref, low_ref, sums_ref)


def feed_back(dy, w2, slope, w1, x, gain, res, cuts, deps=()):
    tokens, d = x.shape
    block = d // 2
    ff = w1.shape[1]
    whole = pl.BlockSpec((tokens, d), lambda j: (0, 0), pipeline_mode=pl.Buffered(1))
    part = pl.BlockSpec((tokens, block), lambda j: (0, j))
    return run(
        feed_back_kernel,
        (2 * cuts,),
        [
            (dy, whole),
            (w2, pl.BlockSpec((block, d), lambda j: (j % 2, j // 2))),
            (slope, part),
            (w1, pl.BlockSpec((d, block), lambda j: (0, j))),
            (x, whole),
            (gain, pl.BlockSpec((1, d), lambda j: (0, 0))),
            (res, whole),
        ],
        [
            (shaped((tokens, ff), BF), part),
            (shaped((tokens, d), F32), whole),
            (shaped((tokens, d), BF), whole),
            (shaped((2, d), F32), pl.BlockSpec((2, d), lambda j: (0, 0))),
        ],
        scratch=[pltpu.VMEM((tokens, d), F32)],
        deps=deps,
        cost=costs(4 * tokens * d * ff, 4 * d * ff + 4 * tokens * ff + 16 * tokens * d),
        name="feed_back",
    )


def norm_back_kernel(further, g_ref, w_ref, x_ref, gain_ref, res_ref, *refs):
    w2_ref = refs[0] if further else None
    refs = refs[1:] if further else refs
    dx_ref, sums_ref, acc = refs[0], refs[-2], refs[-1]
    low_ref = refs[1] if further else None
    accumulate(acc, dot_nt(g_ref[...], w_ref[...]))

    @pl.when(pl.program_id(0) == pl.num_programs(0) - 1)
    def _():
        norm_back_store(acc, x_ref, gain_ref, res_ref, dx_ref, low_ref, sums_ref)
        if further:
            refs[2][...] = dot_nt(low_ref[...], w2_ref[...]).astype(BF)


def through_norm(g, w, x, gain, res, further=None, deps=()):
    tokens, d = x.shape
    block = 512
    per = g.shape[2] // block
    count = g.shape[0] * per
    whole = pl.BlockSpec((tokens, d), lambda j: (0, 0), pipeline_mode=pl.Buffered(1))
    whole_weight = pl.BlockSpec((d, d), lambda j: (0, 0), pipeline_mode=pl.Buffered(1))
    outs = [(shaped((tokens, d), F32), whole)]
    if further is not None:
        outs += [(shaped((tokens, d), BF), whole)] * 2
    outs.append((shaped((2, d), F32), pl.BlockSpec((2, d), lambda j: (0, 0))))
    return run(
        functools.partial(norm_back_kernel, further is not None),
        (count,),
        [
            (g, pl.BlockSpec((None, tokens, block), lambda j: (j // per, 0, j % per))),
            (w, pl.BlockSpec((d, block), lambda j: (0, j))),
            (x, whole),
            (gain, pl.BlockSpec((1, d), lambda j: (0, 0))),
            (res, whole),
        ]
        + ([] if further is None else [(further, whole_weight)]),
        outs,
        scratch=[pltpu.VMEM((tokens, d), F32)],
        deps=deps,
        cost=costs(2 * tokens * d * block * count, 2 * d * block * count + 16 * tokens * d),
        name="through_norm",
    )


def scatter_far(grads):
    return swap(grads[1], XBIT), swap(grads[2], YBIT)


def pass_on_kernel(x_ref, y_ref, from_x, from_y, to_x, to_y):
    half = from_x.shape[0]
    to_x[:half] = x_ref[:half]
    to_x[half:] = x_ref[half:] + from_y[...]
    to_y[:half] = y_ref[:half] + from_x[...]
    to_y[half:] = y_ref[half:]


def sum_kernel(own, got_x, got_y, out):
    total = own[...].astype(F32) + got_x[...].astype(F32) + got_y[...].astype(F32)
    out[...] = total.astype(out.dtype)


def column_blocks(columns):
    return columns if columns <= 2304 else next(b for b in (2048, 1024, 640) if columns % b == 0)


def rows_spec(rows, block, at=0):
    return pl.BlockSpec((rows, block), lambda j: (at, j))


def scatter_near(near, far):
    rows, columns = near.shape[0] // 3, near.shape[1]
    block = column_blocks(columns)
    far_spec, out = rows_spec(rows // 2, block), (shaped((rows, columns), BF), rows_spec(rows, block))
    to_x, to_y = run(
        pass_on_kernel,
        (columns // block,),
        [
            (near, rows_spec(rows, block, 1)),
            (near, rows_spec(rows, block, 2)),
            (far[0], far_spec),
            (far[1], far_spec),
        ],
        [out, out],
        cost=costs(rows * columns, 10 * rows * columns),
        name="pass_on",
    )
    return swap(to_x, XBIT), swap(to_y, YBIT)


def add_pairs_kernel(a, b, c, d, first, second):
    first[...] = a[...] + b[...]
    second[...] = c[...] + d[...]


def sum_halves_kernel(own, x_low, x_high, y_low, y_high, out):
    half = x_low.shape[0]
    for k, (x, y) in enumerate(((x_low, y_low), (x_high, y_high))):
        part = own[k * half : (k + 1) * half].astype(F32) + x[...].astype(F32)
        out[k * half : (k + 1) * half] = (part + y[...].astype(F32)).astype(BF)


def early_first(grads):
    _, x_low, _, _, y_high, low, high = grads
    return swap(low, XBIT), swap(high, YBIT), swap(x_low, XBIT), swap(y_high, YBIT)


def early_second(grads, came):
    rows, columns = came[0].shape
    block = column_blocks(columns)
    spec = rows_spec(rows, block)
    out = (shaped((rows, columns), BF), spec)
    to_x, to_y = run(
        add_pairs_kernel,
        (columns // block,),
        [(a, spec) for a in (grads[2], came[1], grads[3], came[0])],
        [out, out],
        cost=costs(2 * rows * columns, 12 * rows * columns),
        name="pass_on",
    )
    return swap(to_x, XBIT), swap(to_y, YBIT)


def early_line(grads, came, last):
    rows, columns = grads[0].shape
    block = column_blocks(columns)
    half = rows_spec(rows // 2, block)
    total = run(
        sum_halves_kernel,
        (columns // block,),
        [(grads[0], rows_spec(rows, block))]
        + [(a, half) for a in (came[2], last[0], last[1], came[3])],
        [(shaped((rows, columns), BF), rows_spec(rows, block))],
        cost=costs(2 * rows * columns, 8 * rows * columns),
        name="plane_sum",
    )
    return lax.psum_scatter(total, "gx", scatter_dimension=0, tiled=True)


def plane_sum(near, got, dtype):
    rows, columns = got[0].shape
    block = column_blocks(columns)
    return run(
        sum_kernel,
        (columns // block,),
        [(a, rows_spec(rows, block)) for a in (near, *got)],
        [(shaped((rows, columns), dtype), rows_spec(rows, block))],
        cost=costs(2 * rows * columns, 8 * rows * columns),
        name="plane_sum",
    )


def scatter_line(near, got):
    total = plane_sum(near, got, BF)
    return lax.psum_scatter(total, "gx", scatter_dimension=0, tiled=True)


def line_kernel(bits_ref, own, got_x, got_y, mine, *sends):
    rows = mine.shape[0]
    for step in range(4):
        at = pl.ds(lax.rem(bits_ref[3] + step, 4) * rows, rows)
        total = own[at, :].astype(F32) + got_x[at, :].astype(F32) + got_y[at, :].astype(F32)
        if step == 0:
            mine[...] = total
        else:
            sends[step - 1][...] = total.astype(BF)


def line_parts(near, got, bits):
    rows, columns = got[0].shape
    spec = pl.BlockSpec((rows, columns), lambda j, _: (0, 0))
    out = pl.BlockSpec((rows // 4, columns), lambda j, _: (0, 0))
    mine, *sends = run(
        line_kernel,
        (1,),
        [(a, spec) for a in (near, *got)],
        [(shaped((rows // 4, columns), F32), out)] + [(shaped((rows // 4, columns), BF), out)] * 3,
        prefetch=(bits,),
        cost=costs(3 * rows * columns, 8 * rows * columns),
        name="line_parts",
    )
    came = [
        lax.ppermute(part, ALL, [(i, (i + 8 * step) % 32) for i in range(32)])
        for step, part in zip((1, 2, 3), sends, strict=True)
    ]
    return [mine] + came


def four_sum(refs, columns):
    total = refs[0][:, columns]
    for ref in refs[1:]:
        total = total + ref[:, columns].astype(F32)
    return total


def finish_first_kernel(*refs):
    d = refs[4].shape[1]
    refs[4][...] = four_sum(refs[:4], slice(0, d))
    refs[5][...] = four_sum(refs[:4], slice(d, 2 * d))


def finish_last_kernel(*refs):
    q, qkv, gains, biases = refs[4:]
    d = q.shape[1]
    qkv[:, :d] = q[...]
    qkv[:, d:] = four_sum(refs[:4], slice(0, 2 * d))
    sums = four_sum(refs[:4], slice(2 * d, 2 * d + 128)).T
    gains[...] = sums[0:3]
    biases[...] = sums[3:6]


def finish(kernel, ins, outs):
    def whole(shape):
        return pl.BlockSpec(shape, lambda j: (0,) * len(shape))

    return run(
        kernel,
        (1,),
        [(a, whole(a.shape)) for a in ins],
        [(shaped(s, F32), whole(s)) for s in outs],
        cost=costs(4 * ins[0].size, 16 * ins[0].size),
        name="finish",
    )


def turn_kernel(select_ref, a_ref, mine, theirs):
    rows = dot_nt(select_ref[...], a_ref[...]).astype(BF)
    half = pl.num_programs(0) // 2

    @pl.when(pl.program_id(0) < half)
    def _():
        mine[...] = rows

    @pl.when(pl.program_id(0) >= half)
    def _():
        theirs[...] = rows


def turn(select, a):
    tokens, d = a.shape
    steps = 4
    block, half = d // steps, steps // 2
    out = shaped((d // 2, tokens), BF)
    return run(
        turn_kernel,
        (steps,),
        [
            (select, pl.BlockSpec((block, d), lambda j: (j, 0))),
            (a, pl.BlockSpec((tokens, d), lambda j: (0, 0))),
        ],
        [
            (out, pl.BlockSpec((block, tokens), lambda j: (jnp.minimum(j, half - 1), 0))),
            (out, pl.BlockSpec((block, tokens), lambda j: (jnp.maximum(j - half, 0), 0))),
        ],
        cost=costs(2 * d * d * tokens, 2 * d * d + 4 * d * tokens),
        name="turn",
    )


def hidden_order_kernel(to_hidden, rows, cuts, src, out):
    lines = 4
    width = lines * cuts * rows
    at = lax.broadcasted_iota(jnp.int32, (width, width), 0)
    to = lax.broadcasted_iota(jnp.int32, (width, width), 1)
    first, second = (lines, cuts) if to_hidden else (cuts, lines)
    moved = (at // rows % second * first + at // (rows * second)) * rows + at % rows
    swap_two = (moved == to).astype(F32).astype(BF)
    for place_at in range(8):
        if to_hidden:
            step, parts, wide = cuts * rows, lines, cuts * rows
        else:
            step, parts, wide = lines * rows, cuts, lines * rows
        pieces = [
            src[:, (k * 8 + place_at) * step : (k * 8 + place_at) * step + wide]
            for k in range(parts)
        ]
        done = dot(jnp.concatenate(pieces, axis=1), swap_two)
        out_step = lines * rows if to_hidden else cuts * rows
        for k in range(cuts if to_hidden else lines):
            at_column = (k * 8 + place_at) * out_step
            out[:, at_column : at_column + out_step] = done[
                :, k * out_step : (k + 1) * out_step
            ].astype(out.dtype)


def hidden_order(a, to_hidden, cuts, dtype):
    rows, ff = a.shape
    whole = pl.BlockSpec((rows, ff), lambda j: (0, 0))
    return run(
        functools.partial(hidden_order_kernel, to_hidden, ff // 32 // cuts, cuts),
        (1,),
        [(a, whole)],
        [(shaped((rows, ff), dtype), whole)],
        cost=costs(2 * rows * ff * 512, 6 * rows * ff),
        name="hidden_order",
    )


def memory_grad_kernel(g_ref, w_ref, out_ref):
    part = dot_nt(g_ref[...], w_ref[...])[: out_ref.shape[0]]

    @pl.when(pl.program_id(0) == 0)
    def _():
        out_ref[...] = part

    @pl.when(pl.program_id(0) > 0)
    def _():
        out_ref[...] += part


def memory_grad(g, w, rows):
    _, padded, d = g.shape
    block = d // 2
    return run(
        memory_grad_kernel,
        (4,),
        [
            (g, pl.BlockSpec((None, padded, block), lambda j: (j // 2, 0, j % 2))),
            (w, pl.BlockSpec((d, block), lambda j: (0, j))),
        ],
        [(shaped((rows, d), F32), pl.BlockSpec((rows, d), lambda j: (0, 0)))],
        cost=costs(4 * padded * d * d, 8 * d * d + 4 * rows * d),
        name="memory_grad",
    )


def shards_plane(
    hidden,
    memory,
    lengths,
    page_class,
    cotangent,
    w_self_qkv,
    w_self_out,
    w_cross_q,
    w_cross_kv,
    w_cross_out,
    w_fc1,
    w_fc2,
    norm_gains,
    norm_biases,
):
    tokens, d = hidden.shape
    rows, ff = w_fc1.shape
    cuts = w_fc2.shape[0] // rows
    mem_rows = -(-memory.shape[0] // 16) * 16
    slots_used = jnp.where(page_class == 0, MEM_BIG, MEM_BIG // 4).astype(jnp.int32)
    along = lax.axis_index("gy")
    x_at, y_at, core = (along // 2) % 2, along // 4, along % 2
    z_at = lax.axis_index("gx")
    bits = jnp.stack([x_at, y_at, core, z_at]).astype(jnp.int32)

    norm_cols = jnp.concatenate([norm_gains, norm_biases], axis=0).T
    norm_cols = jnp.pad(norm_cols, ((0, 0), (0, 128 - norm_cols.shape[1])))
    up_local = hidden_order(w_fc1, True, cuts, BF)
    down_local = jnp.concatenate(
        [w_fc2[c * rows : (c + 1) * rows] for c in range(cuts)], axis=1
    )
    place_at = jnp.arange(d)
    r = place_at % rows
    z = (place_at // rows) % 4
    rel = (place_at // (4 * rows)) % 4
    source_core = core ^ (place_at // (16 * rows))
    device = z * 8 + (y_at ^ (rel // 2)) * 4 + (x_at ^ (rel % 2)) * 2 + source_core
    select = ((device * rows + r)[:, None] == place_at[None, :]).astype(BF)

    def turned(a):
        mine, theirs = turn(select, a)
        return mine, swap(theirs, CORE)

    pack1 = jnp.concatenate([w_self_qkv, norm_cols], axis=1)
    pack2 = jnp.concatenate([w_cross_kv, w_self_out, w_cross_q, w_cross_out], axis=1)
    blocks = d // PAIR
    memory_pad = jnp.pad(memory, ((0, mem_rows - memory.shape[0]), (0, 0)))

    line1, pack2, memory_pad, hidden = fence(gather_line(pack1), pack2, memory_pad, hidden)

    line2 = gather_line(pack2)
    near1 = gather_near(line1)
    mem_t = turned(jnp.pad(memory_pad, ((0, -mem_rows % 128), (0, 0))))
    unit1, _ = norm_parts(hidden)
    near1, mem_t, unit1 = fence(near1, mem_t, unit1)

    near1, far1, cores1, line2, pack3 = fence(
        near1, gather_far(near1), swap_cores(near1), line2, up_local
    )

    line3 = gather_line(pack3)
    near2 = gather_near(line2)
    first = near1 + far1 + cores1 + swap_cores(far1)
    norms = place(first, 3 * d, 128, bits)[:, :6].T.astype(F32)
    gains, biases = norms[:3], norms[3:]
    h1 = (unit1 * gains[0] + biases[0]).astype(BF)
    wqkv, qkv = place_dot(first, 0, 3 * d, bits, h1, BF)
    o, lse = attn_fwd((qkv, 0), qkv, blocks, 2 * blocks, lengths, True)
    near2, o, h1, gains, biases = fence(near2, o, h1, gains, biases)

    far2, cores2 = gather_far(near2), swap_cores(near2)
    h1_turn, o_turn = turn(select, h1), turn(select, o)
    near2, far2, cores2, h1_turn, o_turn, o, line3, pack4 = fence(
        near2, far2, cores2, h1_turn, o_turn, o, line3, down_local
    )

    wdown = lax.all_gather(pack4, ("gy", "gx"), axis=0, tiled=True)
    near3 = gather_near(line3)
    second = near2 + far2 + cores2 + swap_cores(far2)
    wso, y1 = place_dot(second, 2 * d, d, bits, o, F32)
    x1 = hidden + y1
    unit2, _ = norm_parts(x1)
    h2 = (unit2 * gains[1] + biases[1]).astype(BF)
    wcq, qc = place_dot(second, 3 * d, d, bits, h2, BF)
    wckv, kvc = place_dot(second, 0, 2 * d, bits, memory_pad, BF)
    h1_t, o_t = ((mine, swap(theirs, CORE)) for mine, theirs in (h1_turn, o_turn))
    near3, second, qc, kvc, h2, x1, h1_t, o_t = fence(
        near3, second, qc, kvc, h2, x1, h1_t, o_t
    )

    far3, cores3 = gather_far(near3), swap_cores(near3)
    o2, lse2 = attn_fwd((qc, 0), kvc, 0, blocks, slots_used, False)
    near3, cores3, o2, h2, cotangent = fence(near3, cores3, o2, h2, cotangent)

    wco, y2 = place_dot(second, 4 * d, d, bits, o2, F32)
    x2 = x1 + y2
    unit3, _ = norm_parts(x2)
    h3 = (unit3 * gains[2] + biases[2]).astype(BF)
    valid = (jnp.arange(tokens) < lengths[0])[:, None].astype(F32)
    dout = cotangent * valid
    dy3 = dout.astype(BF)
    dy3_other = swap(dy3, CORE)
    far3, h3, x2, o2, dout, dy3, dy3_other = fence(far3, h3, x2, o2, dout, dy3, dy3_other)

    third = near3 + far3 + cores3 + swap_cores(far3)
    wup, g, slope, g_send = feed_up(bits, h3, third, ff)
    wup, g, slope, g_send, h3, o2 = fence(wup, g, slope, g_send, h3, o2)

    h2_t, h3_t, o2_t = turned(h2), turned(h3), turned(o2)
    g_other, h2_t, h3_t, o2_t, g = fence(swap(g_send, CORE), h2_t, h3_t, o2_t, g)

    grad_down = wgrad_down(bits, g, g_other, dy3, dy3_other, cuts)
    grad_down, dy3, slope, wdown = fence(grad_down, dy3, slope, wdown)

    du, dx2, dy2, sums3 = feed_back(dy3, wdown, slope, wup, x2, gains[2:3], dout, cuts)
    far1, du, dx2, dy2, g = fence(early_first(grad_down), du, dx2, dy2, g)

    got1 = early_second(grad_down, far1)
    do2 = dot_nt(dy2, wco).astype(BF)
    du_other, do2, du = fence(swap(du, CORE), do2, du)

    grad_up = wgrad([h3_t + (du[None], du_other[None])])
    grad_up, do2, dy2 = fence(grad_up, do2, dy2)

    dqc, dkvc = attn_bwd((qc, 0), kvc, 0, blocks, o2, do2, lse2, slots_used, False)
    far2, got1, dqc, dkvc, dy2_other, dx2 = fence(
        scatter_far(grad_up), got1, dqc, dkvc, swap(dy2, CORE), dx2
    )

    own_down = early_line(grad_down, far1, got1)
    got2 = scatter_near(grad_up[0], far2)
    dx1, dy1, do, sums2 = through_norm(dqc, wcq, x1, gains[1:2], dx2, further=wso)
    dqc_other, dkvc_other, dx1, dy1, do, dqc, dkvc = fence(
        swap(dqc, CORE), swap(dkvc, CORE), dx1, dy1, do, dqc, dkvc
    )

    grad_mid = wgrad(
        [
            o2_t + (dy2[None], dy2_other[None]),
            h2_t + (dqc, dqc_other),
            mem_t + (dkvc, dkvc_other),
        ],
        name="wgrad_mid",
    )
    grad_mid, do, dy1 = fence(grad_mid, do, dy1)

    dqkv = attn_bwd((qkv, 0), qkv, blocks, 2 * blocks, o, do, lse, lengths, True)
    far3, dy1_other, dqkv, got2, dx1 = fence(
        scatter_far(grad_mid), swap(dy1, CORE), dqkv, got2, dx1
    )

    own_up = scatter_line(grad_up[0], got2)
    got3 = scatter_near(grad_mid[0], far3)
    grad_hidden, sums1 = through_norm(dqkv, wqkv, hidden, gains[0:1], dx1)
    sums = jnp.stack([sums1, sums2, sums3], axis=1).reshape(6, d)
    sums = jnp.pad(sums, ((0, 122), (0, 0))).astype(BF)
    dqkv_other, grad_hidden, sums_t = fence(swap(dqkv, CORE), grad_hidden, turned(sums))

    grad_a = wgrad(
        [o_t + (dy1[None], dy1_other[None]), h1_t + (dqkv, dqkv_other, 0, 1)]
    )
    grad_a, dqkv, dqkv_other, sums_t = fence(grad_a, dqkv, dqkv_other, sums_t)

    grad_b = wgrad([h1_t + (dqkv, dqkv_other, 1, 3)], extra=sums_t)
    far_a, grad_b, got3, dkvc, own_down, g = fence(
        scatter_far(grad_a), grad_b, got3, dkvc, own_down, g
    )

    got_a = scatter_near(grad_a[0], far_a)
    own_mid = scatter_line(grad_mid[0], got3)
    result = feed_down(g, wdown, x2, cuts)
    far_b, got_a, result, own_up, dkvc = fence(
        scatter_far(grad_b), got_a, result, own_up, dkvc
    )

    got_b = scatter_near(grad_b[0], far_b)
    came_a = line_parts(grad_a[0], got_a, bits)
    own_up = hidden_order(own_up, False, cuts, F32)
    grad_memory = memory_grad(dkvc, wckv, memory.shape[0])
    got_b, own_up, grad_memory = fence(got_b, own_up, grad_memory)

    came_b = line_parts(grad_b[0], got_b, bits)
    own_mid = own_mid.astype(F32)
    mids = [own_mid[:, k * d : k * d + w * d] for k, w in ((0, 1), (1, 1), (2, 2))]
    grad_so, grad_q = finish(finish_first_kernel, came_a, [(rows, d)] * 2)
    came_b[1], mids, grad_so, grad_q = fence(came_b[1], mids, grad_so, grad_q)

    own_qkv, own_gains, own_biases = finish(
        finish_last_kernel, came_b + [grad_q], [(rows, 3 * d), (3, rows), (3, rows)]
    )
    own_down = jnp.concatenate(
        [own_down[:, c * d : (c + 1) * d] for c in range(cuts)], axis=0
    )
    return (
        result,
        grad_hidden,
        grad_memory,
        own_qkv,
        grad_so,
        mids[1],
        mids[2],
        mids[0],
        own_up,
        own_down.astype(F32),
        own_gains,
        own_biases,
    )


def solution(mesh):
    row = P(ALL, None)
    col = P(None, ALL)
    nx, ny = mesh.shape["gx"], mesh.shape["gy"]
    body = shards_plane if (nx, ny) == (4, 8) else functools.partial(shards_any, nx=nx, ny=ny)
    return jax.shard_map(
        body,
        mesh=mesh,
        in_specs=(row, row, P(ALL), P(ALL), row) + (row,) * 7 + (col, col),
        out_specs=(row,) * 10 + (col, col),
        check_vma=False,
    )
```

```python
import functools

import jax
import jax.numpy as jnp
from jax import lax
from jax.experimental import pallas as pl
from jax.experimental.pallas import tpu as pltpu
from jax.sharding import PartitionSpec as P

HEADS = 16
MEM_BIG = 588
ALL = ("gx", "gy")
BF = jnp.bfloat16
F32 = jnp.float32
PAIR = 128
LIMITS = {'feed_back': 50, 'pass_on': 8, 'plane_sum': 8, 'place': 8, 'hidden_order': 8, 'memory_grad': 12, 'turn': 12, 'wgrad': 44, 'wgrad_down': 44, 'wgrad_mid': 44, 'finish': 12, 'line_parts': 12, 'wgrad_a': 44}
FAR_OUTS = {'wgrad': (0, 1, 2), 'wgrad_down': (0, 1, 2, 3, 4, 5, 6), 'feed_up': (0, 1, 2), 'place_dot': (0,), 'feed_back': (0, 1), 'wgrad_mid': (0, 1, 2), 'wgrad_a': (0, 1, 2)}
FAR_INS = {'pass_on': (0, 1, 2, 3), 'plane_sum': (0, 1, 2), 'wgrad_mid': (0, 1, 2, 3, 4, 5, 6, 7, 8, 9, 10, 11), 'attn_bwd': (0, 1, 2, 3, 4), 'wgrad_a': (0, 1, 2, 3, 4, 5, 6, 7)}


def dot(a, b):
    return jnp.dot(a, b, preferred_element_type=F32)


def dot_nt(a, b):
    return lax.dot_general(a, b, (((1,), (1,)), ((), ())), preferred_element_type=F32)


def dot_tn(a, b):
    return lax.dot_general(a, b, (((0,), (0,)), ((), ())), preferred_element_type=F32)


def run(
    kernel, grid, ins, outs, prefetch=(), scratch=(), deps=(), cost=None, name=None
):
    count = len(prefetch) + len(ins)

    def body(*refs):
        return kernel(*refs[:count], *refs[count + len(deps) :])

    result = pl.pallas_call(
        body,
        grid_spec=pltpu.PrefetchScalarGridSpec(
            num_scalar_prefetch=len(prefetch),
            grid=grid,
            in_specs=[spec for _, spec in ins] + [pl.BlockSpec(memory_space=pl.ANY)] * len(deps),
            out_specs=[spec for _, spec in outs],
            scratch_shapes=scratch,
        ),
        out_shape=[
            pltpu.HBM(shape.shape, shape.dtype) if k in FAR_OUTS.get(name, ()) else shape
            for k, (shape, _) in enumerate(outs)
        ],
        compiler_params=pltpu.CompilerParams(
            dimension_semantics=("arbitrary",) * len(grid), vmem_limit_bytes=LIMITS.get(name, 30) * 1024 * 1024
        ),
        cost_estimate=cost,
        name=name,
    )(
        *prefetch,
        *[
            pltpu.with_memory_space_constraint(a, pltpu.HBM)
            if k in FAR_INS.get(name, ())
            else a
            for k, (a, _) in enumerate(ins)
        ],
        *deps,
    )
    return result if len(outs) > 1 else result[0]


def costs(flops, nbytes, transcendentals=0):
    return pl.CostEstimate(
        flops=flops, bytes_accessed=nbytes, transcendentals=transcendentals
    )


def shaped(shape, dtype):
    return jax.ShapeDtypeStruct(shape, dtype)


def allowed_t(key_count, q0, q1, limit, causal):
    key_at = lax.broadcasted_iota(jnp.int32, (key_count, q1 - q0), 0)
    ok = key_at < limit
    if causal:
        query_at = lax.broadcasted_iota(jnp.int32, (key_count, q1 - q0), 1) + q0
        ok = ok & (key_at <= query_at)
    return ok


def half_mask(width, half):
    lane = lax.broadcasted_iota(jnp.int32, (1, width), 1)
    return ((lane // (width // 2)) == half).astype(F32).astype(BF)


def attn_fwd_kernel(spans, causal, limit_ref, q_ref, k_ref, v_ref, o_ref, lse_ref):
    width = q_ref.shape[1]
    half = width // 2
    limit = limit_ref[0]
    scale = BF(half**-0.5)
    v_t = v_ref[...].T
    work = [(q0, q1, keys, h) for q0, q1, keys in spans for h in range(2)]
    scores = [
        dot_nt(k_ref[:keys, :], q_ref[q0:q1, :] * scale * half_mask(width, h))
        for q0, q1, keys, h in work
    ]
    outs = {}
    for (q0, q1, keys, h), s in zip(work, scores, strict=True):
        s = jnp.where(allowed_t(keys, q0, q1, limit, causal), s, -1e30)
        top = jnp.max(s, axis=0, keepdims=True)
        e = jnp.exp(s - top)
        total = jnp.sum(e, axis=0, keepdims=True)
        outs[q0, h] = dot(v_t[h * half : (h + 1) * half, :keys], e.astype(BF)) / total
        lse_ref[0, h : h + 1, q0:q1] = top + jnp.log(total)
    for q0, q1, _ in spans:
        o_ref[q0:q1, :] = jnp.concatenate([outs[q0, 0], outs[q0, 1]], axis=0).T.astype(BF)


def attn_bwd_kernel(
    spans, causal, limit_ref, q_ref, k_ref, v_ref, o_ref, do_ref, lse_ref, *outs_ref
):
    dq_ref = outs_ref[0].at[0]
    dk_ref, dv_ref = (outs_ref[-1].at[k - 2 + outs_ref[-1].shape[0]] for k in range(2))
    width = q_ref.shape[1]
    half = width // 2
    limit = limit_ref[0]
    scale = BF(half**-0.5)
    k_t = k_ref[...].T * scale
    total_k = k_ref.shape[0]
    masks = [half_mask(width, h) for h in range(2)]
    dk = jnp.zeros((total_k, width), F32)
    dv = jnp.zeros((total_k, width), F32)
    for q0, q1, keys in spans:
        query = q_ref[q0:q1, :] * scale
        grad_o = do_ref[q0:q1, :]
        ok = allowed_t(keys, q0, q1, limit, causal)
        both = (grad_o.astype(F32) * o_ref[q0:q1, :].astype(F32)).T
        query_h = [query * m for m in masks]
        grad_h = [grad_o * m for m in masks]
        scores = [dot_nt(k_ref[:keys, :], a) for a in query_h]
        dps = [dot_nt(v_ref[:keys, :], a) for a in grad_h]
        probs, dss = [], []
        for h in range(2):
            inner = jnp.sum(both[h * half : (h + 1) * half], axis=0, keepdims=True)
            p = jnp.where(ok, jnp.exp(scores[h] - lse_ref[0, h : h + 1, q0:q1]), 0.0)
            probs.append(p.astype(BF))
            dss.append((p * (dps[h] - inner)).astype(BF))
        dv_part = dot(probs[0], grad_h[0]) + dot(probs[1], grad_h[1])
        dk_part = dot(dss[0], query_h[0]) + dot(dss[1], query_h[1])
        outs = [dot(k_t[h * half : (h + 1) * half, :keys], dss[h]) for h in range(2)]
        dq_ref[q0:q1, :] = jnp.concatenate(outs, axis=0).T.astype(BF)
        if keys < total_k:
            pad = jnp.zeros((total_k - keys, width), F32)
            dk_part = jnp.concatenate([dk_part, pad], axis=0)
            dv_part = jnp.concatenate([dv_part, pad], axis=0)
        dk += dk_part
        dv += dv_part
    dk_ref[...] = dk.astype(BF)
    dv_ref[...] = dv.astype(BF)


def make_spans(queries, keys, causal):
    step = 256
    return tuple(
        (q, q + step, min(q + step, keys) if causal else keys) for q in range(0, queries, step)
    )


def attn_fwd(q, kv, k_at, v_at, limit, causal, deps=()):
    q_arr, q_at = q
    queries, keys = q_arr.shape[0], kv.shape[0]
    pairs = HEADS // 2
    return run(
        functools.partial(attn_fwd_kernel, make_spans(queries, keys, causal), causal),
        (pairs,),
        [
            (q_arr, pl.BlockSpec((queries, PAIR), lambda p, _: (0, q_at + p))),
            (kv, pl.BlockSpec((keys, PAIR), lambda p, _: (0, k_at + p))),
            (kv, pl.BlockSpec((keys, PAIR), lambda p, _: (0, v_at + p))),
        ],
        [
            (
                shaped((queries, pairs * PAIR), BF),
                pl.BlockSpec((queries, PAIR), lambda p, _: (0, p)),
            ),
            (
                shaped((pairs, 2, queries), F32),
                pl.BlockSpec((1, 2, queries), lambda p, _: (p, 0, 0)),
            ),
        ],
        prefetch=(limit,),
        deps=deps,
        cost=costs(16 * queries * keys * 1024, 8 * queries * 1024, 16 * queries * keys),
        name="attn_fwd",
    )


def attn_bwd(q, kv, k_at, v_at, o, do, lse, limit, causal, deps=()):
    q_arr, q_at = q
    queries, keys = q_arr.shape[0], kv.shape[0]
    pairs = HEADS // 2
    q_block = pl.BlockSpec((queries, PAIR), lambda p, _: (0, p))

    def stacked(count, rows):
        return (
            shaped((count, rows, pairs * PAIR), BF),
            pl.BlockSpec((count, rows, PAIR), lambda p, _: (0, 0, p)),
        )

    return run(
        functools.partial(attn_bwd_kernel, make_spans(queries, keys, causal), causal),
        (pairs,),
        [
            (q_arr, pl.BlockSpec((queries, PAIR), lambda p, _: (0, q_at + p))),
            (kv, pl.BlockSpec((keys, PAIR), lambda p, _: (0, k_at + p))),
            (kv, pl.BlockSpec((keys, PAIR), lambda p, _: (0, v_at + p))),
            (o, q_block),
            (do, q_block),
            (lse, pl.BlockSpec((1, 2, queries), lambda p, _: (p, 0, 0))),
        ],
        [stacked(3, queries)] if queries == keys else [stacked(1, queries), stacked(2, keys)],
        prefetch=(limit,),
        deps=deps,
        cost=costs(16 * queries * keys * 2560, 16 * queries * 1024, 16 * queries * keys),
        name="attn_bwd",
    )


def norm_parts(v):
    center = v - jnp.mean(v, -1, keepdims=True)
    inverse = lax.rsqrt(jnp.mean(center * center, -1, keepdims=True) + 1e-05)
    return center * inverse, inverse


def norm_back(grad, unit, inverse, gain):
    gain_grad = jnp.sum(grad * unit, axis=0)
    bias_grad = jnp.sum(grad, axis=0)
    scaled = grad * gain
    mean_a = jnp.mean(scaled, -1, keepdims=True)
    mean_b = jnp.mean(scaled * unit, -1, keepdims=True)
    return inverse * (scaled - mean_a - unit * mean_b), gain_grad, bias_grad


def gather_rows(w):
    return lax.all_gather(w, ALL, axis=0, tiled=True)


def scatter_rows(g):
    part = lax.psum_scatter(g, "gy", scatter_dimension=0, tiled=True)
    return lax.psum_scatter(part, "gx", scatter_dimension=0, tiled=True)


def shards_any(
    hidden,
    memory,
    lengths,
    page_class,
    cotangent,
    w_self_qkv,
    w_self_out,
    w_cross_q,
    w_cross_kv,
    w_cross_out,
    w_fc1,
    w_fc2,
    norm_gains,
    norm_biases,
    *,
    nx,
    ny,
):
    n = nx * ny
    tokens, d = hidden.shape
    rows = w_fc1.shape[0]
    ff = w_fc1.shape[1]
    cuts = w_fc2.shape[0] // rows
    mem_rows = -(-memory.shape[0] // 16) * 16
    slots_used = jnp.where(page_class == 0, MEM_BIG, MEM_BIG // 4).astype(jnp.int32)

    norm_cols = jnp.concatenate([norm_gains, norm_biases], axis=0).T
    norm_cols = jnp.pad(norm_cols, ((0, 0), (0, 128 - norm_cols.shape[1])))
    first = jnp.concatenate([w_self_qkv, w_cross_kv, norm_cols], axis=1)
    second = jnp.concatenate([w_self_out, w_cross_q, w_cross_out], axis=1)
    up_local = (
        w_fc1.reshape(rows, nx, ny, cuts, rows).transpose(0, 3, 2, 1, 4).reshape(rows, ff)
    )
    down_local = jnp.concatenate(
        [w_fc2[c * rows : (c + 1) * rows] for c in range(cuts)], axis=1
    )
    w_first = gather_rows(first)
    w_second = gather_rows(second)
    wup = gather_rows(up_local)
    wdown = lax.all_gather(down_local, ("gy", "gx"), axis=0, tiled=True)

    wqkv = w_first[:, : 3 * d]
    wckv = w_first[:, 3 * d : 5 * d]
    norms = w_first[:, 5 * d : 5 * d + 6].T.astype(F32)
    gains, biases = norms[:3], norms[3:]
    wso, wcq, wco = w_second[:, :d], w_second[:, d : 2 * d], w_second[:, 2 * d :]

    place = jnp.arange(d)
    source = place % rows + ((place // rows) % nx * ny + place // (rows * nx)) * rows
    select = (source[:, None] == place[None, :]).astype(BF)

    def turned(a):
        return dot_nt(select, a).astype(BF)

    unit1, inv1 = norm_parts(hidden)
    h1 = (unit1 * gains[0] + biases[0]).astype(BF)
    qkv = dot(h1, wqkv).astype(BF)
    blocks = d // PAIR
    o, lse = attn_fwd((qkv, 0), qkv, blocks, 2 * blocks, lengths, True)
    x1 = hidden + dot(o, wso)
    unit2, inv2 = norm_parts(x1)
    h2 = (unit2 * gains[1] + biases[1]).astype(BF)
    qc = dot(h2, wcq).astype(BF)
    memory_pad = jnp.pad(memory, ((0, mem_rows - memory.shape[0]), (0, 0)))
    kvc = dot(memory_pad, wckv).astype(BF)
    o2, lse2 = attn_fwd((qc, 0), kvc, 0, blocks, slots_used, False)
    x2 = x1 + dot(o2, wco)
    unit3, inv3 = norm_parts(x2)
    h3 = (unit3 * gains[2] + biases[2]).astype(BF)
    u = dot(h3, wup)
    cdf = 0.5 * (1.0 + lax.erf(u * (0.5**0.5)))
    g = (u * cdf).astype(BF)
    slope = (cdf + u * (jnp.exp(-0.5 * u * u) * 0.3989422804014327)).astype(BF)
    result = x2
    for c in range(cuts):
        result = result + dot(g[:, c * d : (c + 1) * d], wdown[:, c * d : (c + 1) * d])

    valid = (jnp.arange(tokens) < lengths[0])[:, None].astype(F32)
    dout = cotangent * valid
    dy3 = dout.astype(BF)
    grad_down = jnp.concatenate(
        [dot_tn(g[:, c * d : (c + 1) * d], dy3).astype(BF) for c in range(cuts)], axis=1
    )
    own_down = scatter_rows(grad_down)
    dg = jnp.concatenate(
        [dot_nt(dy3, wdown[:, c * d : (c + 1) * d]) for c in range(cuts)], axis=1
    )
    du = (dg * slope.astype(F32)).astype(BF)
    grad_up = dot(turned(h3), du).astype(BF)
    own_up = scatter_rows(grad_up)
    dh3 = dot_nt(du, wup)
    back3, gain3, bias3 = norm_back(dh3, unit3, inv3, gains[2])
    dx2 = dout + back3
    dy2 = dx2.astype(BF)
    do2 = dot_nt(dy2, wco).astype(BF)
    dqc, dkv = attn_bwd((qc, 0), kvc, 0, blocks, o2, do2, lse2, slots_used, False)
    dqc = dqc[0]
    dkvc = jnp.concatenate([dkv[0], dkv[1]], axis=1)
    mem_turned = turned(memory_pad)
    grad_mid = jnp.concatenate(
        [
            dot(turned(o2), dy2).astype(BF),
            dot(turned(h2), dqc).astype(BF),
            dot(mem_turned, dkvc).astype(BF),
        ],
        axis=1,
    )
    own_mid = scatter_rows(grad_mid)
    grad_memory = dot_nt(dkvc, wckv)[: memory.shape[0]]
    dh2 = dot_nt(dqc, wcq)
    back2, gain2, bias2 = norm_back(dh2, unit2, inv2, gains[1])
    dx1 = dx2 + back2
    dy1 = dx1.astype(BF)
    do = dot_nt(dy1, wso).astype(BF)
    dqkv = attn_bwd((qkv, 0), qkv, blocks, 2 * blocks, o, do, lse, lengths, True)
    dqkv = jnp.concatenate([dqkv[0], dqkv[1], dqkv[2]], axis=1)
    dh1 = dot_nt(dqkv, wqkv)
    back1, gain1, bias1 = norm_back(dh1, unit1, inv1, gains[0])
    grad_hidden = dx1 + back1
    norm_grads = jnp.stack([gain1, gain2, gain3, bias1, bias2, bias3])
    norm_grads = jnp.pad(norm_grads, ((0, 122), (0, 0))).astype(BF)
    grad_last = jnp.concatenate(
        [
            dot(turned(o), dy1).astype(BF),
            dot(turned(h1), dqkv).astype(BF),
            turned(norm_grads),
        ],
        axis=1,
    )
    own_last = scatter_rows(grad_last)

    own_up = (
        own_up.reshape(rows, cuts, ny, nx, rows).transpose(0, 3, 2, 1, 4).reshape(rows, ff)
    )
    own_down = jnp.concatenate(
        [own_down[:, c * d : (c + 1) * d] for c in range(cuts)], axis=0
    )
    own_norms = own_last[:, 4 * d : 4 * d + 6].T.astype(F32)
    return (
        result,
        grad_hidden,
        grad_memory,
        own_last[:, d : 4 * d].astype(F32),
        own_last[:, :d].astype(F32),
        own_mid[:, d : 2 * d].astype(F32),
        own_mid[:, 2 * d :].astype(F32),
        own_mid[:, :d].astype(F32),
        own_up.astype(F32),
        own_down.astype(F32),
        own_norms[:3],
        own_norms[3:],
    )


CORE, XBIT, YBIT = 1, 2, 4


def swap(a, bit):
    return lax.ppermute(a, ALL, [(i, i ^ bit) for i in range(32)])


def fence(*values):
    return lax.optimization_barrier(values)


def gather_line(w):
    return lax.all_gather(w, "gx", axis=0)


def gather_near(here):
    return here, swap(here, XBIT), swap(here, YBIT)


def gather_far(near):
    return swap(near[2][:2], XBIT), swap(near[1][2:], YBIT)


def swap_cores(pieces):
    return tuple(swap(p, CORE) for p in pieces)


def put_pieces(bits_ref, pieces, out):
    x, y, core = bits_ref[0], bits_ref[1], bits_ref[2]
    for k in range(10):
        at_core = core if k < 5 else 1 - core
        at_x = x if k % 5 in (0, 2) else 1 - x
        at_y = y if k % 5 in (0, 1) else 1 - y
        z0, z1 = {3: (0, 2), 4: (2, 4)}.get(k % 5, (0, 4))
        out[z0:z1, at_y * 4 + at_x * 2 + at_core] = pieces[k][...]


def place_kernel(bits_ref, *refs):
    put_pieces(bits_ref, refs[:10], refs[-1])


def place_dot_kernel(bits_ref, *refs):
    a, w, y = refs[10], refs[11], refs[12]
    put_pieces(bits_ref, refs[:10], w)
    whole = w[...].reshape(a.shape[1], w.shape[3])
    y[...] = dot(a[...], whole).astype(y.dtype)


def piece_specs(pieces, start, block):
    rows = pieces[0].shape[1]
    return [
        (p, pl.BlockSpec((p.shape[0], rows, block), lambda j, _: (0, 0, start // block + j)))
        for p in pieces
    ]


def place_out(rows, width, block):
    return (
        shaped((4, 8, rows, width), BF),
        pl.BlockSpec((4, 8, rows, block), lambda j, _: (0, 0, 0, j)),
    )


def place(pieces, start, width, bits, deps=()):
    rows = pieces[0].shape[1]
    block = min(width, 512)
    out = run(
        place_kernel,
        (width // block,),
        piece_specs(pieces, start, block),
        [place_out(rows, width, block)],
        prefetch=(bits,),
        deps=deps,
        cost=costs(0, 4 * 32 * rows * width),
        name="place",
    )
    return out.reshape(32 * rows, width)


def place_dot(pieces, start, width, bits, a, dtype, deps=()):
    rows, block = pieces[0].shape[1], 512
    whole = pl.BlockSpec(a.shape, lambda j, _: (0, 0))
    w, y = run(
        place_dot_kernel,
        (width // block,),
        piece_specs(pieces, start, block) + [(a, whole)],
        [
            place_out(rows, width, block),
            (
                shaped((a.shape[0], width), dtype),
                pl.BlockSpec((a.shape[0], block), lambda j, _: (0, j)),
            ),
        ],
        prefetch=(bits,),
        deps=deps,
        cost=costs(2 * a.shape[0] * 32 * rows * width, 4 * 32 * rows * width),
        name="place_dot",
    )
    return w.reshape(32 * rows, width), y


def store_rows(value, outs):
    at = 0
    for out in outs:
        out[:, : value.shape[1]] = value[at : at + out.shape[0]]
        at += out.shape[0]


def row_outs(rows, columns, block):
    return [
        (shaped((r, columns), BF), pl.BlockSpec((r, block), lambda j, *_: (0, j)))
        for r in (rows * 3 // 4, rows // 8, rows // 8)
    ]


def half_outs(rows, columns, block):
    return [
        (shaped((r, columns), BF), pl.BlockSpec((r, block), lambda j, *_: (0, j)))
        for r in (rows // 4,) + (rows // 8,) * 6
    ]


def wgrad_kernel(starts, extra, *refs):
    outs = refs[-3:]
    j = pl.program_id(0)
    for s in range(len(starts) - 1):
        a, a2, g, g2 = refs[4 * s : 4 * s + 4]

        @pl.when((j >= starts[s]) & (j < starts[s + 1]))
        def _(a=a, a2=a2, g=g, g2=g2):
            tokens = g.shape[0]
            part = dot(a[...][:, :tokens], g[...]) + dot(a2[...][:, :tokens], g2[...])
            store_rows(part.astype(BF), outs)

    if extra:

        @pl.when(j == starts[-1])
        def _():
            mine, theirs = refs[-5], refs[-4]
            store_rows((mine[...].astype(F32) + theirs[...].astype(F32)).astype(BF), outs)


def wgrad(segments, extra=(), deps=(), block=1024, name="wgrad"):
    starts, ins = [0], []
    for a, a2, g, g2, *span in segments:
        per = g.shape[2] // block
        first, end = span or (0, g.shape[0] * per)
        count, start = end - first, starts[-1]

        def at(j, start=start, count=count, per=per, first=first):
            k = first + jnp.clip(j - start, 0, count - 1)
            return (k // per, 0, k % per)

        whole = pl.BlockSpec(a.shape, lambda j: (0, 0))
        grads = pl.BlockSpec((None, g.shape[1], block), at)
        ins += [(a, whole), (a2, whole), (g, grads), (g2, grads)]
        starts.append(start + count)
    rows = segments[0][0].shape[0]
    columns = starts[-1] * block
    steps = starts[-1]
    if extra:
        ins += [(e, pl.BlockSpec(e.shape, lambda j: (0, 0))) for e in extra]
        columns += extra[0].shape[1]
        steps += 1
    return run(
        functools.partial(wgrad_kernel, tuple(starts), bool(extra)),
        (steps,),
        ins,
        row_outs(rows, columns, block),
        deps=deps,
        cost=costs(2 * rows * 1024 * columns, 4 * 512 * columns + 2 * rows * columns),
        name=name,
    )


def wgrad_down_kernel(bits_ref, *refs):
    blocks, other, dy, dy2 = refs[:4], refs[4:8], refs[8], refs[9]
    mine = jnp.concatenate([r[...].T for r in blocks], axis=0)
    theirs = jnp.concatenate([r[...].T for r in other], axis=0)
    store_rows((dot(mine, dy[...]) + dot(theirs, dy2[...])).astype(BF), refs[10:])


def wgrad_down(bits, g, g_other, dy, dy_other, cuts):
    tokens, d = dy.shape

    def spec(rel, whole):
        def at(b, bits_ref):
            x = bits_ref[0] ^ (rel & 1)
            y = bits_ref[1] ^ (rel >> 1)
            block = b * 4 + y * 2 + x
            return (0, block * 2 + bits_ref[2] if whole else block)

        return pl.BlockSpec((tokens, 128), at)

    rows = pl.BlockSpec((tokens, d), lambda b, _: (0, 0))
    return run(
        wgrad_down_kernel,
        (cuts,),
        [(g, spec(r, True)) for r in range(4)]
        + [(g_other, spec(r, False)) for r in range(4)]
        + [(dy, rows), (dy_other, rows)],
        half_outs(512, cuts * d, d),
        prefetch=(bits,),
        cost=costs(2 * 512 * 1024 * cuts * d, 16 * tokens * d),
        name="wgrad_down",
    )


def up_kernel(bits_ref, *refs):
    h_ref, w_ref, g_ref, slope_ref, send_ref = refs[10:]
    put_pieces(bits_ref, refs[:10], w_ref)
    u = dot(h_ref[...], w_ref[...].reshape(h_ref.shape[1], w_ref.shape[3]))
    cdf = 0.5 * (1.0 + lax.erf(u * (0.5**0.5)))
    g = (u * cdf).astype(BF)
    g_ref[...] = g
    slope_ref[...] = (cdf + u * (jnp.exp(-0.5 * u * u) * 0.3989422804014327)).astype(BF)
    core = bits_ref[2]
    for k in range(0, g.shape[1], 256):
        send_ref[:, k // 2 : k // 2 + 128] = jnp.where(
            core == 0, g[:, k + 128 : k + 256], g[:, k : k + 128]
        )


def feed_up(bits, h, pieces, ff, deps=(), block=512):
    tokens, d = h.shape
    rows = pieces[0].shape[1]
    out = (shaped((tokens, ff), BF), pl.BlockSpec((tokens, block), lambda j, _: (0, j)))
    w, *rest = run(
        up_kernel,
        (ff // block,),
        piece_specs(pieces, 0, block) + [(h, pl.BlockSpec((tokens, d), lambda j, _: (0, 0)))],
        [
            place_out(rows, ff, block),
            out,
            out,
            (
                shaped((tokens, ff // 2), BF),
                pl.BlockSpec((tokens, block // 2), lambda j, _: (0, j)),
            ),
        ],
        prefetch=(bits,),
        deps=deps,
        cost=costs(2 * tokens * d * ff, 4 * d * ff + 4 * tokens * ff, 2 * tokens * ff),
        name="feed_up",
    )
    return w.reshape(d, ff), *rest


def down_kernel(g_ref, w_ref, x_ref, out_ref):
    @pl.when(pl.program_id(0) == 0)
    def _():
        out_ref[...] = x_ref[...]

    out_ref[...] += dot(g_ref[...], w_ref[...])


def feed_down(g, w, x, cuts, deps=()):
    tokens, d = x.shape
    block = d // 2
    whole = pl.BlockSpec((tokens, d), lambda j: (0, 0))
    return run(
        down_kernel,
        (2 * cuts,),
        [
            (g, pl.BlockSpec((tokens, block), lambda j: (0, j))),
            (w, pl.BlockSpec((block, d), lambda j: (j % 2, j // 2))),
            (x, whole),
        ],
        [(shaped((tokens, d), F32), whole)],
        deps=deps,
        cost=costs(2 * tokens * d * d * cuts, 2 * d * d * cuts + 10 * tokens * d),
        name="feed_down",
    )


def norm_back_store(acc, x_ref, gain_ref, res_ref, dx_ref, low_ref, sums_ref):
    gain_grad, bias_grad = 0.0, 0.0
    step = 128
    for r in range(0, x_ref.shape[0], step):
        part = slice(r, r + step)
        x, dh = x_ref[part, :], acc[part, :]
        center = x - jnp.mean(x, -1, keepdims=True)
        inverse = lax.rsqrt(jnp.mean(center * center, -1, keepdims=True) + 1e-05)
        unit = center * inverse
        gain_grad += jnp.sum(dh * unit, axis=0, keepdims=True)
        bias_grad += jnp.sum(dh, axis=0, keepdims=True)
        scaled = dh * gain_ref[...]
        mean_a = jnp.mean(scaled, -1, keepdims=True)
        mean_b = jnp.mean(scaled * unit, -1, keepdims=True)
        dx = res_ref[part, :] + inverse * (scaled - mean_a - unit * mean_b)
        dx_ref[part, :] = dx
        if low_ref is not None:
            low_ref[part, :] = dx.astype(BF)
    sums_ref[0:1, :] = gain_grad
    sums_ref[1:2, :] = bias_grad


def accumulate(acc, part):
    j = pl.program_id(0)

    @pl.when(j == 0)
    def _():
        acc[...] = part

    @pl.when(j > 0)
    def _():
        acc[...] += part


def feed_back_kernel(
    dy_ref, w2_ref, slope_ref, w1_ref, x_ref, gain_ref, res_ref, du_ref, dx_ref, low_ref, sums_ref, acc
):
    du = (dot_nt(dy_ref[...], w2_ref[...]) * slope_ref[...].astype(F32)).astype(BF)
    du_ref[...] = du
    accumulate(acc, dot_nt(du, w1_ref[...]))

    @pl.when(pl.program_id(0) == pl.num_programs(0) - 1)
    def _():
        norm_back_store(acc, x_ref, gain_ref, res_ref, dx_ref, low_ref, sums_ref)


def feed_back(dy, w2, slope, w1, x, gain, res, cuts, deps=()):
    tokens, d = x.shape
    block = d // 2
    ff = w1.shape[1]
    whole = pl.BlockSpec((tokens, d), lambda j: (0, 0), pipeline_mode=pl.Buffered(1))
    part = pl.BlockSpec((tokens, block), lambda j: (0, j))
    return run(
        feed_back_kernel,
        (2 * cuts,),
        [
            (dy, whole),
            (w2, pl.BlockSpec((block, d), lambda j: (j % 2, j // 2))),
            (slope, part),
            (w1, pl.BlockSpec((d, block), lambda j: (0, j))),
            (x, whole),
            (gain, pl.BlockSpec((1, d), lambda j: (0, 0))),
            (res, whole),
        ],
        [
            (shaped((tokens, ff), BF), part),
            (shaped((tokens, d), F32), whole),
            (shaped((tokens, d), BF), whole),
            (shaped((2, d), F32), pl.BlockSpec((2, d), lambda j: (0, 0))),
        ],
        scratch=[pltpu.VMEM((tokens, d), F32)],
        deps=deps,
        cost=costs(4 * tokens * d * ff, 4 * d * ff + 4 * tokens * ff + 16 * tokens * d),
        name="feed_back",
    )


def norm_back_kernel(further, g_ref, w_ref, x_ref, gain_ref, res_ref, *refs):
    w2_ref = refs[0] if further else None
    refs = refs[1:] if further else refs
    dx_ref, sums_ref, acc = refs[0], refs[-2], refs[-1]
    low_ref = refs[1] if further else None
    accumulate(acc, dot_nt(g_ref[...], w_ref[...]))

    @pl.when(pl.program_id(0) == pl.num_programs(0) - 1)
    def _():
        norm_back_store(acc, x_ref, gain_ref, res_ref, dx_ref, low_ref, sums_ref)
        if further:
            refs[2][...] = dot_nt(low_ref[...], w2_ref[...]).astype(BF)


def through_norm(g, w, x, gain, res, further=None, deps=()):
    tokens, d = x.shape
    block = 512
    per = g.shape[2] // block
    count = g.shape[0] * per
    whole = pl.BlockSpec((tokens, d), lambda j: (0, 0), pipeline_mode=pl.Buffered(1))
    whole_weight = pl.BlockSpec((d, d), lambda j: (0, 0), pipeline_mode=pl.Buffered(1))
    outs = [(shaped((tokens, d), F32), whole)]
    if further is not None:
        outs += [(shaped((tokens, d), BF), whole)] * 2
    outs.append((shaped((2, d), F32), pl.BlockSpec((2, d), lambda j: (0, 0))))
    return run(
        functools.partial(norm_back_kernel, further is not None),
        (count,),
        [
            (g, pl.BlockSpec((None, tokens, block), lambda j: (j // per, 0, j % per))),
            (w, pl.BlockSpec((d, block), lambda j: (0, j))),
            (x, whole),
            (gain, pl.BlockSpec((1, d), lambda j: (0, 0))),
            (res, whole),
        ]
        + ([] if further is None else [(further, whole_weight)]),
        outs,
        scratch=[pltpu.VMEM((tokens, d), F32)],
        deps=deps,
        cost=costs(2 * tokens * d * block * count, 2 * d * block * count + 16 * tokens * d),
        name="through_norm",
    )


def scatter_far(grads):
    return swap(grads[1], XBIT), swap(grads[2], YBIT)


def pass_on_kernel(x_ref, y_ref, from_x, from_y, to_x, to_y):
    half = from_x.shape[0]
    to_x[:half] = x_ref[:half]
    to_x[half:] = x_ref[half:] + from_y[...]
    to_y[:half] = y_ref[:half] + from_x[...]
    to_y[half:] = y_ref[half:]


def sum_kernel(own, got_x, got_y, out):
    total = own[...].astype(F32) + got_x[...].astype(F32) + got_y[...].astype(F32)
    out[...] = total.astype(out.dtype)


def column_blocks(columns):
    return columns if columns <= 2304 else next(b for b in (2048, 1024, 640) if columns % b == 0)


def rows_spec(rows, block, at=0):
    return pl.BlockSpec((rows, block), lambda j: (at, j))


def scatter_near(near, far):
    rows, columns = near.shape[0] // 3, near.shape[1]
    block = column_blocks(columns)
    far_spec, out = rows_spec(rows // 2, block), (shaped((rows, columns), BF), rows_spec(rows, block))
    to_x, to_y = run(
        pass_on_kernel,
        (columns // block,),
        [
            (near, rows_spec(rows, block, 1)),
            (near, rows_spec(rows, block, 2)),
            (far[0], far_spec),
            (far[1], far_spec),
        ],
        [out, out],
        cost=costs(rows * columns, 10 * rows * columns),
        name="pass_on",
    )
    return swap(to_x, XBIT), swap(to_y, YBIT)


def add_pairs_kernel(a, b, c, d, first, second):
    first[...] = a[...] + b[...]
    second[...] = c[...] + d[...]


def sum_halves_kernel(own, x_low, x_high, y_low, y_high, out):
    half = x_low.shape[0]
    for k, (x, y) in enumerate(((x_low, y_low), (x_high, y_high))):
        part = own[k * half : (k + 1) * half].astype(F32) + x[...].astype(F32)
        out[k * half : (k + 1) * half] = (part + y[...].astype(F32)).astype(BF)


def early_first(grads):
    _, x_low, _, _, y_high, low, high = grads
    return swap(low, XBIT), swap(high, YBIT), swap(x_low, XBIT), swap(y_high, YBIT)


def early_second(grads, came):
    rows, columns = came[0].shape
    block = column_blocks(columns)
    spec = rows_spec(rows, block)
    out = (shaped((rows, columns), BF), spec)
    to_x, to_y = run(
        add_pairs_kernel,
        (columns // block,),
        [(a, spec) for a in (grads[2], came[1], grads[3], came[0])],
        [out, out],
        cost=costs(2 * rows * columns, 12 * rows * columns),
        name="pass_on",
    )
    return swap(to_x, XBIT), swap(to_y, YBIT)


def early_line(grads, came, last):
    rows, columns = grads[0].shape
    block = column_blocks(columns)
    half = rows_spec(rows // 2, block)
    total = run(
        sum_halves_kernel,
        (columns // block,),
        [(grads[0], rows_spec(rows, block))]
        + [(a, half) for a in (came[2], last[0], last[1], came[3])],
        [(shaped((rows, columns), BF), rows_spec(rows, block))],
        cost=costs(2 * rows * columns, 8 * rows * columns),
        name="plane_sum",
    )
    return lax.psum_scatter(total, "gx", scatter_dimension=0, tiled=True)


def plane_sum(near, got, dtype):
    rows, columns = got[0].shape
    block = column_blocks(columns)
    return run(
        sum_kernel,
        (columns // block,),
        [(a, rows_spec(rows, block)) for a in (near, *got)],
        [(shaped((rows, columns), dtype), rows_spec(rows, block))],
        cost=costs(2 * rows * columns, 8 * rows * columns),
        name="plane_sum",
    )


def scatter_line(near, got):
    total = plane_sum(near, got, BF)
    return lax.psum_scatter(total, "gx", scatter_dimension=0, tiled=True)


def line_kernel(bits_ref, own, got_x, got_y, mine, *sends):
    rows = mine.shape[0]
    for step in range(4):
        at = pl.ds(lax.rem(bits_ref[3] + step, 4) * rows, rows)
        total = own[at, :].astype(F32) + got_x[at, :].astype(F32) + got_y[at, :].astype(F32)
        if step == 0:
            mine[...] = total
        else:
            sends[step - 1][...] = total.astype(BF)


def line_parts(near, got, bits):
    rows, columns = got[0].shape
    spec = pl.BlockSpec((rows, columns), lambda j, _: (0, 0))
    out = pl.BlockSpec((rows // 4, columns), lambda j, _: (0, 0))
    mine, *sends = run(
        line_kernel,
        (1,),
        [(a, spec) for a in (near, *got)],
        [(shaped((rows // 4, columns), F32), out)] + [(shaped((rows // 4, columns), BF), out)] * 3,
        prefetch=(bits,),
        cost=costs(3 * rows * columns, 8 * rows * columns),
        name="line_parts",
    )
    came = [
        lax.ppermute(part, ALL, [(i, (i + 8 * step) % 32) for i in range(32)])
        for step, part in zip((1, 2, 3), sends, strict=True)
    ]
    return [mine] + came


def four_sum(refs, columns):
    total = refs[0][:, columns]
    for ref in refs[1:]:
        total = total + ref[:, columns].astype(F32)
    return total


def finish_first_kernel(*refs):
    d = refs[4].shape[1]
    refs[4][...] = four_sum(refs[:4], slice(0, d))
    refs[5][...] = four_sum(refs[:4], slice(d, 2 * d))


def finish_last_kernel(*refs):
    q, qkv, gains, biases = refs[4:]
    d = q.shape[1]
    qkv[:, :d] = q[...]
    qkv[:, d:] = four_sum(refs[:4], slice(0, 2 * d))
    sums = four_sum(refs[:4], slice(2 * d, 2 * d + 128)).T
    gains[...] = sums[0:3]
    biases[...] = sums[3:6]


def finish(kernel, ins, outs):
    def whole(shape):
        return pl.BlockSpec(shape, lambda j: (0,) * len(shape))

    return run(
        kernel,
        (1,),
        [(a, whole(a.shape)) for a in ins],
        [(shaped(s, F32), whole(s)) for s in outs],
        cost=costs(4 * ins[0].size, 16 * ins[0].size),
        name="finish",
    )


def turn_kernel(select_ref, a_ref, mine, theirs):
    rows = dot_nt(select_ref[...], a_ref[...]).astype(BF)
    half = pl.num_programs(0) // 2

    @pl.when(pl.program_id(0) < half)
    def _():
        mine[...] = rows

    @pl.when(pl.program_id(0) >= half)
    def _():
        theirs[...] = rows


def turn(select, a):
    tokens, d = a.shape
    steps = 4
    block, half = d // steps, steps // 2
    out = shaped((d // 2, tokens), BF)
    return run(
        turn_kernel,
        (steps,),
        [
            (select, pl.BlockSpec((block, d), lambda j: (j, 0))),
            (a, pl.BlockSpec((tokens, d), lambda j: (0, 0))),
        ],
        [
            (out, pl.BlockSpec((block, tokens), lambda j: (jnp.minimum(j, half - 1), 0))),
            (out, pl.BlockSpec((block, tokens), lambda j: (jnp.maximum(j - half, 0), 0))),
        ],
        cost=costs(2 * d * d * tokens, 2 * d * d + 4 * d * tokens),
        name="turn",
    )


def hidden_order_kernel(to_hidden, rows, cuts, src, out):
    lines = 4
    width = lines * cuts * rows
    at = lax.broadcasted_iota(jnp.int32, (width, width), 0)
    to = lax.broadcasted_iota(jnp.int32, (width, width), 1)
    first, second = (lines, cuts) if to_hidden else (cuts, lines)
    moved = (at // rows % second * first + at // (rows * second)) * rows + at % rows
    swap_two = (moved == to).astype(F32).astype(BF)
    for place_at in range(8):
        if to_hidden:
            step, parts, wide = cuts * rows, lines, cuts * rows
        else:
            step, parts, wide = lines * rows, cuts, lines * rows
        pieces = [
            src[:, (k * 8 + place_at) * step : (k * 8 + place_at) * step + wide]
            for k in range(parts)
        ]
        done = dot(jnp.concatenate(pieces, axis=1), swap_two)
        out_step = lines * rows if to_hidden else cuts * rows
        for k in range(cuts if to_hidden else lines):
            at_column = (k * 8 + place_at) * out_step
            out[:, at_column : at_column + out_step] = done[
                :, k * out_step : (k + 1) * out_step
            ].astype(out.dtype)


def hidden_order(a, to_hidden, cuts, dtype):
    rows, ff = a.shape
    whole = pl.BlockSpec((rows, ff), lambda j: (0, 0))
    return run(
        functools.partial(hidden_order_kernel, to_hidden, ff // 32 // cuts, cuts),
        (1,),
        [(a, whole)],
        [(shaped((rows, ff), dtype), whole)],
        cost=costs(2 * rows * ff * 512, 6 * rows * ff),
        name="hidden_order",
    )


def memory_grad_kernel(g_ref, w_ref, out_ref):
    part = dot_nt(g_ref[...], w_ref[...])[: out_ref.shape[0]]

    @pl.when(pl.program_id(0) == 0)
    def _():
        out_ref[...] = part

    @pl.when(pl.program_id(0) > 0)
    def _():
        out_ref[...] += part


def memory_grad(g, w, rows):
    _, padded, d = g.shape
    block = d // 2
    return run(
        memory_grad_kernel,
        (4,),
        [
            (g, pl.BlockSpec((None, padded, block), lambda j: (j // 2, 0, j % 2))),
            (w, pl.BlockSpec((d, block), lambda j: (0, j))),
        ],
        [(shaped((rows, d), F32), pl.BlockSpec((rows, d), lambda j: (0, 0)))],
        cost=costs(4 * padded * d * d, 8 * d * d + 4 * rows * d),
        name="memory_grad",
    )


def shards_plane(
    hidden,
    memory,
    lengths,
    page_class,
    cotangent,
    w_self_qkv,
    w_self_out,
    w_cross_q,
    w_cross_kv,
    w_cross_out,
    w_fc1,
    w_fc2,
    norm_gains,
    norm_biases,
):
    tokens, d = hidden.shape
    rows, ff = w_fc1.shape
    cuts = w_fc2.shape[0] // rows
    mem_rows = -(-memory.shape[0] // 16) * 16
    slots_used = jnp.where(page_class == 0, MEM_BIG, MEM_BIG // 4).astype(jnp.int32)
    along = lax.axis_index("gy")
    x_at, y_at, core = (along // 2) % 2, along // 4, along % 2
    z_at = lax.axis_index("gx")
    bits = jnp.stack([x_at, y_at, core, z_at]).astype(jnp.int32)

    norm_cols = jnp.concatenate([norm_gains, norm_biases], axis=0).T
    norm_cols = jnp.pad(norm_cols, ((0, 0), (0, 128 - norm_cols.shape[1])))
    up_local = hidden_order(w_fc1, True, cuts, BF)
    down_local = jnp.concatenate(
        [w_fc2[c * rows : (c + 1) * rows] for c in range(cuts)], axis=1
    )
    place_at = jnp.arange(d)
    r = place_at % rows
    z = (place_at // rows) % 4
    rel = (place_at // (4 * rows)) % 4
    source_core = core ^ (place_at // (16 * rows))
    device = z * 8 + (y_at ^ (rel // 2)) * 4 + (x_at ^ (rel % 2)) * 2 + source_core
    select = ((device * rows + r)[:, None] == place_at[None, :]).astype(BF)

    def turned(a):
        mine, theirs = turn(select, a)
        return mine, swap(theirs, CORE)

    pack1 = jnp.concatenate([w_self_qkv, norm_cols], axis=1)
    pack2 = jnp.concatenate([w_cross_kv, w_self_out, w_cross_q, w_cross_out], axis=1)
    blocks = d // PAIR
    memory_pad = jnp.pad(memory, ((0, mem_rows - memory.shape[0]), (0, 0)))

    line1, pack2, memory_pad, hidden = fence(gather_line(pack1), pack2, memory_pad, hidden)

    line2 = gather_line(pack2)
    near1 = gather_near(line1)
    mem_t = turned(jnp.pad(memory_pad, ((0, -mem_rows % 128), (0, 0))))
    unit1, _ = norm_parts(hidden)
    near1, mem_t, unit1 = fence(near1, mem_t, unit1)

    near1, far1, cores1, line2, pack3 = fence(
        near1, gather_far(near1), swap_cores(near1), line2, up_local
    )

    line3 = gather_line(pack3)
    near2 = gather_near(line2)
    first = near1 + far1 + cores1 + swap_cores(far1)
    norms = place(first, 3 * d, 128, bits)[:, :6].T.astype(F32)
    gains, biases = norms[:3], norms[3:]
    h1 = (unit1 * gains[0] + biases[0]).astype(BF)
    wqkv, qkv = place_dot(first, 0, 3 * d, bits, h1, BF)
    o, lse = attn_fwd((qkv, 0), qkv, blocks, 2 * blocks, lengths, True)
    near2, o, h1, gains, biases = fence(near2, o, h1, gains, biases)

    far2, cores2 = gather_far(near2), swap_cores(near2)
    h1_turn, o_turn = turn(select, h1), turn(select, o)
    near2, far2, cores2, h1_turn, o_turn, o, line3, pack4 = fence(
        near2, far2, cores2, h1_turn, o_turn, o, line3, down_local
    )

    wdown = lax.all_gather(pack4, ("gy", "gx"), axis=0, tiled=True)
    near3 = gather_near(line3)
    second = near2 + far2 + cores2 + swap_cores(far2)
    wso, y1 = place_dot(second, 2 * d, d, bits, o, F32)
    x1 = hidden + y1
    unit2, _ = norm_parts(x1)
    h2 = (unit2 * gains[1] + biases[1]).astype(BF)
    wcq, qc = place_dot(second, 3 * d, d, bits, h2, BF)
    wckv, kvc = place_dot(second, 0, 2 * d, bits, memory_pad, BF)
    h1_t, o_t = ((mine, swap(theirs, CORE)) for mine, theirs in (h1_turn, o_turn))
    h2_t = turned(h2)
    near3, second, qc, kvc, x1, h1_t, o_t, h2_t = fence(
        near3, second, qc, kvc, x1, h1_t, o_t, h2_t
    )

    far3, cores3 = gather_far(near3), swap_cores(near3)
    o2, lse2 = attn_fwd((qc, 0), kvc, 0, blocks, slots_used, False)
    near3, cores3, o2, cotangent = fence(near3, cores3, o2, cotangent)

    wco, y2 = place_dot(second, 4 * d, d, bits, o2, F32)
    x2 = x1 + y2
    unit3, _ = norm_parts(x2)
    h3 = (unit3 * gains[2] + biases[2]).astype(BF)
    valid = (jnp.arange(tokens) < lengths[0])[:, None].astype(F32)
    dout = cotangent * valid
    dy3 = dout.astype(BF)
    dy3_other = swap(dy3, CORE)
    far3, h3, x2, o2, dout, dy3, dy3_other = fence(far3, h3, x2, o2, dout, dy3, dy3_other)

    third = near3 + far3 + cores3 + swap_cores(far3)
    wup, g, slope, g_send = feed_up(bits, h3, third, ff)
    wup, g, slope, g_send, h3, o2 = fence(wup, g, slope, g_send, h3, o2)

    h3_t, o2_t = turned(h3), turned(o2)
    g_other, h3_t, o2_t, g = fence(swap(g_send, CORE), h3_t, o2_t, g)

    grad_down = wgrad_down(bits, g, g_other, dy3, dy3_other, cuts)
    grad_down, dy3, slope, wdown = fence(grad_down, dy3, slope, wdown)

    du, dx2, dy2, sums3 = feed_back(dy3, wdown, slope, wup, x2, gains[2:3], dout, cuts)
    far1, du, dx2, dy2, g = fence(early_first(grad_down), du, dx2, dy2, g)

    got1 = early_second(grad_down, far1)
    do2 = dot_nt(dy2, wco).astype(BF)
    du_other, do2, du = fence(swap(du, CORE), do2, du)

    grad_up = wgrad([h3_t + (du[None], du_other[None])])
    grad_up, do2, dy2 = fence(grad_up, do2, dy2)

    dqc, dkvc = attn_bwd((qc, 0), kvc, 0, blocks, o2, do2, lse2, slots_used, False)
    far2, got1, dqc, dkvc, dy2_other, dx2 = fence(
        scatter_far(grad_up), got1, dqc, dkvc, swap(dy2, CORE), dx2
    )

    own_down = early_line(grad_down, far1, got1)
    got2 = scatter_near(grad_up[0], far2)
    dx1, dy1, do, sums2 = through_norm(dqc, wcq, x1, gains[1:2], dx2, further=wso)
    dqc_other, dkvc_other, dx1, dy1, do, dqc, dkvc = fence(
        swap(dqc, CORE), swap(dkvc, CORE), dx1, dy1, do, dqc, dkvc
    )

    grad_mid = wgrad(
        [
            o2_t + (dy2[None], dy2_other[None]),
            h2_t + (dqc, dqc_other),
            mem_t + (dkvc, dkvc_other),
        ],
        name="wgrad_mid",
    )
    grad_mid, do, dy1 = fence(grad_mid, do, dy1)

    dqkv = attn_bwd((qkv, 0), qkv, blocks, 2 * blocks, o, do, lse, lengths, True)
    far3, dy1_other, dqkv, got2, dx1 = fence(
        scatter_far(grad_mid), swap(dy1, CORE), dqkv, got2, dx1
    )

    own_up = scatter_line(grad_up[0], got2)
    got3 = scatter_near(grad_mid[0], far3)
    grad_hidden, sums1 = through_norm(dqkv, wqkv, hidden, gains[0:1], dx1)
    sums = jnp.stack([sums1, sums2, sums3], axis=1).reshape(6, d)
    sums = jnp.pad(sums, ((0, 122), (0, 0))).astype(BF)
    dqkv_other, grad_hidden, sums = fence(swap(dqkv, CORE), grad_hidden, sums)

    grad_a = wgrad(
        [o_t + (dy1[None], dy1_other[None]), h1_t + (dqkv, dqkv_other, 0, 1)],
        name="wgrad_a",
    )
    grad_a, dqkv, dqkv_other, sums_t = fence(grad_a, dqkv, dqkv_other, turned(sums))

    grad_b = wgrad([h1_t + (dqkv, dqkv_other, 1, 3)], extra=sums_t)
    far_a, grad_b, got3, dkvc, own_down, g = fence(
        scatter_far(grad_a), grad_b, got3, dkvc, own_down, g
    )

    got_a = scatter_near(grad_a[0], far_a)
    own_mid = scatter_line(grad_mid[0], got3)
    result = feed_down(g, wdown, x2, cuts)
    far_b, got_a, result, own_up, dkvc = fence(
        scatter_far(grad_b), got_a, result, own_up, dkvc
    )

    got_b = scatter_near(grad_b[0], far_b)
    came_a = line_parts(grad_a[0], got_a, bits)
    own_up = hidden_order(own_up, False, cuts, F32)
    grad_memory = memory_grad(dkvc, wckv, memory.shape[0])
    got_b, own_up, grad_memory = fence(got_b, own_up, grad_memory)

    came_b = line_parts(grad_b[0], got_b, bits)
    own_mid = own_mid.astype(F32)
    mids = [own_mid[:, k * d : k * d + w * d] for k, w in ((0, 1), (1, 1), (2, 2))]
    grad_so, grad_q = finish(finish_first_kernel, came_a, [(rows, d)] * 2)
    came_b[1], mids, grad_so, grad_q = fence(came_b[1], mids, grad_so, grad_q)

    own_qkv, own_gains, own_biases = finish(
        finish_last_kernel, came_b + [grad_q], [(rows, 3 * d), (3, rows), (3, rows)]
    )
    own_down = jnp.concatenate(
        [own_down[:, c * d : (c + 1) * d] for c in range(cuts)], axis=0
    )
    return (
        result,
        grad_hidden,
        grad_memory,
        own_qkv,
        grad_so,
        mids[1],
        mids[2],
        mids[0],
        own_up,
        own_down.astype(F32),
        own_gains,
        own_biases,
    )


def solution(mesh):
    row = P(ALL, None)
    col = P(None, ALL)
    nx, ny = mesh.shape["gx"], mesh.shape["gy"]
    body = shards_plane if (nx, ny) == (4, 8) else functools.partial(shards_any, nx=nx, ny=ny)
    return jax.shard_map(
        body,
        mesh=mesh,
        in_specs=(row, row, P(ALL), P(ALL), row) + (row,) * 7 + (col, col),
        out_specs=(row,) * 10 + (col, col),
        check_vma=False,
    )
```
